128 devices in a mesh: comp: 2 (over z_hi), gx: 32 (over y, x, z_lo), gy: 2 (over core).
Axes of the slice: x: 4, y: 4, z: 4 (z_hi: 2, z_lo: 2; z = z_hi * 2 + z_lo), core: 2. Of those that a mesh axis runs over, the one named last changes fastest.
Arguments:
- layered_heat_profile: float32 [2, 8, 8192, 256], P('comp', None, 'gx', 'gy'), may hold values from -6 to 6
- prior_marine_heat: float32 [8192, 256], P('gx', 'gy'), may hold values from -6 to 6
- transfer_factor_table: float32 [8, 8192, 256], P(None, 'gx', 'gy'), may hold values from 0.1 to 1
- depth_fraction_matrix: float32 [8, 8], replicated, may hold values from -2 to 2
- adjacent_cell_table: int32 [6, 8192, 256], P(None, 'gx', 'gy'), may hold values from 0 to 33539, as said below
- destination_water_peer: int32 [16384, 2], P(('gx', 'gy')), may hold values from 0 to 63, all different within a row; in each aligned block of 256 rows (0 to 255, 256 to 511, ...) at most 18 rows name the same one
- destination_water_line: int32 [16384, 2], P(('gx', 'gy')), may hold values from 0 to 255
- interpolation_matrix_blocks: bfloat16 [16384, 2, 128, 128], P(('gx', 'gy')), may hold values from -0.5 to 0.5
Outputs:
- state_out: float32 [2, 8, 8192, 256], P('comp', None, 'gx', 'gy')
- boundary_coupled_pair: float32 [2, 8192, 256], P('comp', 'gx', 'gy')
The draws below stay inside these ranges and needn't reach their ends.
Inputs may be any that keep to these rules, and one draw needn't show every extreme that they name: `destination_water_peer`: each row names 2 different ocean ranks; among the rows of one device no rank is named by more than 18 routes, and exactly 18 for some rank. `adjacent_cell_table`: each entry indexes a device's block of 256 x 128 cells extended by one cell on every side, flattened row by row; a cell's entries are its six hexagonal neighbours in offset rows, except land neighbours, which are the cell's own index.
All inputs are finite; a program needn't handle non-finite values.
Results may differ from the reference program's by a relative error of at most 0.0054.
Values may be sent and summed in bfloat16 or wider, within the bound.
No kernel may reach another device: no remote copies, remote signals or barrier semaphores. Data moves between devices by JAX's collectives and lax.ppermute only.
A program may use at most 320 MiB of HBM per device.

```python
import math
import jax
import jax.numpy as jnp
import numpy as np
from jax import lax

LEV = 8
NF = 8
NB = 6
K = 2
CHIP_SPAN_FIRST = 256
CHIP_SPAN_SECOND = 128
CAP = 18
GRID_SPAN_FIRST = 8192
GRID_SPAN_SECOND = 256
ROUTES = 16384
N_GX = 32
N_GY = 2


def draw_adjacent_cell_table(key, part):
    key = jax.random.fold_in(key, 7)
    rows_all = CHIP_SPAN_FIRST * N_GX
    cols_all = CHIP_SPAN_SECOND * N_GY
    row_index = jnp.arange(rows_all)[:, None] % CHIP_SPAN_FIRST
    col_index = jnp.arange(cols_all)[None, :] % CHIP_SPAN_SECOND
    odd_rows = row_index % 2
    shift_even = [(0, -1), (0, 1), (-1, -1), (-1, 0), (1, -1), (1, 0)]
    shift_odd = [(0, -1), (0, 1), (-1, 0), (-1, 1), (1, 0), (1, 1)]
    land_mask = jax.random.randint(key, (NB, rows_all, cols_all), 0, 5) == 0
    self_index = (row_index + 1) * (CHIP_SPAN_SECOND + 2) + col_index + 1
    table_list = []
    for slot_index in range(NB):
        row_step = jnp.where(odd_rows == 1, shift_odd[slot_index][0], shift_even[slot_index][0])
        col_step = jnp.where(odd_rows == 1, shift_odd[slot_index][1], shift_even[slot_index][1])
        neighbour_index = (row_index + 1 + row_step) * (CHIP_SPAN_SECOND + 2) + (col_index + 1 + col_step)
        table_list.append(jnp.where(land_mask[slot_index], self_index, neighbour_index))
    return jnp.stack(table_list).astype(jnp.int32)


def place_ends(values, own_key, smallest, top_value):
    place = [jax.random.randint(jax.random.fold_in(own_key, axis), (), 0, length) for axis, length in enumerate(values.shape)]
    longest = values.shape.index(max(values.shape))
    beside = place[:longest] + [(place[longest] + 1) % values.shape[longest]] + place[longest + 1:]
    return values.at[tuple(place)].set(smallest).at[tuple(beside)].set(top_value)


def block_scale(stream_key, dims, split, smallest, high):
    level = 1.0
    for axis_at, blocks in split:
        draws = jax.random.uniform(jax.random.fold_in(jax.random.fold_in(stream_key, 6), axis_at), (blocks,), jnp.float32, smallest / len(split), high / len(split))
        level = level * jnp.repeat(jnp.exp(draws), dims[axis_at] // blocks).reshape((-1,) + (1,) * (len(dims) - 1 - axis_at))
    return level


def deal_out(own_key, own, number, rows, amount, top, limit, lean):
    ranking = jax.random.permutation(own_key, amount)
    packed, ordinary = load_shares(amount, rows * top, limit, lean, True), load_shares(amount, rows * top, limit, lean, False)
    places = jnp.arange(amount)

    def named(lengths, offset_by):
        used = int((lengths > 0).sum())
        fixed = max(1, used // 4)
        moved = fixed + (places - fixed + offset_by * (used - fixed)) % max(1, amount - fixed)
        return jnp.zeros((amount,), jnp.int32).at[ranking[jnp.where(places < fixed, places, moved)]].set(jnp.asarray(lengths, jnp.int32))

    lengths = jnp.where(number % 4 == 0, named(packed, number // 4), named(ordinary, number - number // 4 - 1))
    mixed = jax.random.permutation(jax.random.fold_in(own, 3), amount)
    donor, receiver = mixed[0:amount // 2 * 2:2], mixed[1:amount // 2 * 2:2]
    room = jnp.minimum(lengths[donor] - 1, limit - lengths[receiver]) // 2
    room = jnp.where((donor == ranking[0]) | (receiver == ranking[0]) | (lengths[receiver] == 0), 0, jnp.maximum(room, 0))
    moved = jax.random.randint(jax.random.fold_in(own, 4), (amount // 2,), 0, 1 << 20) % (room + 1)
    lengths = lengths.at[donor].add(-moved).at[receiver].add(moved)
    items = jnp.searchsorted(jnp.cumsum(lengths), jnp.arange(rows * top), side="right").astype(jnp.int32)
    listing = items.reshape(top, rows).T
    listing = listing[jax.random.permutation(jax.random.fold_in(own, 1), rows)]
    offset_by = jax.random.randint(jax.random.fold_in(own, 2), (rows, 1), 0, top)
    return jnp.take_along_axis(listing, (jnp.arange(top)[None, :] + offset_by) % top, axis=1)


def load_shares(number_of, total, limit, lean, full):
    loads = [(1 << 20) // math.isqrt(rank ** lean) + 1 for rank in range(1, number_of + 1)]
    largest = limit if full else min(limit, max(-(-total // number_of), total * loads[0] // sum(loads)))
    least = 1 if total - largest >= number_of - 1 else 0
    holding, spare = [largest] + [least] * (number_of - 1), total - largest - least * (number_of - 1)
    while spare > 0:
        movable = [i for i in range(1, number_of) if holding[i] < largest] or [i for i in range(1, number_of) if holding[i] < limit]
        whole, left = sum([loads[i] for i in movable]), spare
        for i in movable:
            addition = min(limit - holding[i], max(1, left * loads[i] // whole), spare)
            holding[i] = holding[i] + addition
            spare = spare - addition
    return np.array(holding)


def noise(stream_key, dims, scale, bound, pieces=(), held_as=jnp.bfloat16):
    values = jax.random.normal(stream_key, dims, jnp.float32) * scale
    if len(pieces) > 0:
        values = block_scale(stream_key, dims, pieces, -0.22, 0.18) * values
    return jnp.clip(values, min=-bound, max=bound).astype(held_as)


def setup_inputs(seed: int = 0) -> dict:
    keys = jax.random.split(jax.random.key(seed), 9)
    layered_heat_profile = noise(keys[0], (2, LEV, GRID_SPAN_FIRST, GRID_SPAN_SECOND), 1.0, 6.0, ((0, 2), (2, 32), (3, 2)), jnp.float32)
    prior_marine_heat = noise(keys[1], (GRID_SPAN_FIRST, GRID_SPAN_SECOND), 1.0, 6.0, ((0, 32), (1, 2)), jnp.float32)
    transfer_factor_table = jnp.clip(jnp.exp(math.log(1.0) - 2.3025851 * jax.random.uniform(keys[2], (NF, GRID_SPAN_FIRST, GRID_SPAN_SECOND), jnp.float32) ** block_scale(keys[2], (NF, GRID_SPAN_FIRST, GRID_SPAN_SECOND), ((1, 32), (2, 2)), -0.2, 0.2)), 0.1, 1.0)
    depth_fraction_matrix = noise(keys[3], (LEV, NF), NF ** -0.5, 2.0, (), jnp.float32)
    adjacent_cell_table = draw_adjacent_cell_table(jax.random.fold_in(keys[8], 71), 0)
    destination_water_peer_keys = jax.random.split(jax.random.fold_in(keys[5], 1), ROUTES // CHIP_SPAN_FIRST)
    destination_water_peer_turns = jax.random.permutation(jax.random.fold_in(keys[5], 3), ROUTES // CHIP_SPAN_FIRST)
    destination_water_peer = jax.vmap(lambda own, number: deal_out(jax.random.fold_in(keys[5], 2), own, number, CHIP_SPAN_FIRST, N_GX * N_GY, K, CAP, 2))(destination_water_peer_keys, destination_water_peer_turns).reshape((ROUTES, K))
    destination_water_line = place_ends(jax.random.randint(keys[6], (ROUTES, K), 0, CHIP_SPAN_FIRST), jax.random.fold_in(keys[6], 1), 0, CHIP_SPAN_FIRST - 1).astype(jnp.int32)
    interpolation_matrix_blocks = noise(keys[7], (ROUTES, K, CHIP_SPAN_SECOND, CHIP_SPAN_SECOND), CHIP_SPAN_SECOND ** -0.5, 0.5, ((0, 64),))
    return {"layered_heat_profile": layered_heat_profile, "prior_marine_heat": prior_marine_heat, "transfer_factor_table": transfer_factor_table, "depth_fraction_matrix": depth_fraction_matrix, "adjacent_cell_table": adjacent_cell_table, "destination_water_peer": destination_water_peer, "destination_water_line": destination_water_line, "interpolation_matrix_blocks": interpolation_matrix_blocks}


ATMOS_DIFFUSION = 0.01
MIXING = 0.2
OCEAN_DIFFUSION = 0.12

def second_table():
    gll_nodes = np.array([-1.0, -1.0 / np.sqrt(5.0), 1.0 / np.sqrt(5.0), 1.0])
    poly_order = 3
    legendre = (5.0 * gll_nodes ** 3 - 3.0 * gll_nodes) / 2.0
    derivative = np.zeros((4, 4))
    for row_index in range(4):
        for col_index in range(4):
            if row_index != col_index:
                derivative[row_index, col_index] = legendre[row_index] / (legendre[col_index] * (gll_nodes[row_index] - gll_nodes[col_index]))
    derivative[0, 0] = -poly_order * (poly_order + 1) / 4.0
    derivative[3, 3] = poly_order * (poly_order + 1) / 4.0
    return derivative @ derivative

def vertical(field):
    padded = jnp.concatenate([field[:1], field, field[-1:]], axis=0)
    return padded[2:] + padded[:-2] - 2.0 * field

def average_pairs(field, along_axis):
    extent = field.shape[along_axis]
    view_shape = [1] * field.ndim
    view_shape[along_axis] = extent
    phase = (jnp.arange(extent) % 4).reshape(view_shape)
    ahead = jnp.roll(field, -1, along_axis)
    behind = jnp.roll(field, 1, along_axis)
    return jnp.where(phase == 3, 0.5 * (field + ahead), jnp.where(phase == 0, 0.5 * (field + behind), field))

def atmos_local(field):
    second_diff = jnp.asarray(second_table(), jnp.float32)
    levels, extent_x, extent_y = field.shape
    along_x = jnp.einsum('ij,lejy->leiy', second_diff, field.reshape(levels, extent_x // 4, 4, extent_y), precision=lax.Precision.HIGHEST).reshape(levels, extent_x, extent_y)
    along_y = jnp.einsum('ij,lxej->lxei', second_diff, field.reshape(levels, extent_x, extent_y // 4, 4), precision=lax.Precision.HIGHEST).reshape(levels, extent_x, extent_y)
    return field + ATMOS_DIFFUSION * (along_x + along_y) + MIXING * vertical(field)

def ocean_step(ocean_now, adjacent_cell_table, depth_fraction_matrix, boundary_driving_term):
    levels, extent_x, extent_y = ocean_now.shape
    row_index = jnp.arange(extent_x)[:, None]
    col_index = jnp.arange(extent_y)[None, :]
    across_row = adjacent_cell_table // (CHIP_SPAN_SECOND + 2)
    along_col = adjacent_cell_table % (CHIP_SPAN_SECOND + 2)
    near_rows = (row_index - row_index % CHIP_SPAN_FIRST + across_row - 1) % extent_x
    near_cols = (col_index - col_index % CHIP_SPAN_SECOND + along_col - 1) % extent_y
    near_values = ocean_now[:, near_rows, near_cols]
    spread = lax.optimization_barrier(jnp.sum(near_values - ocean_now[:, None], axis=1))
    forcing_push = jnp.einsum('lf,fxy->lxy', depth_fraction_matrix, boundary_driving_term, precision=lax.Precision.HIGHEST)
    return ocean_now + OCEAN_DIFFUSION * spread + MIXING * vertical(ocean_now) + forcing_push

def forward_rank(operands):
    rank_flux, rank_tiles = operands
    return jnp.einsum('bfp,bkpq->bkfq', rank_flux.astype(jnp.float32), rank_tiles.astype(jnp.float32)).astype(jnp.bfloat16)

def backward_rank(operands):
    rank_tiles, rank_values = operands
    return jnp.einsum('bkpq,bkq->bp', rank_tiles.astype(jnp.float32), rank_values.astype(jnp.float32))

def reference(layered_heat_profile, prior_marine_heat, transfer_factor_table, depth_fraction_matrix, adjacent_cell_table, destination_water_peer, destination_water_line, interpolation_matrix_blocks):
    rank_count = N_GX * N_GY
    air_component_block = layered_heat_profile[0]
    ocean_now = layered_heat_profile[1]
    boundary_transport_quantity = (transfer_factor_table * (air_component_block[0] - prior_marine_heat)[None]).astype(jnp.bfloat16)
    blocks = boundary_transport_quantity.reshape(NF, N_GX, CHIP_SPAN_FIRST, N_GY, CHIP_SPAN_SECOND).transpose(1, 3, 2, 0, 4).reshape(rank_count, CHIP_SPAN_FIRST, NF, CHIP_SPAN_SECOND)
    tile_blocks = interpolation_matrix_blocks.reshape(rank_count, CHIP_SPAN_FIRST, K, CHIP_SPAN_SECOND, CHIP_SPAN_SECOND)
    partials = lax.map(forward_rank, (blocks, tile_blocks))
    target = (destination_water_peer * CHIP_SPAN_FIRST + destination_water_line).reshape(-1).astype(jnp.int32)
    gathered = jnp.zeros((rank_count * CHIP_SPAN_FIRST, NF, CHIP_SPAN_SECOND), jnp.float32).at[target].add(partials.reshape(-1, NF, CHIP_SPAN_SECOND).astype(jnp.float32))
    boundary_driving_term = gathered.reshape(N_GX, N_GY, CHIP_SPAN_FIRST, NF, CHIP_SPAN_SECOND).transpose(3, 0, 2, 1, 4).reshape(NF, GRID_SPAN_FIRST, GRID_SPAN_SECOND)
    ocean_new = ocean_step(ocean_now, adjacent_cell_table, depth_fraction_matrix, boundary_driving_term)
    current = air_component_block
    for substep in range(2):
        current = average_pairs(average_pairs(atmos_local(current), 1), 2)
    surface_top = ocean_new[0].astype(jnp.bfloat16)
    top_blocks = surface_top.reshape(N_GX, CHIP_SPAN_FIRST, N_GY, CHIP_SPAN_SECOND).transpose(0, 2, 1, 3).reshape(rank_count * CHIP_SPAN_FIRST, CHIP_SPAN_SECOND)
    fetched = top_blocks[target].reshape(rank_count, CHIP_SPAN_FIRST, K, CHIP_SPAN_SECOND)
    gathered_results = lax.map(backward_rank, (tile_blocks, fetched))
    updated_marine_heat = gathered_results.reshape(N_GX, N_GY, CHIP_SPAN_FIRST, CHIP_SPAN_SECOND).transpose(0, 2, 1, 3).reshape(GRID_SPAN_FIRST, GRID_SPAN_SECOND)
    state_out = jnp.stack([current, ocean_new], axis=0)
    boundary_coupled_pair = jnp.stack([updated_marine_heat, boundary_driving_term[0]], axis=0)
    return (state_out, boundary_coupled_pair)
```

```python
import functools

import jax
import jax.numpy as jnp
import numpy as np
from jax import lax
from jax.experimental import pallas as pl
from jax.experimental.pallas import tpu as pltpu
from jax.sharding import PartitionSpec as P

ATMOS_DIFFUSION = 0.01
MIXING = 0.2
OCEAN_DIFFUSION = 0.12

RANKS = 64
CAP = 18
LEV = 8
NF = 8
ROWS = 256
COLS = 128
K = 2
OCEAN_SLOTS = 19
ATMOS_SLOTS = 24

VMEM = pl.BlockSpec(memory_space=pltpu.VMEM)
SMEM = pl.BlockSpec(memory_space=pltpu.SMEM)
F32 = jnp.float32
BF16 = jnp.bfloat16


def second_table():
    gll_nodes = np.array([-1.0, -1.0 / np.sqrt(5.0), 1.0 / np.sqrt(5.0), 1.0])
    poly_order = 3
    legendre = (5.0 * gll_nodes**3 - 3.0 * gll_nodes) / 2.0
    derivative = np.zeros((4, 4))
    for row_index in range(4):
        for col_index in range(4):
            if row_index != col_index:
                derivative[row_index, col_index] = legendre[row_index] / (
                    legendre[col_index] * (gll_nodes[row_index] - gll_nodes[col_index])
                )
    derivative[0, 0] = -poly_order * (poly_order + 1) / 4.0
    derivative[3, 3] = poly_order * (poly_order + 1) / 4.0
    return derivative @ derivative


SECOND = second_table()


def call(body, out_shape, specs, **params):
    return pl.pallas_call(
        body,
        out_shape=out_shape,
        in_specs=specs,
        out_specs=jax.tree.map(lambda _: VMEM, out_shape),
        compiler_params=pltpu.CompilerParams(vmem_limit_bytes=params.pop("vmem", 24 << 20)),
        **params,
    )


def positions_body(peer_ref, line_ref, pos_ref, label_ref):
    count = ROWS * K
    peer = jnp.concatenate([peer_ref[k : k + 1, :] for k in range(K)], axis=1)
    line = jnp.concatenate([line_ref[k : k + 1, :] for k in range(K)], axis=1)
    hits = lax.broadcasted_iota(jnp.int32, (RANKS, count), 0) == peer
    hits_f = jnp.where(hits, 1.0, 0.0)
    earlier = lax.broadcasted_iota(jnp.int32, (count, count), 0) < lax.broadcasted_iota(
        jnp.int32, (count, count), 1
    )
    before = jnp.dot(
        hits_f.astype(BF16),
        jnp.where(earlier, 1.0, 0.0).astype(BF16),
        preferred_element_type=F32,
    )
    slot = jnp.sum(hits_f * before, axis=0, keepdims=True).astype(jnp.int32)
    for width, at in ((OCEAN_SLOTS, 0), (ATMOS_SLOTS, K)):
        position = peer * width + slot
        for k in range(K):
            pos_ref[at + k : at + k + 1, :] = position[:, k * ROWS : (k + 1) * ROWS]
    slot_hits = lax.broadcasted_iota(jnp.int32, (COLS, count), 0) == slot
    shifted = jnp.where(hits, (line + 1).astype(F32), 0.0).astype(BF16)
    label_ref[...] = (
        lax.dot_general(
            shifted,
            jnp.where(slot_hits, 1.0, 0.0).astype(BF16),
            (((1,), (1,)), ((), ())),
            preferred_element_type=F32,
        )
        - 1.0
    )


def positions(peer, line):
    return call(
        positions_body,
        (
            jax.ShapeDtypeStruct((2 * K, ROWS), jnp.int32),
            jax.ShapeDtypeStruct((RANKS, COLS), F32),
        ),
        [VMEM, VMEM],
    )(peer.T, line.T)


def ocean_flux_body(per, pos_ref, label_ref, air_ref, prior_ref, factor_ref, w_ref, out_ref, rows):
    step = pl.program_id(0)

    @pl.when(step == 0)
    def _():
        out_ref[...] = jnp.zeros_like(out_ref)
        for d in range(RANKS):
            out_ref[d * OCEAN_SLOTS + CAP] = jnp.broadcast_to(
                label_ref[d : d + 1, :], (NF, COLS)
            ).astype(BF16)

    difference = air_ref[...] - prior_ref[...]
    for f in range(NF):
        rows[pl.ds(f, per, stride=NF), :] = factor_ref[f] * difference
    for b in range(per):
        flux = rows[b * NF : (b + 1) * NF, :].astype(BF16)
        for k in range(K):
            part = jnp.dot(flux, w_ref[b, k], preferred_element_type=F32)
            out_ref[pos_ref[k, step * per + b]] = part.astype(BF16)


def flux_specs(per):
    return [
        SMEM,
        pl.BlockSpec((RANKS, COLS), lambda i: (0, 0)),
        pl.BlockSpec((per, COLS), lambda i: (i, 0)),
        pl.BlockSpec((per, COLS), lambda i: (i, 0)),
        pl.BlockSpec((NF, per, COLS), lambda i: (0, i, 0)),
        pl.BlockSpec((per, K, COLS, COLS), lambda i: (i, 0, 0, 0)),
    ]


def ocean_flux(pos, labels, air, prior, factors, weights, per=16):
    return pl.pallas_call(
        functools.partial(ocean_flux_body, per),
        out_shape=jax.ShapeDtypeStruct((RANKS * OCEAN_SLOTS, NF, COLS), BF16),
        grid=(ROWS // per,),
        in_specs=flux_specs(per),
        out_specs=pl.BlockSpec((RANKS * OCEAN_SLOTS, NF, COLS), lambda i: (0, 0, 0)),
        scratch_shapes=[pltpu.VMEM((per * NF, COLS), F32)],
        compiler_params=pltpu.CompilerParams(vmem_limit_bytes=32 << 20),
    )(pos, labels, air, prior, factors, weights)


def atmos_flux_body(
    per, pos_ref, label_ref, air_ref, prior_ref, factor_ref, w_ref, share_ref, out_ref, packed, rows
):
    step = pl.program_id(0)

    @pl.when(step == 0)
    def _():
        packed[...] = jnp.zeros_like(packed)
        for d in range(RANKS):
            packed[d * ATMOS_SLOTS + CAP : d * ATMOS_SLOTS + CAP + 1, :] = label_ref[d : d + 1, :]

    mixed = share_ref[0, 0] * factor_ref[0]
    for f in range(1, NF):
        mixed += share_ref[0, f] * factor_ref[f]
    flux = mixed * (air_ref[...] - prior_ref[...])
    high = flux.astype(BF16).astype(F32)
    rows[...] = jnp.zeros_like(rows)
    rows[pl.ds(0, per, stride=8), :] = high
    rows[pl.ds(1, per, stride=8), :] = flux - high
    for b in range(per):
        pair = rows[b * 8 : (b + 1) * 8, :].astype(BF16)
        for k in range(K):
            part = jnp.dot(pair, w_ref[b, k], preferred_element_type=F32)
            packed[pl.ds(pos_ref[K + k, step * per + b], 1), :] = part[0:1, :] + part[1:2, :]

    @pl.when(step == pl.num_programs(0) - 1)
    def _():
        out_ref[...] = packed[...].astype(BF16).reshape(RANKS, ATMOS_SLOTS, COLS)


def atmos_flux(pos, labels, air, prior, factors, weights, share, per=16):
    return pl.pallas_call(
        functools.partial(atmos_flux_body, per),
        out_shape=jax.ShapeDtypeStruct((RANKS, ATMOS_SLOTS, COLS), BF16),
        grid=(ROWS // per,),
        in_specs=flux_specs(per) + [SMEM],
        out_specs=pl.BlockSpec((RANKS, ATMOS_SLOTS, COLS), lambda i: (0, 0, 0)),
        scratch_shapes=[
            pltpu.VMEM((RANKS * ATMOS_SLOTS, COLS), F32),
            pltpu.VMEM((per * 8, COLS), F32),
        ],
        compiler_params=pltpu.CompilerParams(vmem_limit_bytes=32 << 20),
    )(pos, labels, air, prior, factors, weights, share)


def iotas():
    return (
        lax.broadcasted_iota(jnp.int32, (ROWS, COLS), 0),
        lax.broadcasted_iota(jnp.int32, (ROWS, COLS), 1),
    )


def side_lanes(lane, level):
    return (lane == 2 * level) | (lane == (2 * level - 1) % COLS)


def packed_sides(fields, lane):
    packed = jnp.zeros((ROWS, COLS), F32)
    for l, field in enumerate(fields):
        turned = field if l == 0 else pltpu.roll(field, 2 * l, 1)
        packed = jnp.where(side_lanes(lane, l), turned, packed)
    return packed


def unpacked_sides(packed, level):
    return packed if level == 0 else pltpu.roll(packed, COLS - 2 * level, 1)


def row_above(field, before, row):
    return jnp.where(row == 0, before, pltpu.roll(field, 1, 0))


def row_below(field, after, row):
    return jnp.where(row == ROWS - 1, after, pltpu.roll(field, ROWS - 1, 0))


def column_left(field, sides, lane):
    return pltpu.roll(jnp.where(lane == COLS - 1, sides, field), 1, 1)


def column_right(field, sides, lane):
    return pltpu.roll(jnp.where(lane == 0, sides, field), COLS - 1, 1)


def second_along(field, axis, index, extent):
    phase = index % 4
    total = None
    for shift in range(-3, 4):
        factor = jnp.zeros(index.shape, F32)
        for p in range(4):
            if 0 <= p + shift < 4:
                factor = jnp.where(phase == p, F32(SECOND[p, p + shift]), factor)
        moved = field if shift == 0 else pltpu.roll(field, (-shift) % extent, axis)
        total = factor * moved if total is None else total + factor * moved
    return total


def atmos_local(levels, row, lane):
    out = []
    for l, field in enumerate(levels):
        below, above = levels[max(l - 1, 0)], levels[min(l + 1, LEV - 1)]
        along = second_along(field, 0, row, ROWS) + second_along(field, 1, lane, COLS)
        out.append(field + ATMOS_DIFFUSION * along + MIXING * (above + below - 2.0 * field))
    return out


def assembled_rows(field, before, after, row):
    phase = row % 4
    return jnp.where(
        phase == 3,
        0.5 * (field + row_below(field, after, row)),
        jnp.where(phase == 0, 0.5 * (field + row_above(field, before, row)), field),
    )


def assembled_columns(field, sides, lane):
    phase = lane % 4
    return jnp.where(
        phase == 3,
        0.5 * (field + column_right(field, sides, lane)),
        jnp.where(phase == 0, 0.5 * (field + column_left(field, sides, lane)), field),
    )


def assembled(levels_ref, sides_ref, before_ref, after_ref, sides_row, row, lane):
    end = sides_row
    sides = assembled_rows(
        sides_ref[...], before_ref[end : end + 1, :], after_ref[end : end + 1, :], row
    )
    out = []
    for l in range(LEV):
        half = assembled_rows(
            levels_ref[l], before_ref[l : l + 1, :], after_ref[l : l + 1, :], row
        )
        out.append(assembled_columns(half, unpacked_sides(sides, l), lane))
    return out


def neighbour_counts(table_ref, row, lane):
    own = (row + 1) * (COLS + 2) + lane + 1
    counts = {}
    for dr in (-1, 0, 1):
        for dc in (-1, 0, 1):
            if dr or dc:
                target = own + (dr * (COLS + 2) + dc)
                count = jnp.zeros((ROWS, COLS), F32)
                for e in range(table_ref.shape[0]):
                    count += jnp.where(table_ref[e] == target, 1.0, 0.0)
                counts[dr, dc] = count
    return counts


def neighbour_spread(field, sides, before, after, sides_before, sides_after, counts, row, lane):
    total = jnp.zeros((ROWS, COLS), F32)
    for dr in (-1, 0, 1):
        if dr == 0:
            line, ends = field, sides
        elif dr == -1:
            line, ends = row_above(field, before, row), row_above(sides, sides_before, row)
        else:
            line, ends = row_below(field, after, row), row_below(sides, sides_after, row)
        total += counts[dr, -1] * (column_left(line, ends, lane) - field)
        total += counts[dr, 1] * (column_right(line, ends, lane) - field)
        if dr:
            total += counts[dr, 0] * (line - field)
    return total


def atmos_first_body(u_ref, sea_ref, out_ref, sides_ref):
    row, lane = iotas()
    moved = atmos_local([u_ref[l] for l in range(LEV)], row, lane)
    for l in range(LEV):
        out_ref[l] = moved[l]
    sides_ref[...] = packed_sides(moved + [sea_ref[0].astype(F32)], lane)


def atmos_second_body(
    u_ref, sides_ref, before_ref, after_ref, sea_ref, table_ref, out_ref, packed_ref, base_ref
):
    row, lane = iotas()
    level_list = assembled(u_ref, sides_ref, before_ref, after_ref, LEV + 1, row, lane)
    moved = atmos_local(level_list, row, lane)
    for l in range(LEV):
        out_ref[l] = moved[l]
    packed_ref[...] = packed_sides(moved, lane)
    top, under = sea_ref[0].astype(F32), sea_ref[1].astype(F32)
    sides = unpacked_sides(sides_ref[...], LEV)
    ends = [unpacked_sides(r[LEV + 1 : LEV + 2, :], LEV) for r in (before_ref, after_ref)]
    spread = neighbour_spread(
        top,
        sides,
        before_ref[LEV : LEV + 1, :],
        after_ref[LEV : LEV + 1, :],
        ends[0],
        ends[1],
        neighbour_counts(table_ref, row, lane),
        row,
        lane,
    )
    base_ref[...] = top + OCEAN_DIFFUSION * spread + MIXING * (under - top)


def atmos_third_body(u_ref, sides_ref, before_ref, after_ref, out_ref):
    row, lane = iotas()
    final = assembled(u_ref, sides_ref, before_ref, after_ref, LEV, row, lane)
    for l in range(LEV):
        out_ref[l] = final[l]


def ocean_sides_body(o_ref, sides_ref):
    _, lane = iotas()
    sides_ref[...] = packed_sides([o_ref[l] for l in range(LEV)], lane)


def ocean_base_body(o_ref, sides_ref, before_ref, after_ref, table_ref, out_ref, counts_ref):
    row, lane = iotas()
    order = [(dr, dc) for dr in (-1, 0, 1) for dc in (-1, 0, 1) if dr or dc]
    found = neighbour_counts(table_ref, row, lane)
    for n, key in enumerate(order):
        counts_ref[n] = found[key]
    for l in range(LEV):
        field = o_ref[l]
        sides = unpacked_sides(sides_ref[...], l)
        ends = [unpacked_sides(r[LEV : LEV + 1, :], l) for r in (before_ref, after_ref)]
        spread = neighbour_spread(
            field,
            sides,
            before_ref[l : l + 1, :],
            after_ref[l : l + 1, :],
            ends[0],
            ends[1],
            {key: counts_ref[n] for n, key in enumerate(order)},
            row,
            lane,
        )
        below, above = o_ref[max(l - 1, 0)], o_ref[min(l + 1, LEV - 1)]
        out_ref[l] = field + OCEAN_DIFFUSION * spread + MIXING * (above + below - 2.0 * field)


def exchanged(levels, sides):
    size = lax.axis_size("gx")
    up = [(i, (i + 1) % size) for i in range(size)]
    down = [(j, i) for i, j in up]
    sides = lax.ppermute(sides, "gy", [(0, 1), (1, 0)])
    last = jnp.concatenate([v[:, ROWS - 1, :] for v in levels] + [sides[ROWS - 1 :, :]], axis=0)
    first = jnp.concatenate([v[:, 0, :] for v in levels] + [sides[:1, :]], axis=0)
    return sides, lax.ppermute(last, "gx", up), lax.ppermute(first, "gx", down)


def row_hits(labels):
    width = ATMOS_SLOTS
    shape = (RANKS, width, COLS)
    diagonal = lax.broadcasted_iota(jnp.int32, shape, 1) == lax.broadcasted_iota(jnp.int32, shape, 2)
    spread = jnp.where(diagonal, labels[:, None, :], 0.0)
    column = jnp.sum(spread, axis=2, keepdims=True).reshape(RANKS * width, 1)
    slot = lax.broadcasted_iota(jnp.int32, (RANKS, width, 1), 1).reshape(RANKS * width, 1)
    column = jnp.where(slot < CAP, column, -1.0).astype(jnp.int32)
    rows = lax.broadcasted_iota(jnp.int32, (RANKS * width, ROWS), 1)
    return jnp.where(column == rows, 1.0, 0.0).astype(BF16)


def top_body(arrived_ref, base_ref, out_ref):
    arrived = arrived_ref[...].astype(F32)
    hits = row_hits(arrived[:, CAP, :])
    values = arrived.reshape(RANKS * ATMOS_SLOTS, COLS).astype(BF16)
    pushed = lax.dot_general(hits, values, (((0,), (0,)), ((), ())), preferred_element_type=F32)
    top = (base_ref[...] + pushed).astype(BF16)
    picked = jnp.dot(hits, top, preferred_element_type=F32)
    out_ref[...] = picked.astype(BF16).reshape(RANKS, ATMOS_SLOTS, COLS)


def sums_body(arrived_ref, base_ref, share_ref, out_ref, first_ref, wide, hits):
    f = pl.program_id(0)
    slots = RANKS * OCEAN_SLOTS

    @pl.when(f == 0)
    def _():
        wide[...] = arrived_ref[...].astype(F32).reshape(slots * NF, COLS)
        width = OCEAN_SLOTS * NF
        labels = wide[pl.ds(CAP * NF, RANKS, stride=width), :]
        hits[...] = row_hits(labels)
        out_ref[...] = base_ref[...]

    parts = []
    for d in range(RANKS):
        begin = d * OCEAN_SLOTS * NF + f
        parts.append(wide[pl.ds(begin, 16, stride=NF), :])
        parts.append(wide[pl.ds(begin + 16 * NF, 3, stride=NF), :])
        parts.append(jnp.zeros((5, COLS), F32))
    values = jnp.concatenate(parts, axis=0).astype(BF16)
    forcing = lax.dot_general(
        hits[...], values, (((0,), (0,)), ((), ())), preferred_element_type=F32
    )
    for l in range(LEV):
        out_ref[l] += share_ref[l, f] * forcing

    @pl.when(f == 0)
    def _():
        first_ref[...] = forcing


def ocean_sums(arrived, base, share):
    whole = lambda shape: pl.BlockSpec(shape, lambda f: (0,) * len(shape))
    slots = RANKS * OCEAN_SLOTS
    return pl.pallas_call(
        sums_body,
        out_shape=(
            jax.ShapeDtypeStruct((LEV, ROWS, COLS), F32),
            jax.ShapeDtypeStruct((ROWS, COLS), F32),
        ),
        grid=(NF,),
        in_specs=[whole((slots, NF, COLS)), whole((LEV, ROWS, COLS)), SMEM],
        out_specs=(whole((LEV, ROWS, COLS)), whole((ROWS, COLS))),
        scratch_shapes=[
            pltpu.VMEM((slots * NF, COLS), F32),
            pltpu.VMEM((RANKS * ATMOS_SLOTS, ROWS), BF16),
        ],
        compiler_params=pltpu.CompilerParams(vmem_limit_bytes=40 << 20),
    )(arrived, base, share)


def remap_body(per, pos_ref, arrived_ref, w_ref, out_ref, wide):
    step = pl.program_id(0)

    @pl.when(step == 0)
    def _():
        wide[...] = arrived_ref[...].astype(F32).reshape(RANKS * ATMOS_SLOTS, COLS)

    for b in range(per):
        total = None
        for k in range(K):
            value = wide[pl.ds(pos_ref[K + k, step * per + b], 1), :].astype(BF16)
            part = lax.dot_general(
                value, w_ref[b, k], (((1,), (1,)), ((), ())), preferred_element_type=F32
            )
            total = part if total is None else total + part
        out_ref[b : b + 1, :] = total


def remap(pos, arrived, weights, per=16):
    return pl.pallas_call(
        functools.partial(remap_body, per),
        out_shape=jax.ShapeDtypeStruct((ROWS, COLS), F32),
        grid=(ROWS // per,),
        in_specs=[
            SMEM,
            pl.BlockSpec((RANKS, ATMOS_SLOTS, COLS), lambda i: (0, 0, 0)),
            pl.BlockSpec((per, K, COLS, COLS), lambda i: (i, 0, 0, 0)),
        ],
        out_specs=pl.BlockSpec((per, COLS), lambda i: (i, 0)),
        scratch_shapes=[pltpu.VMEM((RANKS * ATMOS_SLOTS, COLS), F32)],
        compiler_params=pltpu.CompilerParams(vmem_limit_bytes=32 << 20),
    )(pos, arrived, weights)


def to_peers(payload):
    return lax.all_to_all(payload, ("gx", "gy"), split_axis=0, concat_axis=0, tiled=True)


def local(
    layered_heat_profile,
    prior_marine_heat,
    transfer_factor_table,
    depth_fraction_matrix,
    adjacent_cell_table,
    destination_water_peer,
    destination_water_line,
    interpolation_matrix_blocks,
):
    is_atmosphere_side = lax.axis_index("comp") == 0
    own = layered_heat_profile[0]
    block = jax.ShapeDtypeStruct((LEV, ROWS, COLS), F32)
    plane = jax.ShapeDtypeStruct((ROWS, COLS), F32)

    air = lax.ppermute(own[0], "comp", [(0, 1)])
    sea = lax.ppermute(own[:2].astype(BF16), "comp", [(1, 0)])
    pos, labels = positions(destination_water_peer, destination_water_line)

    def early_flux():
        return atmos_flux(
            pos,
            labels,
            own[0],
            prior_marine_heat,
            transfer_factor_table,
            interpolation_matrix_blocks,
            depth_fraction_matrix,
        )

    packed = lax.cond(
        is_atmosphere_side,
        early_flux,
        lambda: jnp.zeros((RANKS, ATMOS_SLOTS, COLS), BF16),
    )

    def atmosphere():
        arrived = to_peers(packed)
        moved, sides = call(atmos_first_body, (block, plane), [VMEM, VMEM])(own, sea)
        halo = exchanged([moved, sea[:1].astype(F32)], sides)
        moved, sides, base = call(atmos_second_body, (block, plane, plane), [VMEM] * 6)(
            moved, *halo, sea, adjacent_cell_table
        )
        picked = call(
            top_body, jax.ShapeDtypeStruct((RANKS, ATMOS_SLOTS, COLS), BF16), [VMEM, VMEM]
        )(arrived, base)
        returned = to_peers(picked)
        halo = exchanged([moved], sides)
        final = call(atmos_third_body, block, [VMEM] * 4)(moved, *halo)
        return final, remap(pos, returned, interpolation_matrix_blocks)

    def ocean():
        payload = ocean_flux(
            pos,
            labels,
            air,
            prior_marine_heat,
            transfer_factor_table,
            interpolation_matrix_blocks,
        )
        arrived = to_peers(payload.reshape(RANKS, OCEAN_SLOTS * NF, COLS))
        sides = call(ocean_sides_body, plane, [VMEM])(own)
        halo = exchanged([own], sides)
        base = call(
            ocean_base_body,
            block,
            [VMEM] * 5,
            scratch_shapes=[pltpu.VMEM((8, ROWS, COLS), F32)],
        )(own, *halo, adjacent_cell_table)
        return ocean_sums(
            arrived.reshape(RANKS * OCEAN_SLOTS, NF, COLS), base, depth_fraction_matrix
        )

    state, plane_out = lax.cond(is_atmosphere_side, atmosphere, ocean)
    return state[None], plane_out[None]


def solution(mesh):
    return jax.shard_map(
        local,
        mesh=mesh,
        in_specs=(
            P("comp", None, "gx", "gy"),
            P("gx", "gy"),
            P(None, "gx", "gy"),
            P(),
            P(None, "gx", "gy"),
            P(("gx", "gy"), None),
            P(("gx", "gy"), None),
            P(("gx", "gy"), None, None, None),
        ),
        out_specs=(P("comp", None, "gx", "gy"), P("comp", "gx", "gy")),
        check_vma=False,
    )
```

```python
import functools

import jax
import jax.numpy as jnp
import numpy as np
from jax import lax
from jax.experimental import pallas as pl
from jax.experimental.pallas import tpu as pltpu
from jax.sharding import PartitionSpec as P

ATMOS_DIFFUSION = 0.01
MIXING = 0.2
OCEAN_DIFFUSION = 0.12

RANKS = 64
CAP = 18
LEV = 8
NF = 8
ROWS = 256
COLS = 128
K = 2
OCEAN_SLOTS = 19
ATMOS_SLOTS = 24

VMEM = pl.BlockSpec(memory_space=pltpu.VMEM)
SMEM = pl.BlockSpec(memory_space=pltpu.SMEM)
ANY = pl.BlockSpec(memory_space=pl.ANY)
F32 = jnp.float32
BF16 = jnp.bfloat16


def second_table():
    gll_nodes = np.array([-1.0, -1.0 / np.sqrt(5.0), 1.0 / np.sqrt(5.0), 1.0])
    poly_order = 3
    legendre = (5.0 * gll_nodes**3 - 3.0 * gll_nodes) / 2.0
    derivative = np.zeros((4, 4))
    for row_index in range(4):
        for col_index in range(4):
            if row_index != col_index:
                derivative[row_index, col_index] = legendre[row_index] / (
                    legendre[col_index] * (gll_nodes[row_index] - gll_nodes[col_index])
                )
    derivative[0, 0] = -poly_order * (poly_order + 1) / 4.0
    derivative[3, 3] = poly_order * (poly_order + 1) / 4.0
    return derivative @ derivative


SECOND = second_table()


def call(body, out_shape, specs, **params):
    return pl.pallas_call(
        body,
        out_shape=out_shape,
        in_specs=specs,
        out_specs=jax.tree.map(lambda _: VMEM, out_shape),
        compiler_params=pltpu.CompilerParams(vmem_limit_bytes=params.pop("vmem", 24 << 20)),
        **params,
    )


def shadow_call(body, out_shape, specs, **params):
    nothing = pl.CostEstimate(flops=0, bytes_accessed=0, transcendentals=0)
    return call(body, out_shape, specs, cost_estimate=nothing, **params)


def positions_body(peer_ref, line_ref, pos_ref, label_ref):
    count = ROWS * K
    peer = jnp.concatenate([peer_ref[k : k + 1, :] for k in range(K)], axis=1)
    line = jnp.concatenate([line_ref[k : k + 1, :] for k in range(K)], axis=1)
    hits = lax.broadcasted_iota(jnp.int32, (RANKS, count), 0) == peer
    hits_f = jnp.where(hits, 1.0, 0.0)
    earlier = lax.broadcasted_iota(jnp.int32, (count, count), 0) < lax.broadcasted_iota(
        jnp.int32, (count, count), 1
    )
    before = jnp.dot(
        hits_f.astype(BF16),
        jnp.where(earlier, 1.0, 0.0).astype(BF16),
        preferred_element_type=F32,
    )
    slot = jnp.sum(hits_f * before, axis=0, keepdims=True).astype(jnp.int32)
    for width, at in ((OCEAN_SLOTS, 0), (ATMOS_SLOTS, K)):
        position = peer * width + slot
        for k in range(K):
            pos_ref[at + k : at + k + 1, :] = position[:, k * ROWS : (k + 1) * ROWS]
    slot_hits = lax.broadcasted_iota(jnp.int32, (COLS, count), 0) == slot
    shifted = jnp.where(hits, (line + 1).astype(F32), 0.0).astype(BF16)
    label_ref[...] = (
        lax.dot_general(
            shifted,
            jnp.where(slot_hits, 1.0, 0.0).astype(BF16),
            (((1,), (1,)), ((), ())),
            preferred_element_type=F32,
        )
        - 1.0
    )


def positions(peer, line):
    return call(
        positions_body,
        (
            jax.ShapeDtypeStruct((2 * K, ROWS), jnp.int32),
            jax.ShapeDtypeStruct((RANKS, COLS), F32),
        ),
        [VMEM, VMEM],
    )(peer.T, line.T)


FLUX_ROWS = 16
REMAP_ROWS = 32


def weight_copies(source, held, sems, per):
    def copy(c):
        part = pl.ds(c * per, per)
        return pltpu.make_async_copy(source.at[part], held.at[part], sems.at[c])

    return copy


def side_by_side(held, b):
    return jnp.concatenate([held[b, k] for k in range(K)], axis=1)


def ocean_flux_body(
    pos_ref, label_ref, air_ref, prior_ref, factor_ref, w_ref, out_ref, held, rows, sems
):
    copy = weight_copies(w_ref, held, sems, FLUX_ROWS)
    for c in range(ROWS // FLUX_ROWS):
        copy(c).start()
    out_ref[...] = jnp.zeros_like(out_ref)
    for d in range(RANKS):
        out_ref[d * OCEAN_SLOTS + CAP] = jnp.broadcast_to(
            label_ref[d : d + 1, :], (NF, COLS)
        ).astype(BF16)
    difference = air_ref[...] - prior_ref[...]
    for f in range(NF):
        rows[pl.ds(f, ROWS, stride=NF), :] = factor_ref[f] * difference

    @pl.loop(0, ROWS // FLUX_ROWS)
    def _(c):
        copy(c).wait()
        for i in range(FLUX_ROWS):
            b = c * FLUX_ROWS + i
            flux = rows[pl.ds(pl.multiple_of(b * NF, NF), NF), :].astype(BF16)
            part = jnp.dot(flux, side_by_side(held, b), preferred_element_type=F32).astype(BF16)
            for k in range(K):
                out_ref[pos_ref[k, b]] = part[:, k * COLS : (k + 1) * COLS]


WEIGHTS_HELD = [
    pltpu.VMEM((ROWS, K, COLS, COLS), BF16),
]


def ocean_flux(pos, labels, air, prior, factors, weights):
    return pl.pallas_call(
        ocean_flux_body,
        out_shape=jax.ShapeDtypeStruct((RANKS * OCEAN_SLOTS, NF, COLS), BF16),
        in_specs=[SMEM, VMEM, VMEM, VMEM, VMEM, ANY],
        out_specs=VMEM,
        scratch_shapes=WEIGHTS_HELD
        + [
            pltpu.VMEM((ROWS * NF, COLS), F32),
            pltpu.SemaphoreType.DMA((ROWS // FLUX_ROWS,)),
        ],
        compiler_params=pltpu.CompilerParams(vmem_limit_bytes=32 << 20),
    )(pos, labels, air, prior, factors, weights)


def atmos_flux_body(
    pos_ref,
    label_ref,
    air_ref,
    prior_ref,
    factor_ref,
    w_ref,
    share_ref,
    out_ref,
    held,
    packed,
    rows,
    sems,
):
    copy = weight_copies(w_ref, held, sems, FLUX_ROWS)
    for c in range(ROWS // FLUX_ROWS):
        copy(c).start()
    packed[...] = jnp.zeros_like(packed)
    for d in range(RANKS):
        packed[d * ATMOS_SLOTS + CAP : d * ATMOS_SLOTS + CAP + 1, :] = label_ref[d : d + 1, :]
    mixed = share_ref[0, 0] * factor_ref[0]
    for f in range(1, NF):
        mixed += share_ref[0, f] * factor_ref[f]
    flux = mixed * (air_ref[...] - prior_ref[...])
    high = flux.astype(BF16).astype(F32)
    rows[...] = jnp.zeros_like(rows)
    rows[pl.ds(0, ROWS, stride=8), :] = high
    rows[pl.ds(1, ROWS, stride=8), :] = flux - high

    @pl.loop(0, ROWS // FLUX_ROWS)
    def _(c):
        copy(c).wait()
        for i in range(FLUX_ROWS):
            b = c * FLUX_ROWS + i
            pair = rows[pl.ds(pl.multiple_of(b * 8, 8), 8), :].astype(BF16)
            part = jnp.dot(pair, side_by_side(held, b), preferred_element_type=F32)
            part = part[0:1, :] + part[1:2, :]
            for k in range(K):
                packed[pl.ds(pos_ref[K + k, b], 1), :] = part[:, k * COLS : (k + 1) * COLS]

    out_ref[...] = packed[...].astype(BF16).reshape(RANKS, ATMOS_SLOTS, COLS)


def atmos_flux(pos, labels, air, prior, factors, weights, share):
    return pl.pallas_call(
        atmos_flux_body,
        out_shape=jax.ShapeDtypeStruct((RANKS, ATMOS_SLOTS, COLS), BF16),
        in_specs=[SMEM, VMEM, VMEM, VMEM, VMEM, ANY, SMEM],
        out_specs=VMEM,
        scratch_shapes=WEIGHTS_HELD
        + [
            pltpu.VMEM((RANKS * ATMOS_SLOTS, COLS), F32),
            pltpu.VMEM((ROWS * 8, COLS), F32),
            pltpu.SemaphoreType.DMA((ROWS // FLUX_ROWS,)),
        ],
        compiler_params=pltpu.CompilerParams(vmem_limit_bytes=32 << 20),
    )(pos, labels, air, prior, factors, weights, share)


WIDE = 8
EXTENDED = ROWS + 2 * WIDE


def iotas(rows):
    return (
        lax.broadcasted_iota(jnp.int32, (rows, COLS), 0),
        lax.broadcasted_iota(jnp.int32, (rows, COLS), 1),
    )


def turned(field, lanes):
    lanes = lanes % COLS
    return field if lanes == 0 else pltpu.roll(field, lanes, 1)


def sides_body(u_ref, out_ref):
    _, lane = iotas(ROWS)
    packed = jnp.zeros((ROWS, COLS), F32)
    for l in range(LEV):
        packed = jnp.where(lane // (2 * WIDE) == l, turned(u_ref[l], WIDE + 2 * WIDE * l), packed)
    out_ref[...] = packed


def mate_ends(sides, level):
    return turned(sides, -(2 * WIDE * level + WIDE))


def column_left(field, ends, lane):
    return pltpu.roll(jnp.where(lane == COLS - 1, ends, field), 1, 1)


def column_right(field, ends, lane):
    return pltpu.roll(jnp.where(lane == 0, ends, field), COLS - 1, 1)


def second_along(field, axis, index, extent):
    phase = index % 4
    total = None
    for shift in range(-3, 4):
        factor = jnp.zeros(index.shape, F32)
        for p in range(4):
            if 0 <= p + shift < 4:
                factor = jnp.where(phase == p, F32(SECOND[p, p + shift]), factor)
        moved = field if shift == 0 else pltpu.roll(field, (-shift) % extent, axis)
        total = factor * moved if total is None else total + factor * moved
    return total


def diffused(field, above, below, row, lane):
    along = second_along(field, 0, row, EXTENDED) + second_along(field, 1, lane, COLS)
    return field + ATMOS_DIFFUSION * along + MIXING * (above + below - 2.0 * field)


def assembled(field, axis, phase, ahead, behind):
    return jnp.where(
        phase == 3,
        0.5 * (field + ahead),
        jnp.where(phase == 0, 0.5 * (field + behind), field),
    )


def assembled_rows(field, row):
    ahead = pltpu.roll(field, EXTENDED - 1, 0)
    return assembled(field, 0, row % 4, ahead, pltpu.roll(field, 1, 0))


def substeps_body(u_ref, sides_ref, before_ref, after_ref, _, out_ref, main, moved):
    row, lane = iotas(EXTENDED)
    phase, part = lane % 4, lane % (2 * WIDE)
    for l in range(LEV):
        main[l, :WIDE] = before_ref[l]
        main[l, WIDE : WIDE + ROWS] = u_ref[l]
        main[l, WIDE + ROWS :] = after_ref[l]
    sides = jnp.concatenate([before_ref[LEV], sides_ref[...], after_ref[LEV]], axis=0)
    for substep in range(2):
        over = jnp.where(lane < COLS - 2 * WIDE, turned(sides, -2 * WIDE), sides)
        under = jnp.where(lane >= 2 * WIDE, turned(sides, 2 * WIDE), sides)
        sides = assembled_rows(diffused(sides, over, under, row, lane), row)
        edges = jnp.zeros((EXTENDED, COLS), F32)
        for l in range(LEV):
            field = main[l]
            half = assembled_rows(
                diffused(field, main[min(l + 1, LEV - 1)], main[max(l - 1, 0)], row, lane), row
            )
            if substep == 0:
                first = turned(half, 2 * WIDE * l + WIDE - 1)
                last = turned(half, 2 * WIDE * l + WIDE + 1)
                own_level = lane // (2 * WIDE) == l
                edges = jnp.where(own_level, jnp.where(part < WIDE, first, last), edges)
            ends = mate_ends(sides, l)
            whole = assembled(
                half, 1, phase, column_right(half, ends, lane), column_left(half, ends, lane)
            )
            if substep == 0:
                moved[l] = whole
            else:
                out_ref[l] = whole[WIDE : WIDE + ROWS]
        if substep == 0:
            ahead = jnp.where(part == WIDE - 1, edges, turned(sides, -1))
            behind = jnp.where(part == WIDE, edges, turned(sides, 1))
            sides = assembled(sides, 1, phase, ahead, behind)
            for l in range(LEV):
                main[l] = moved[l]


ORDER = [(dr, dc) for dr in (-1, 0, 1) for dc in (-1, 0, 1) if dr or dc]


def neighbour_counts(table_ref, row, lane):
    own = (row + 1) * (COLS + 2) + lane + 1
    counts = []
    for dr, dc in ORDER:
        target = own + (dr * (COLS + 2) + dc)
        count = jnp.zeros((ROWS, COLS), F32)
        for e in range(table_ref.shape[0]):
            count += jnp.where(table_ref[e] == target, 1.0, 0.0)
        counts.append(count)
    return counts


def neighbour_spread(field, ends, before, after, ends_before, ends_after, counts, row, lane):
    total = jnp.zeros((ROWS, COLS), F32)
    lines = {
        0: (field, ends),
        -1: tuple(
            jnp.where(row == 0, edge, pltpu.roll(v, 1, 0))
            for v, edge in ((field, before), (ends, ends_before))
        ),
        1: tuple(
            jnp.where(row == ROWS - 1, edge, pltpu.roll(v, ROWS - 1, 0))
            for v, edge in ((field, after), (ends, ends_after))
        ),
    }
    for (dr, dc), count in zip(ORDER, counts):
        line, line_ends = lines[dr]
        if dc == -1:
            line = column_left(line, line_ends, lane)
        elif dc == 1:
            line = column_right(line, line_ends, lane)
        total += count * (line - field)
    return total


def top_base_body(top_ref, under_ref, mate_ref, before_ref, after_ref, table_ref, out_ref):
    row, lane = iotas(ROWS)
    top = top_ref[...]
    spread = neighbour_spread(
        top,
        mate_ref[...],
        before_ref[LEV + 1, WIDE - 1 :, :],
        after_ref[LEV + 1, :1, :],
        before_ref[LEV + 2, WIDE - 1 :, :],
        after_ref[LEV + 2, :1, :],
        neighbour_counts(table_ref, row, lane),
        row,
        lane,
    )
    out_ref[...] = top + OCEAN_DIFFUSION * spread + MIXING * (under_ref[...].astype(F32) - top)


def ocean_base_body(o_ref, sides_ref, before_ref, after_ref, table_ref, out_ref, counts_ref):
    row, lane = iotas(ROWS)
    for n, count in enumerate(neighbour_counts(table_ref, row, lane)):
        counts_ref[n] = count
    for l in range(LEV):
        field = o_ref[l]
        spread = neighbour_spread(
            field,
            mate_ends(sides_ref[...], l),
            before_ref[l, WIDE - 1 :, :],
            after_ref[l, :1, :],
            mate_ends(before_ref[LEV, WIDE - 1 :, :], l),
            mate_ends(after_ref[LEV, :1, :], l),
            [counts_ref[n] for n in range(len(ORDER))],
            row,
            lane,
        )
        below, above = o_ref[max(l - 1, 0)], o_ref[min(l + 1, LEV - 1)]
        out_ref[l] = field + OCEAN_DIFFUSION * spread + MIXING * (above + below - 2.0 * field)


def exchanged(levels, planes):
    size = lax.axis_size("gx")
    up = [(i, (i + 1) % size) for i in range(size)]
    down = [(j, i) for i, j in up]
    mate = lax.ppermute(planes, "gy", [(0, 1), (1, 0)])
    parts = [levels, mate[:1], planes[1:], mate[1:]]
    last = jnp.concatenate([v[:, ROWS - WIDE :, :] for v in parts], axis=0)
    first = jnp.concatenate([v[:, :WIDE, :] for v in parts], axis=0)
    return mate, lax.ppermute(last, "gx", up), lax.ppermute(first, "gx", down)


def row_hits(labels):
    width = ATMOS_SLOTS
    shape = (RANKS, width, COLS)
    diagonal = lax.broadcasted_iota(jnp.int32, shape, 1) == lax.broadcasted_iota(jnp.int32, shape, 2)
    spread = jnp.where(diagonal, labels[:, None, :], 0.0)
    column = jnp.sum(spread, axis=2, keepdims=True).reshape(RANKS * width, 1)
    slot = lax.broadcasted_iota(jnp.int32, (RANKS, width, 1), 1).reshape(RANKS * width, 1)
    column = jnp.where(slot < CAP, column, -1.0).astype(jnp.int32)
    rows = lax.broadcasted_iota(jnp.int32, (RANKS * width, ROWS), 1)
    return jnp.where(column == rows, 1.0, 0.0).astype(BF16)


def top_body(arrived_ref, base_ref, out_ref):
    arrived = arrived_ref[...].astype(F32)
    hits = row_hits(arrived[:, CAP, :])
    values = arrived.reshape(RANKS * ATMOS_SLOTS, COLS).astype(BF16)
    pushed = lax.dot_general(hits, values, (((0,), (0,)), ((), ())), preferred_element_type=F32)
    top = (base_ref[...] + pushed).astype(BF16)
    picked = jnp.dot(hits, top, preferred_element_type=F32)
    out_ref[...] = picked.astype(BF16).reshape(RANKS, ATMOS_SLOTS, COLS)


def sums_body(arrived_ref, base_ref, share_ref, out_ref, first_ref, wide):
    width = OCEAN_SLOTS * NF
    wide[...] = arrived_ref[...].astype(F32).reshape(RANKS * width, COLS)
    labels = wide[pl.ds(CAP * NF, RANKS, stride=width), :]
    by_slot = jnp.concatenate([labels, labels], axis=0).T
    row = lax.broadcasted_iota(jnp.int32, (ROWS, COLS), 0).astype(F32)
    lane = lax.broadcasted_iota(jnp.int32, (1, COLS), 1)
    pieces = []
    for s in range(0, CAP, 2):
        pair = jnp.where(lane < RANKS, by_slot[s : s + 1, :], by_slot[s + 1 : s + 2, :])
        pieces.append(jnp.where(row == pair, 1.0, 0.0).astype(BF16))
    hits = jnp.concatenate(pieces, axis=1)
    for f in range(NF):
        values = jnp.concatenate(
            [wide[pl.ds(s * NF + f, RANKS, stride=width), :] for s in range(CAP)], axis=0
        ).astype(BF16)
        forcing = jnp.dot(hits, values, preferred_element_type=F32)
        if f == 0:
            first_ref[...] = forcing
        for l in range(LEV):
            before = base_ref[l] if f == 0 else out_ref[l]
            out_ref[l] = before + share_ref[l, f] * forcing


def ocean_sums(arrived, base, share):
    return pl.pallas_call(
        sums_body,
        out_shape=(
            jax.ShapeDtypeStruct((LEV, ROWS, COLS), F32),
            jax.ShapeDtypeStruct((ROWS, COLS), F32),
        ),
        in_specs=[VMEM, VMEM, SMEM],
        out_specs=(VMEM, VMEM),
        scratch_shapes=[pltpu.VMEM((RANKS * OCEAN_SLOTS * NF, COLS), F32)],
        compiler_params=pltpu.CompilerParams(vmem_limit_bytes=24 << 20),
    )(arrived, base, share)


def remap_body(pos_ref, arrived_ref, w_ref, out_ref, held, wide, near, sems):
    copy = weight_copies(w_ref, held, sems, REMAP_ROWS)
    for c in range(ROWS // REMAP_ROWS):
        copy(c).start()
    wide[...] = arrived_ref[...].astype(F32).reshape(RANKS * ATMOS_SLOTS, COLS)
    lane = lax.broadcasted_iota(jnp.int32, (COLS, REMAP_ROWS), 1)

    @pl.loop(0, ROWS // REMAP_ROWS)
    def _(c):
        for i in range(REMAP_ROWS):
            for k in range(K):
                value = wide[pl.ds(pos_ref[K + k, c * REMAP_ROWS + i], 1), :]
                near[i : i + 1, k * COLS : (k + 1) * COLS] = value
        values = near[...].astype(BF16)
        copy(c).wait()
        block = held.at[pl.ds(c * REMAP_ROWS, REMAP_ROWS)]
        tiles = jnp.concatenate(
            [block[:, k].reshape(REMAP_ROWS * COLS, COLS) for k in range(K)], axis=1
        )
        crossed = lax.dot_general(
            tiles, values, (((1,), (1,)), ((), ())), preferred_element_type=F32
        )
        own = jnp.zeros((COLS, REMAP_ROWS), F32)
        for i in range(REMAP_ROWS):
            own = jnp.where(lane == i, crossed[i * COLS : (i + 1) * COLS], own)
        out_ref[pl.ds(pl.multiple_of(c * REMAP_ROWS, REMAP_ROWS), REMAP_ROWS), :] = own.T


def remap(pos, arrived, weights):
    return pl.pallas_call(
        remap_body,
        out_shape=jax.ShapeDtypeStruct((ROWS, COLS), F32),
        in_specs=[SMEM, VMEM, ANY],
        out_specs=VMEM,
        scratch_shapes=WEIGHTS_HELD
        + [
            pltpu.VMEM((RANKS * ATMOS_SLOTS, COLS), F32),
            pltpu.VMEM((REMAP_ROWS, K * COLS), F32),
            pltpu.SemaphoreType.DMA((ROWS // REMAP_ROWS,)),
        ],
        compiler_params=pltpu.CompilerParams(vmem_limit_bytes=32 << 20),
    )(pos, arrived, weights)


def to_peers(payload):
    return lax.all_to_all(payload, ("gx", "gy"), split_axis=0, concat_axis=0, tiled=True)


def local(
    layered_heat_profile,
    prior_marine_heat,
    transfer_factor_table,
    depth_fraction_matrix,
    adjacent_cell_table,
    destination_water_peer,
    destination_water_line,
    interpolation_matrix_blocks,
):
    is_atmosphere_side = lax.axis_index("comp") == 0
    own = layered_heat_profile[0]
    block = jax.ShapeDtypeStruct((LEV, ROWS, COLS), F32)
    plane = jax.ShapeDtypeStruct((ROWS, COLS), F32)
    swap = [(0, 1), (1, 0)]

    other_top = lax.ppermute(own[0], "comp", swap)
    other_under = lax.ppermute(own[1].astype(BF16), "comp", swap)
    pos, labels = positions(destination_water_peer, destination_water_line)

    def sides_of(levels):
        return shadow_call(sides_body, plane, [VMEM])(levels)

    def atmosphere_early():
        packed = atmos_flux(
            pos,
            labels,
            own[0],
            prior_marine_heat,
            transfer_factor_table,
            interpolation_matrix_blocks,
            depth_fraction_matrix,
        )
        rows = jnp.zeros((LEV + 1, WIDE, COLS), F32)
        return packed, jnp.zeros((1, ROWS, COLS), F32), rows, rows

    def ocean_early():
        halo = exchanged(own, sides_of(own)[None])
        return jnp.zeros((RANKS, ATMOS_SLOTS, COLS), BF16), *halo

    packed, *ocean_halo = lax.cond(is_atmosphere_side, atmosphere_early, ocean_early)

    def atmosphere():
        arrived = to_peers(packed)
        mate, before, after = exchanged(own, jnp.stack([sides_of(own), other_top]))
        base = shadow_call(top_base_body, plane, [VMEM] * 6)(
            other_top, other_under, mate[1], before, after, adjacent_cell_table
        )
        picked = call(
            top_body, jax.ShapeDtypeStruct((RANKS, ATMOS_SLOTS, COLS), BF16), [VMEM, VMEM]
        )(arrived, base)
        returned = to_peers(picked)
        wide = pltpu.VMEM((LEV, EXTENDED, COLS), F32)
        final = shadow_call(
            substeps_body, block, [VMEM] * 4 + [ANY], scratch_shapes=[wide, wide]
        )(own, mate[0], before, after, picked)
        return final, remap(pos, returned, interpolation_matrix_blocks)

    def ocean():
        payload = ocean_flux(
            pos,
            labels,
            other_top,
            prior_marine_heat,
            transfer_factor_table,
            interpolation_matrix_blocks,
        )
        arrived = to_peers(payload.reshape(RANKS, OCEAN_SLOTS * NF, COLS))
        mate, before, after = ocean_halo
        base = shadow_call(
            ocean_base_body,
            block,
            [VMEM] * 5,
            scratch_shapes=[pltpu.VMEM((len(ORDER), ROWS, COLS), F32)],
        )(own, mate[0], before, after, adjacent_cell_table)
        return ocean_sums(
            arrived.reshape(RANKS * OCEAN_SLOTS, NF, COLS), base, depth_fraction_matrix
        )

    state, plane_out = lax.cond(is_atmosphere_side, atmosphere, ocean)
    return state[None], plane_out[None]


def solution(mesh):
    return jax.shard_map(
        local,
        mesh=mesh,
        in_specs=(
            P("comp", None, "gx", "gy"),
            P("gx", "gy"),
            P(None, "gx", "gy"),
            P(),
            P(None, "gx", "gy"),
            P(("gx", "gy"), None),
            P(("gx", "gy"), None),
            P(("gx", "gy"), None, None, None),
        ),
        out_specs=(P("comp", None, "gx", "gy"), P("comp", "gx", "gy")),
        check_vma=False,
    )
```

```python
import functools

import jax
import jax.numpy as jnp
import numpy as np
from jax import lax
from jax.experimental import pallas as pl
from jax.experimental.pallas import tpu as pltpu
from jax.sharding import PartitionSpec as P

ATMOS_DIFFUSION = 0.01
MIXING = 0.2
OCEAN_DIFFUSION = 0.12

RANKS = 64
CAP = 18
LEV = 8
NF = 8
ROWS = 256
COLS = 128
K = 2
OCEAN_SLOTS = 19
ATMOS_SLOTS = 24

VMEM = pl.BlockSpec(memory_space=pltpu.VMEM)
SMEM = pl.BlockSpec(memory_space=pltpu.SMEM)
ANY = pl.BlockSpec(memory_space=pl.ANY)
F32 = jnp.float32
BF16 = jnp.bfloat16


def second_table():
    gll_nodes = np.array([-1.0, -1.0 / np.sqrt(5.0), 1.0 / np.sqrt(5.0), 1.0])
    poly_order = 3
    legendre = (5.0 * gll_nodes**3 - 3.0 * gll_nodes) / 2.0
    derivative = np.zeros((4, 4))
    for row_index in range(4):
        for col_index in range(4):
            if row_index != col_index:
                derivative[row_index, col_index] = legendre[row_index] / (
                    legendre[col_index] * (gll_nodes[row_index] - gll_nodes[col_index])
                )
    derivative[0, 0] = -poly_order * (poly_order + 1) / 4.0
    derivative[3, 3] = poly_order * (poly_order + 1) / 4.0
    return derivative @ derivative


SECOND = second_table()


def call(body, out_shape, specs, **params):
    return pl.pallas_call(
        body,
        out_shape=out_shape,
        in_specs=specs,
        out_specs=jax.tree.map(lambda _: VMEM, out_shape),
        compiler_params=pltpu.CompilerParams(vmem_limit_bytes=params.pop("vmem", 24 << 20)),
        **params,
    )


def shadow_call(body, out_shape, specs, **params):
    nothing = pl.CostEstimate(flops=0, bytes_accessed=0, transcendentals=0)
    return call(body, out_shape, specs, cost_estimate=nothing, **params)


def positions_body(peer_ref, line_ref, pos_ref, label_ref):
    count = ROWS * K
    peer = jnp.concatenate([peer_ref[k : k + 1, :] for k in range(K)], axis=1)
    line = jnp.concatenate([line_ref[k : k + 1, :] for k in range(K)], axis=1)
    hits = lax.broadcasted_iota(jnp.int32, (RANKS, count), 0) == peer
    hits_f = jnp.where(hits, 1.0, 0.0)
    earlier = lax.broadcasted_iota(jnp.int32, (count, count), 0) < lax.broadcasted_iota(
        jnp.int32, (count, count), 1
    )
    before = jnp.dot(
        hits_f.astype(BF16),
        jnp.where(earlier, 1.0, 0.0).astype(BF16),
        preferred_element_type=F32,
    )
    slot = jnp.sum(hits_f * before, axis=0, keepdims=True).astype(jnp.int32)
    for width, at in ((OCEAN_SLOTS, 0), (ATMOS_SLOTS, K)):
        position = peer * width + slot
        for k in range(K):
            pos_ref[at + k : at + k + 1, :] = position[:, k * ROWS : (k + 1) * ROWS]
    slot_hits = lax.broadcasted_iota(jnp.int32, (COLS, count), 0) == slot
    shifted = jnp.where(hits, (line + 1).astype(F32), 0.0).astype(BF16)
    label_ref[...] = (
        lax.dot_general(
            shifted,
            jnp.where(slot_hits, 1.0, 0.0).astype(BF16),
            (((1,), (1,)), ((), ())),
            preferred_element_type=F32,
        )
        - 1.0
    )


def positions(peer, line):
    return call(
        positions_body,
        (
            jax.ShapeDtypeStruct((2 * K, ROWS), jnp.int32),
            jax.ShapeDtypeStruct((RANKS, COLS), F32),
        ),
        [VMEM, VMEM],
    )(peer.T, line.T)


FLUX_ROWS = 16
REMAP_ROWS = 32


def weight_copies(source, held, sems, per):
    def copy(c):
        part = pl.ds(c * per, per)
        return pltpu.make_async_copy(source.at[part], held.at[part], sems.at[c])

    return copy


def side_by_side(held, b):
    return jnp.concatenate([held[b, k] for k in range(K)], axis=1)


def ocean_flux_body(
    pos_ref, label_ref, air_ref, prior_ref, factor_ref, w_ref, out_ref, held, packed, rows, sems
):
    copy = weight_copies(w_ref, held, sems, FLUX_ROWS)
    for c in range(ROWS // FLUX_ROWS):
        copy(c).start()
    packed[...] = jnp.zeros_like(packed)
    for d in range(RANKS):
        packed[d * OCEAN_SLOTS + CAP] = jnp.broadcast_to(
            label_ref[d : d + 1, :], (NF, COLS)
        ).astype(BF16)
    difference = air_ref[...] - prior_ref[...]
    for f in range(NF):
        rows[pl.ds(f, ROWS, stride=NF), :] = factor_ref[f] * difference

    @pl.loop(0, ROWS // FLUX_ROWS)
    def _(c):
        copy(c).wait()
        for i in range(FLUX_ROWS):
            b = c * FLUX_ROWS + i
            flux = rows[pl.ds(pl.multiple_of(b * NF, NF), NF), :].astype(BF16)
            part = jnp.dot(flux, side_by_side(held, b), preferred_element_type=F32).astype(BF16)
            for k in range(K):
                packed[pos_ref[k, b]] = part[:, k * COLS : (k + 1) * COLS]

    done = pltpu.make_async_copy(packed, out_ref, sems.at[ROWS // FLUX_ROWS])
    done.start()
    done.wait()


WEIGHTS_HELD = [
    pltpu.VMEM((ROWS, K, COLS, COLS), BF16),
]


def ocean_flux(pos, labels, air, prior, factors, weights):
    return pl.pallas_call(
        ocean_flux_body,
        out_shape=jax.ShapeDtypeStruct((RANKS * OCEAN_SLOTS, NF, COLS), BF16),
        in_specs=[SMEM, VMEM, VMEM, VMEM, VMEM, ANY],
        out_specs=pl.BlockSpec(memory_space=pltpu.HBM),
        scratch_shapes=WEIGHTS_HELD
        + [
            pltpu.VMEM((RANKS * OCEAN_SLOTS, NF, COLS), BF16),
            pltpu.VMEM((ROWS * NF, COLS), F32),
            pltpu.SemaphoreType.DMA((ROWS // FLUX_ROWS + 1,)),
        ],
        compiler_params=pltpu.CompilerParams(vmem_limit_bytes=32 << 20),
    )(pos, labels, air, prior, factors, weights)


def atmos_flux_body(
    pos_ref,
    label_ref,
    air_ref,
    prior_ref,
    factor_ref,
    w_ref,
    share_ref,
    out_ref,
    held,
    packed,
    rows,
    sems,
):
    copy = weight_copies(w_ref, held, sems, FLUX_ROWS)
    for c in range(ROWS // FLUX_ROWS):
        copy(c).start()
    packed[...] = jnp.zeros_like(packed)
    for d in range(RANKS):
        packed[d * ATMOS_SLOTS + CAP : d * ATMOS_SLOTS + CAP + 1, :] = label_ref[d : d + 1, :]
    mixed = share_ref[0, 0] * factor_ref[0]
    for f in range(1, NF):
        mixed += share_ref[0, f] * factor_ref[f]
    flux = mixed * (air_ref[...] - prior_ref[...])
    high = flux.astype(BF16).astype(F32)
    rows[...] = jnp.zeros_like(rows)
    rows[pl.ds(0, ROWS, stride=8), :] = high
    rows[pl.ds(1, ROWS, stride=8), :] = flux - high

    @pl.loop(0, ROWS // FLUX_ROWS)
    def _(c):
        copy(c).wait()
        for i in range(FLUX_ROWS):
            b = c * FLUX_ROWS + i
            pair = rows[pl.ds(pl.multiple_of(b * 8, 8), 8), :].astype(BF16)
            part = jnp.dot(pair, side_by_side(held, b), preferred_element_type=F32)
            part = part[0:1, :] + part[1:2, :]
            for k in range(K):
                packed[pl.ds(pos_ref[K + k, b], 1), :] = part[:, k * COLS : (k + 1) * COLS]

    out_ref[...] = packed[...].astype(BF16).reshape(RANKS, ATMOS_SLOTS, COLS)


def atmos_flux(pos, labels, air, prior, factors, weights, share):
    return pl.pallas_call(
        atmos_flux_body,
        out_shape=jax.ShapeDtypeStruct((RANKS, ATMOS_SLOTS, COLS), BF16),
        in_specs=[SMEM, VMEM, VMEM, VMEM, VMEM, ANY, SMEM],
        out_specs=VMEM,
        scratch_shapes=WEIGHTS_HELD
        + [
            pltpu.VMEM((RANKS * ATMOS_SLOTS, COLS), F32),
            pltpu.VMEM((ROWS * 8, COLS), F32),
            pltpu.SemaphoreType.DMA((ROWS // FLUX_ROWS,)),
        ],
        compiler_params=pltpu.CompilerParams(vmem_limit_bytes=32 << 20),
    )(pos, labels, air, prior, factors, weights, share)


WIDE = 8
EXTENDED = ROWS + 2 * WIDE


def iotas(rows):
    return (
        lax.broadcasted_iota(jnp.int32, (rows, COLS), 0),
        lax.broadcasted_iota(jnp.int32, (rows, COLS), 1),
    )


def turned(field, lanes):
    lanes = lanes % COLS
    return field if lanes == 0 else pltpu.roll(field, lanes, 1)


def sides_body(u_ref, out_ref):
    _, lane = iotas(ROWS)
    packed = jnp.zeros((ROWS, COLS), F32)
    for l in range(LEV):
        packed = jnp.where(lane // (2 * WIDE) == l, turned(u_ref[l], WIDE + 2 * WIDE * l), packed)
    out_ref[...] = packed


def mate_ends(sides, level):
    return turned(sides, -(2 * WIDE * level + WIDE))


def column_left(field, ends, lane):
    return pltpu.roll(jnp.where(lane == COLS - 1, ends, field), 1, 1)


def column_right(field, ends, lane):
    return pltpu.roll(jnp.where(lane == 0, ends, field), COLS - 1, 1)


def second_along(field, axis, index):
    phase = index % 4
    total = None
    for shift in range(-3, 4):
        factor = jnp.zeros(index.shape, F32)
        for p in range(4):
            if 0 <= p + shift < 4:
                factor = jnp.where(phase == p, F32(SECOND[p, p + shift]), factor)
        moved = field if shift == 0 else pltpu.roll(field, (-shift) % field.shape[axis], axis)
        total = factor * moved if total is None else total + factor * moved
    return total


def diffused(field, above, below):
    groups = field.reshape(EXTENDED // 8, 8, COLS)
    along = second_along(groups, 1, lax.broadcasted_iota(jnp.int32, (1, 8, COLS), 1))
    along = along.reshape(EXTENDED, COLS)
    along += second_along(field, 1, lax.broadcasted_iota(jnp.int32, (1, COLS), 1))
    return field + ATMOS_DIFFUSION * along + MIXING * (above + below - 2.0 * field)


def assembled(field, axis, phase, ahead, behind):
    return jnp.where(
        phase == 3,
        0.5 * (field + ahead),
        jnp.where(phase == 0, 0.5 * (field + behind), field),
    )


def assembled_rows(field, row):
    ahead = pltpu.roll(field, EXTENDED - 1, 0)
    return assembled(field, 0, row % 4, ahead, pltpu.roll(field, 1, 0))


def substeps_body(u_ref, sides_ref, before_ref, after_ref, out_ref, main, moved):
    row, lane = iotas(EXTENDED)
    phase, part = lane % 4, lane % (2 * WIDE)
    for l in range(LEV):
        main[l, :WIDE] = before_ref[l]
        main[l, WIDE : WIDE + ROWS] = u_ref[l]
        main[l, WIDE + ROWS :] = after_ref[l]
    sides = jnp.concatenate([before_ref[LEV], sides_ref[...], after_ref[LEV]], axis=0)
    for substep in range(2):
        over = jnp.where(lane < COLS - 2 * WIDE, turned(sides, -2 * WIDE), sides)
        under = jnp.where(lane >= 2 * WIDE, turned(sides, 2 * WIDE), sides)
        sides = assembled_rows(diffused(sides, over, under), row)
        edges = jnp.zeros((EXTENDED, COLS), F32)
        for l in range(LEV):
            field = main[l]
            half = assembled_rows(
                diffused(field, main[min(l + 1, LEV - 1)], main[max(l - 1, 0)]), row
            )
            if substep == 0:
                first = turned(half, 2 * WIDE * l + WIDE - 1)
                last = turned(half, 2 * WIDE * l + WIDE + 1)
                own_level = lane // (2 * WIDE) == l
                edges = jnp.where(own_level, jnp.where(part < WIDE, first, last), edges)
            ends = mate_ends(sides, l)
            whole = assembled(
                half, 1, phase, column_right(half, ends, lane), column_left(half, ends, lane)
            )
            if substep == 0:
                moved[l] = whole
            else:
                out_ref[l] = whole[WIDE : WIDE + ROWS]
        if substep == 0:
            ahead = jnp.where(part == WIDE - 1, edges, turned(sides, -1))
            behind = jnp.where(part == WIDE, edges, turned(sides, 1))
            sides = assembled(sides, 1, phase, ahead, behind)
            for l in range(LEV):
                main[l] = moved[l]


ORDER = [(dr, dc) for dr in (-1, 0, 1) for dc in (-1, 0, 1) if dr or dc]


def neighbour_counts(table_ref, row, lane):
    own = (row + 1) * (COLS + 2) + lane + 1
    counts = []
    for dr, dc in ORDER:
        target = own + (dr * (COLS + 2) + dc)
        count = jnp.zeros((ROWS, COLS), F32)
        for e in range(table_ref.shape[0]):
            count += jnp.where(table_ref[e] == target, 1.0, 0.0)
        counts.append(count)
    return counts


def neighbour_spread(field, ends, before, after, ends_before, ends_after, counts, row, lane):
    total = jnp.zeros((ROWS, COLS), F32)
    lines = {
        0: (field, ends),
        -1: tuple(
            jnp.where(row == 0, edge, pltpu.roll(v, 1, 0))
            for v, edge in ((field, before), (ends, ends_before))
        ),
        1: tuple(
            jnp.where(row == ROWS - 1, edge, pltpu.roll(v, ROWS - 1, 0))
            for v, edge in ((field, after), (ends, ends_after))
        ),
    }
    for (dr, dc), count in zip(ORDER, counts):
        line, line_ends = lines[dr]
        if dc == -1:
            line = column_left(line, line_ends, lane)
        elif dc == 1:
            line = column_right(line, line_ends, lane)
        total += count * (line - field)
    return total


def top_base_body(o_ref, sides_ref, before_ref, after_ref, table_ref, out_ref):
    row, lane = iotas(ROWS)
    top = o_ref[0]
    spread = neighbour_spread(
        top,
        mate_ends(sides_ref[...], 0),
        before_ref[0, WIDE - 1 :, :],
        after_ref[0, :1, :],
        mate_ends(before_ref[LEV, WIDE - 1 :, :], 0),
        mate_ends(after_ref[LEV, :1, :], 0),
        neighbour_counts(table_ref, row, lane),
        row,
        lane,
    )
    out_ref[...] = top + OCEAN_DIFFUSION * spread + MIXING * (o_ref[1] - top)


def ocean_base_body(o_ref, sides_ref, before_ref, after_ref, table_ref, out_ref, counts_ref):
    row, lane = iotas(ROWS)
    for n, count in enumerate(neighbour_counts(table_ref, row, lane)):
        counts_ref[n] = count
    for l in range(LEV):
        field = o_ref[l]
        spread = neighbour_spread(
            field,
            mate_ends(sides_ref[...], l),
            before_ref[l, WIDE - 1 :, :],
            after_ref[l, :1, :],
            mate_ends(before_ref[LEV, WIDE - 1 :, :], l),
            mate_ends(after_ref[LEV, :1, :], l),
            [counts_ref[n] for n in range(len(ORDER))],
            row,
            lane,
        )
        below, above = o_ref[max(l - 1, 0)], o_ref[min(l + 1, LEV - 1)]
        out_ref[l] = field + OCEAN_DIFFUSION * spread + MIXING * (above + below - 2.0 * field)


def exchanged(levels, sides):
    size = lax.axis_size("gx")
    up = [(i, (i + 1) % size) for i in range(size)]
    down = [(j, i) for i, j in up]
    sides = lax.ppermute(sides, "gy", [(0, 1), (1, 0)])
    last = jnp.concatenate([levels[:, ROWS - WIDE :, :], sides[None, ROWS - WIDE :, :]], axis=0)
    first = jnp.concatenate([levels[:, :WIDE, :], sides[None, :WIDE, :]], axis=0)
    return sides, lax.ppermute(last, "gx", up), lax.ppermute(first, "gx", down)


def row_hits(labels):
    width = ATMOS_SLOTS
    shape = (RANKS, width, COLS)
    diagonal = lax.broadcasted_iota(jnp.int32, shape, 1) == lax.broadcasted_iota(jnp.int32, shape, 2)
    spread = jnp.where(diagonal, labels[:, None, :], 0.0)
    column = jnp.sum(spread, axis=2, keepdims=True).reshape(RANKS * width, 1)
    slot = lax.broadcasted_iota(jnp.int32, (RANKS, width, 1), 1).reshape(RANKS * width, 1)
    column = jnp.where(slot < CAP, column, -1.0).astype(jnp.int32)
    rows = lax.broadcasted_iota(jnp.int32, (RANKS * width, ROWS), 1)
    return jnp.where(column == rows, 1.0, 0.0).astype(BF16)


def top_body(arrived_ref, base_ref, out_ref):
    arrived = arrived_ref[...].astype(F32)
    hits = row_hits(arrived[:, CAP, :])
    values = arrived.reshape(RANKS * ATMOS_SLOTS, COLS).astype(BF16)
    pushed = lax.dot_general(hits, values, (((0,), (0,)), ((), ())), preferred_element_type=F32)
    top = (base_ref[...] + pushed).astype(BF16)
    picked = jnp.dot(hits, top, preferred_element_type=F32)
    out_ref[...] = picked.astype(BF16).reshape(RANKS, ATMOS_SLOTS, COLS)


def sums_body(arrived_ref, base_ref, share_ref, out_ref, first_ref, wide):
    width = OCEAN_SLOTS * NF
    wide[...] = arrived_ref[...].astype(F32).reshape(RANKS * width, COLS)
    labels = wide[pl.ds(CAP * NF, RANKS, stride=width), :]
    by_slot = jnp.concatenate([labels, labels], axis=0).T
    row = lax.broadcasted_iota(jnp.int32, (ROWS, COLS), 0).astype(F32)
    lane = lax.broadcasted_iota(jnp.int32, (1, COLS), 1)
    pieces = []
    for s in range(0, CAP, 2):
        pair = jnp.where(lane < RANKS, by_slot[s : s + 1, :], by_slot[s + 1 : s + 2, :])
        pieces.append(jnp.where(row == pair, 1.0, 0.0).astype(BF16))
    hits = jnp.concatenate(pieces, axis=1)
    for f in range(NF):
        values = jnp.concatenate(
            [wide[pl.ds(s * NF + f, RANKS, stride=width), :] for s in range(CAP)], axis=0
        ).astype(BF16)
        forcing = jnp.dot(hits, values, preferred_element_type=F32)
        if f == 0:
            first_ref[...] = forcing
        for l in range(LEV):
            before = base_ref[l] if f == 0 else out_ref[l]
            out_ref[l] = before + share_ref[l, f] * forcing


def ocean_sums(arrived, base, share):
    return pl.pallas_call(
        sums_body,
        out_shape=(
            jax.ShapeDtypeStruct((LEV, ROWS, COLS), F32),
            jax.ShapeDtypeStruct((ROWS, COLS), F32),
        ),
        in_specs=[VMEM, VMEM, SMEM],
        out_specs=(VMEM, VMEM),
        scratch_shapes=[pltpu.VMEM((RANKS * OCEAN_SLOTS * NF, COLS), F32)],
        compiler_params=pltpu.CompilerParams(vmem_limit_bytes=24 << 20),
    )(arrived, base, share)


def remap_body(pos_ref, arrived_ref, w_ref, out_ref, held, wide, near, sems):
    copy = weight_copies(w_ref, held, sems, REMAP_ROWS)
    for c in range(ROWS // REMAP_ROWS):
        copy(c).start()
    wide[...] = arrived_ref[...].astype(F32).reshape(RANKS * ATMOS_SLOTS, COLS)
    lane = lax.broadcasted_iota(jnp.int32, (COLS, REMAP_ROWS), 1)

    @pl.loop(0, ROWS // REMAP_ROWS)
    def _(c):
        for i in range(REMAP_ROWS):
            for k in range(K):
                value = wide[pl.ds(pos_ref[K + k, c * REMAP_ROWS + i], 1), :]
                near[i : i + 1, k * COLS : (k + 1) * COLS] = value
        values = near[...].astype(BF16)
        copy(c).wait()
        block = held.at[pl.ds(c * REMAP_ROWS, REMAP_ROWS)]
        tiles = jnp.concatenate(
            [block[:, k].reshape(REMAP_ROWS * COLS, COLS) for k in range(K)], axis=1
        )
        crossed = lax.dot_general(
            tiles, values, (((1,), (1,)), ((), ())), preferred_element_type=F32
        )
        own = jnp.zeros((COLS, REMAP_ROWS), F32)
        for i in range(REMAP_ROWS):
            own = jnp.where(lane == i, crossed[i * COLS : (i + 1) * COLS], own)
        out_ref[pl.ds(pl.multiple_of(c * REMAP_ROWS, REMAP_ROWS), REMAP_ROWS), :] = own.T


def remap(pos, arrived, weights):
    return pl.pallas_call(
        remap_body,
        out_shape=jax.ShapeDtypeStruct((ROWS, COLS), F32),
        in_specs=[SMEM, VMEM, ANY],
        out_specs=VMEM,
        scratch_shapes=WEIGHTS_HELD
        + [
            pltpu.VMEM((RANKS * ATMOS_SLOTS, COLS), F32),
            pltpu.VMEM((REMAP_ROWS, K * COLS), F32),
            pltpu.SemaphoreType.DMA((ROWS // REMAP_ROWS,)),
        ],
        compiler_params=pltpu.CompilerParams(vmem_limit_bytes=32 << 20),
    )(pos, arrived, weights)


def to_peers(payload):
    return lax.all_to_all(payload, ("gx", "gy"), split_axis=0, concat_axis=0, tiled=True)


def local(
    layered_heat_profile,
    prior_marine_heat,
    transfer_factor_table,
    depth_fraction_matrix,
    adjacent_cell_table,
    destination_water_peer,
    destination_water_line,
    interpolation_matrix_blocks,
):
    is_atmosphere_side = lax.axis_index("comp") == 0
    own = layered_heat_profile[0]
    block = jax.ShapeDtypeStruct((LEV, ROWS, COLS), F32)
    plane = jax.ShapeDtypeStruct((ROWS, COLS), F32)
    swap = [(0, 1), (1, 0)]

    own_first = lax.optimization_barrier(own[0])
    other_first = lax.ppermute(own_first, "comp", swap)
    halo = exchanged(own, shadow_call(sides_body, plane, [VMEM])(own))
    pos, labels = positions(destination_water_peer, destination_water_line)

    packed = lax.cond(
        is_atmosphere_side,
        lambda: atmos_flux(
            pos,
            labels,
            own_first,
            prior_marine_heat,
            transfer_factor_table,
            interpolation_matrix_blocks,
            depth_fraction_matrix,
        ),
        lambda: jnp.zeros((RANKS, ATMOS_SLOTS, COLS), BF16),
    )
    top_base = lax.cond(
        is_atmosphere_side,
        lambda: own_first,
        lambda: shadow_call(top_base_body, plane, [VMEM] * 5)(own, *halo, adjacent_cell_table),
    )
    other_base = lax.ppermute(top_base, "comp", swap)

    def atmosphere():
        arrived = to_peers(packed)
        wide = pltpu.VMEM((LEV, EXTENDED, COLS), F32)
        final = shadow_call(substeps_body, block, [VMEM] * 4, scratch_shapes=[wide, wide])(
            own, *halo
        )
        return final, jnp.zeros((ROWS, COLS), F32), arrived

    def ocean():
        payload = ocean_flux(
            pos,
            labels,
            other_first,
            prior_marine_heat,
            transfer_factor_table,
            interpolation_matrix_blocks,
        )
        arrived = to_peers(payload.reshape(RANKS, OCEAN_SLOTS * NF, COLS))
        base = shadow_call(
            ocean_base_body,
            block,
            [VMEM] * 5,
            scratch_shapes=[pltpu.VMEM((len(ORDER), ROWS, COLS), F32)],
        )(own, *halo, adjacent_cell_table)
        state, first = ocean_sums(
            arrived.reshape(RANKS * OCEAN_SLOTS, NF, COLS), base, depth_fraction_matrix
        )
        return state, first, jnp.zeros((RANKS, ATMOS_SLOTS, COLS), BF16)

    state, first, arrived = lax.cond(is_atmosphere_side, atmosphere, ocean)

    def sea_temperature():
        picked = call(
            top_body, jax.ShapeDtypeStruct((RANKS, ATMOS_SLOTS, COLS), BF16), [VMEM, VMEM]
        )(arrived, other_base)
        return remap(pos, to_peers(picked), interpolation_matrix_blocks)

    plane_out = lax.cond(is_atmosphere_side, sea_temperature, lambda: first)
    return state[None], plane_out[None]


def solution(mesh):
    return jax.shard_map(
        local,
        mesh=mesh,
        in_specs=(
            P("comp", None, "gx", "gy"),
            P("gx", "gy"),
            P(None, "gx", "gy"),
            P(),
            P(None, "gx", "gy"),
            P(("gx", "gy"), None),
            P(("gx", "gy"), None),
            P(("gx", "gy"), None, None, None),
        ),
        out_specs=(P("comp", None, "gx", "gy"), P("comp", "gx", "gy")),
        check_vma=False,
    )
```

```python
import functools

import jax
import jax.numpy as jnp
import numpy as np
from jax import lax
from jax.experimental import pallas as pl
from jax.experimental.pallas import tpu as pltpu
from jax.sharding import PartitionSpec as P

ATMOS_DIFFUSION = 0.01
MIXING = 0.2
OCEAN_DIFFUSION = 0.12

RANKS = 64
CAP = 18
LEV = 8
NF = 8
ROWS = 256
COLS = 128
K = 2
WIDE = 8
OCEAN_SLOTS = 19
ATMOS_SLOTS = 24

VMEM = pl.BlockSpec(memory_space=pltpu.VMEM)
SMEM = pl.BlockSpec(memory_space=pltpu.SMEM)
ANY = pl.BlockSpec(memory_space=pl.ANY)
F32 = jnp.float32
BF16 = jnp.bfloat16


def second_table():
    gll_nodes = np.array([-1.0, -1.0 / np.sqrt(5.0), 1.0 / np.sqrt(5.0), 1.0])
    poly_order = 3
    legendre = (5.0 * gll_nodes**3 - 3.0 * gll_nodes) / 2.0
    derivative = np.zeros((4, 4))
    for row_index in range(4):
        for col_index in range(4):
            if row_index != col_index:
                derivative[row_index, col_index] = legendre[row_index] / (
                    legendre[col_index] * (gll_nodes[row_index] - gll_nodes[col_index])
                )
    derivative[0, 0] = -poly_order * (poly_order + 1) / 4.0
    derivative[3, 3] = poly_order * (poly_order + 1) / 4.0
    return derivative @ derivative


SECOND = second_table()


def call(body, out_shape, specs, **params):
    return pl.pallas_call(
        body,
        out_shape=out_shape,
        in_specs=specs,
        out_specs=jax.tree.map(lambda _: VMEM, out_shape),
        compiler_params=pltpu.CompilerParams(vmem_limit_bytes=params.pop("vmem", 24 << 20)),
        **params,
    )


def shadow_call(body, out_shape, specs, **params):
    nothing = pl.CostEstimate(flops=0, bytes_accessed=0, transcendentals=0)
    return call(body, out_shape, specs, cost_estimate=nothing, **params)


def route(peer_ref, line_ref, pos_ref, label_ref):
    count = ROWS * K
    peer = jnp.concatenate([peer_ref[k : k + 1, :] for k in range(K)], axis=1)
    line = jnp.concatenate([line_ref[k : k + 1, :] for k in range(K)], axis=1)
    hits = lax.broadcasted_iota(jnp.int32, (RANKS, count), 0) == peer
    hits_f = jnp.where(hits, 1.0, 0.0)
    earlier = lax.broadcasted_iota(jnp.int32, (count, count), 0) < lax.broadcasted_iota(
        jnp.int32, (count, count), 1
    )
    before = jnp.dot(
        hits_f.astype(BF16),
        jnp.where(earlier, 1.0, 0.0).astype(BF16),
        preferred_element_type=F32,
    )
    slot = jnp.sum(hits_f * before, axis=0, keepdims=True).astype(jnp.int32)
    for width, at in ((OCEAN_SLOTS, 0), (ATMOS_SLOTS, K)):
        position = peer * width + slot
        for k in range(K):
            pos_ref[at + k : at + k + 1, :] = position[:, k * ROWS : (k + 1) * ROWS]
    slot_hits = lax.broadcasted_iota(jnp.int32, (COLS, count), 0) == slot
    shifted = jnp.where(hits, (line + 1).astype(F32), 0.0).astype(BF16)
    label_ref[...] = (
        lax.dot_general(
            shifted,
            jnp.where(slot_hits, 1.0, 0.0).astype(BF16),
            (((1,), (1,)), ((), ())),
            preferred_element_type=F32,
        )
        - 1.0
    )


def turned(field, lanes):
    lanes = lanes % COLS
    return field if lanes == 0 else pltpu.roll(field, lanes, 1)


def first_body(side_ref, own_ref, peer_ref, line_ref, cross_ref, sides_ref, pos_ref, label_ref):
    top = own_ref[0]
    high = top.astype(BF16)
    rest = top - high.astype(F32)
    cross_ref[0] = high
    other = MIXING * own_ref[1] + (1.0 - MIXING) * rest
    cross_ref[1] = jnp.where(side_ref[0] == 0, rest, other).astype(BF16)
    lane = lax.broadcasted_iota(jnp.int32, (ROWS, COLS), 1)
    packed = jnp.zeros((ROWS, COLS), F32)
    for l in range(LEV):
        packed = jnp.where(lane // (2 * WIDE) == l, turned(own_ref[l], WIDE + 2 * WIDE * l), packed)
    sides_ref[...] = packed
    route(peer_ref, line_ref, pos_ref, label_ref)


def first_kernel(side, own, peer, line):
    return call(
        first_body,
        (
            jax.ShapeDtypeStruct((2, ROWS, COLS), BF16),
            jax.ShapeDtypeStruct((ROWS, COLS), F32),
            jax.ShapeDtypeStruct((2 * K, ROWS), jnp.int32),
            jax.ShapeDtypeStruct((RANKS, COLS), F32),
        ),
        [SMEM, VMEM, VMEM, VMEM],
    )(side, own, peer.T, line.T)


FLUX_ROWS = 16
REMAP_ROWS = 32


def weight_copies(source, held, sems, per):
    def copy(c):
        part = pl.ds(c * per, per)
        return pltpu.make_async_copy(source.at[part], held.at[part], sems.at[c])

    return copy


def side_by_side(held, b):
    return jnp.concatenate([held[b, k] for k in range(K)], axis=1)


def ocean_flux_body(
    pos_ref, label_ref, air_ref, prior_ref, factor_ref, w_ref, out_ref, held, packed, rows, sems
):
    copy = weight_copies(w_ref, held, sems, FLUX_ROWS)
    for c in range(ROWS // FLUX_ROWS):
        copy(c).start()
    packed[...] = jnp.zeros_like(packed)
    for d in range(RANKS):
        packed[d * OCEAN_SLOTS + CAP] = jnp.broadcast_to(
            label_ref[d : d + 1, :], (NF, COLS)
        ).astype(BF16)
    difference = air_ref[0].astype(F32) + air_ref[1].astype(F32) - prior_ref[...]
    for f in range(NF):
        rows[pl.ds(f, ROWS, stride=NF), :] = factor_ref[f] * difference

    @pl.loop(0, ROWS // FLUX_ROWS)
    def _(c):
        copy(c).wait()
        for i in range(FLUX_ROWS):
            b = c * FLUX_ROWS + i
            flux = rows[pl.ds(pl.multiple_of(b * NF, NF), NF), :].astype(BF16)
            part = jnp.dot(flux, side_by_side(held, b), preferred_element_type=F32).astype(BF16)
            for k in range(K):
                packed[pos_ref[k, b]] = part[:, k * COLS : (k + 1) * COLS]

    done = pltpu.make_async_copy(packed, out_ref, sems.at[ROWS // FLUX_ROWS])
    done.start()
    done.wait()


WEIGHTS_HELD = [
    pltpu.VMEM((ROWS, K, COLS, COLS), BF16),
]


def ocean_flux(pos, labels, air, prior, factors, weights):
    return pl.pallas_call(
        ocean_flux_body,
        out_shape=pltpu.HBM((RANKS * OCEAN_SLOTS, NF, COLS), BF16),
        in_specs=[SMEM, VMEM, VMEM, VMEM, VMEM, ANY],
        out_specs=pl.BlockSpec(memory_space=pltpu.HBM),
        scratch_shapes=WEIGHTS_HELD
        + [
            pltpu.VMEM((RANKS * OCEAN_SLOTS, NF, COLS), BF16),
            pltpu.VMEM((ROWS * NF, COLS), F32),
            pltpu.SemaphoreType.DMA((ROWS // FLUX_ROWS + 1,)),
        ],
        compiler_params=pltpu.CompilerParams(vmem_limit_bytes=32 << 20),
    )(pos, labels, air, prior, factors, weights)


def atmos_flux_body(
    pos_ref,
    label_ref,
    own_ref,
    prior_ref,
    factor_ref,
    w_ref,
    share_ref,
    out_ref,
    held,
    air,
    packed,
    rows,
    sems,
):
    air_copy = pltpu.make_async_copy(own_ref.at[0], air, sems.at[ROWS // FLUX_ROWS])
    air_copy.start()
    copy = weight_copies(w_ref, held, sems, FLUX_ROWS)
    for c in range(ROWS // FLUX_ROWS):
        copy(c).start()
    packed[...] = jnp.zeros_like(packed)
    for d in range(RANKS):
        packed[d * ATMOS_SLOTS + CAP : d * ATMOS_SLOTS + CAP + 1, :] = label_ref[d : d + 1, :]
    mixed = share_ref[0, 0] * factor_ref[0]
    for f in range(1, NF):
        mixed += share_ref[0, f] * factor_ref[f]
    air_copy.wait()
    flux = mixed * (air[...] - prior_ref[...])
    high = flux.astype(BF16).astype(F32)
    rows[...] = jnp.zeros_like(rows)
    rows[pl.ds(0, ROWS, stride=8), :] = high
    rows[pl.ds(1, ROWS, stride=8), :] = flux - high

    @pl.loop(0, ROWS // FLUX_ROWS)
    def _(c):
        copy(c).wait()
        for i in range(FLUX_ROWS):
            b = c * FLUX_ROWS + i
            pair = rows[pl.ds(pl.multiple_of(b * 8, 8), 8), :].astype(BF16)
            part = jnp.dot(pair, side_by_side(held, b), preferred_element_type=F32)
            part = part[0:1, :] + part[1:2, :]
            for k in range(K):
                packed[pl.ds(pos_ref[K + k, b], 1), :] = part[:, k * COLS : (k + 1) * COLS]

    out_ref[...] = packed[...].astype(BF16).reshape(RANKS, ATMOS_SLOTS, COLS)


def atmos_flux(pos, labels, own, prior, factors, weights, share):
    return pl.pallas_call(
        atmos_flux_body,
        out_shape=jax.ShapeDtypeStruct((RANKS, ATMOS_SLOTS, COLS), BF16),
        in_specs=[SMEM, VMEM, ANY, VMEM, VMEM, ANY, SMEM],
        out_specs=VMEM,
        scratch_shapes=WEIGHTS_HELD
        + [
            pltpu.VMEM((ROWS, COLS), F32),
            pltpu.VMEM((RANKS * ATMOS_SLOTS, COLS), F32),
            pltpu.VMEM((ROWS * 8, COLS), F32),
            pltpu.SemaphoreType.DMA((ROWS // FLUX_ROWS + 1,)),
        ],
        compiler_params=pltpu.CompilerParams(vmem_limit_bytes=32 << 20),
    )(pos, labels, own, prior, factors, weights, share)


EXTENDED = ROWS + 2 * WIDE


def iotas(rows):
    return (
        lax.broadcasted_iota(jnp.int32, (rows, COLS), 0),
        lax.broadcasted_iota(jnp.int32, (rows, COLS), 1),
    )


def mate_ends(sides, level):
    return turned(sides, -(2 * WIDE * level + WIDE))


def column_left(field, ends, lane):
    return pltpu.roll(jnp.where(lane == COLS - 1, ends, field), 1, 1)


def column_right(field, ends, lane):
    return pltpu.roll(jnp.where(lane == 0, ends, field), COLS - 1, 1)


def second_along(field, axis, index):
    phase = index % 4
    total = None
    for shift in range(-3, 4):
        factor = jnp.zeros(index.shape, F32)
        for p in range(4):
            if 0 <= p + shift < 4:
                factor = jnp.where(phase == p, F32(SECOND[p, p + shift]), factor)
        moved = field if shift == 0 else pltpu.roll(field, (-shift) % field.shape[axis], axis)
        total = factor * moved if total is None else total + factor * moved
    return total


def diffused(field, above, below):
    groups = field.reshape(EXTENDED // 8, 8, COLS)
    along = second_along(groups, 1, lax.broadcasted_iota(jnp.int32, (1, 8, COLS), 1))
    along = along.reshape(EXTENDED, COLS)
    along += second_along(field, 1, lax.broadcasted_iota(jnp.int32, (1, COLS), 1))
    return field + ATMOS_DIFFUSION * along + MIXING * (above + below - 2.0 * field)


def assembled(field, axis, phase, ahead, behind):
    return jnp.where(
        phase == 3,
        0.5 * (field + ahead),
        jnp.where(phase == 0, 0.5 * (field + behind), field),
    )


def assembled_rows(field, row):
    ahead = pltpu.roll(field, EXTENDED - 1, 0)
    return assembled(field, 0, row % 4, ahead, pltpu.roll(field, 1, 0))


def substeps_body(u_ref, sides_ref, before_ref, after_ref, _, out_ref, main, moved):
    row, lane = iotas(EXTENDED)
    phase, part = lane % 4, lane % (2 * WIDE)
    for l in range(LEV):
        main[l, :WIDE] = before_ref[l]
        main[l, WIDE : WIDE + ROWS] = u_ref[l]
        main[l, WIDE + ROWS :] = after_ref[l]
    sides = jnp.concatenate([before_ref[LEV], sides_ref[...], after_ref[LEV]], axis=0)
    for substep in range(2):
        over = jnp.where(lane < COLS - 2 * WIDE, turned(sides, -2 * WIDE), sides)
        under = jnp.where(lane >= 2 * WIDE, turned(sides, 2 * WIDE), sides)
        sides = assembled_rows(diffused(sides, over, under), row)
        edges = jnp.zeros((EXTENDED, COLS), F32)
        for l in range(LEV):
            field = main[l]
            half = assembled_rows(
                diffused(field, main[min(l + 1, LEV - 1)], main[max(l - 1, 0)]), row
            )
            if substep == 0:
                first = turned(half, 2 * WIDE * l + WIDE - 1)
                last = turned(half, 2 * WIDE * l + WIDE + 1)
                own_level = lane // (2 * WIDE) == l
                edges = jnp.where(own_level, jnp.where(part < WIDE, first, last), edges)
            ends = mate_ends(sides, l)
            whole = assembled(
                half, 1, phase, column_right(half, ends, lane), column_left(half, ends, lane)
            )
            if substep == 0:
                moved[l] = whole
            else:
                out_ref[l] = whole[WIDE : WIDE + ROWS]
        if substep == 0:
            ahead = jnp.where(part == WIDE - 1, edges, turned(sides, -1))
            behind = jnp.where(part == WIDE, edges, turned(sides, 1))
            sides = assembled(sides, 1, phase, ahead, behind)
            for l in range(LEV):
                main[l] = moved[l]


ORDER = [(dr, dc) for dr in (-1, 0, 1) for dc in (-1, 0, 1) if dr or dc]


def neighbour_counts(table_ref, row, lane):
    own = (row + 1) * (COLS + 2) + lane + 1
    counts = []
    for dr, dc in ORDER:
        target = own + (dr * (COLS + 2) + dc)
        count = jnp.zeros((ROWS, COLS), F32)
        for e in range(table_ref.shape[0]):
            count += jnp.where(table_ref[e] == target, 1.0, 0.0)
        counts.append(count)
    return counts


def neighbour_spread(field, ends, before, after, ends_before, ends_after, counts, row, lane):
    total = jnp.zeros((ROWS, COLS), F32)
    lines = {
        0: (field, ends),
        -1: tuple(
            jnp.where(row == 0, edge, pltpu.roll(v, 1, 0))
            for v, edge in ((field, before), (ends, ends_before))
        ),
        1: tuple(
            jnp.where(row == ROWS - 1, edge, pltpu.roll(v, ROWS - 1, 0))
            for v, edge in ((field, after), (ends, ends_after))
        ),
    }
    for (dr, dc), count in zip(ORDER, counts):
        line, line_ends = lines[dr]
        if dc == -1:
            line = column_left(line, line_ends, lane)
        elif dc == 1:
            line = column_right(line, line_ends, lane)
        total += count * (line - field)
    return total


def top_base_body(other_ref, mate_ref, before_ref, after_ref, table_ref, out_ref):
    row, lane = iotas(ROWS)
    top = other_ref[0].astype(F32)
    spread = neighbour_spread(
        top,
        mate_ref[0].astype(F32),
        before_ref[LEV + 1, WIDE - 1 :, :],
        after_ref[LEV + 1, :1, :],
        before_ref[LEV + 2, WIDE - 1 :, :],
        after_ref[LEV + 2, :1, :],
        neighbour_counts(table_ref, row, lane),
        row,
        lane,
    )
    out_ref[...] = (1.0 - MIXING) * top + other_ref[1].astype(F32) + OCEAN_DIFFUSION * spread


def ocean_base_body(o_ref, sides_ref, before_ref, after_ref, table_ref, out_ref, counts_ref):
    row, lane = iotas(ROWS)
    for n, count in enumerate(neighbour_counts(table_ref, row, lane)):
        counts_ref[n] = count
    for l in range(LEV):
        field = o_ref[l]
        spread = neighbour_spread(
            field,
            mate_ends(sides_ref[...], l),
            before_ref[l, WIDE - 1 :, :],
            after_ref[l, :1, :],
            mate_ends(before_ref[LEV, WIDE - 1 :, :], l),
            mate_ends(after_ref[LEV, :1, :], l),
            [counts_ref[n] for n in range(len(ORDER))],
            row,
            lane,
        )
        below, above = o_ref[max(l - 1, 0)], o_ref[min(l + 1, LEV - 1)]
        out_ref[l] = field + OCEAN_DIFFUSION * spread + MIXING * (above + below - 2.0 * field)


def edge_rows(*fields):
    last = [v[..., ROWS - WIDE :, :].reshape(-1, WIDE, COLS).astype(F32) for v in fields]
    first = [v[..., :WIDE, :].reshape(-1, WIDE, COLS).astype(F32) for v in fields]
    return jnp.concatenate(last, axis=0), jnp.concatenate(first, axis=0)


def from_neighbours(last, first):
    size = lax.axis_size("gx")
    up = [(i, (i + 1) % size) for i in range(size)]
    down = [(j, i) for i, j in up]
    return lax.ppermute(last, "gx", up), lax.ppermute(first, "gx", down)


def from_mate(field):
    return lax.ppermute(field, "gy", [(0, 1), (1, 0)])


def row_hits(labels):
    width = ATMOS_SLOTS
    shape = (RANKS, width, COLS)
    diagonal = lax.broadcasted_iota(jnp.int32, shape, 1) == lax.broadcasted_iota(jnp.int32, shape, 2)
    spread = jnp.where(diagonal, labels[:, None, :], 0.0)
    column = jnp.sum(spread, axis=2, keepdims=True).reshape(RANKS * width, 1)
    slot = lax.broadcasted_iota(jnp.int32, (RANKS, width, 1), 1).reshape(RANKS * width, 1)
    column = jnp.where(slot < CAP, column, -1.0).astype(jnp.int32)
    rows = lax.broadcasted_iota(jnp.int32, (RANKS * width, ROWS), 1)
    return jnp.where(column == rows, 1.0, 0.0).astype(BF16)


def top_body(arrived_ref, base_ref, out_ref):
    arrived = arrived_ref[...].astype(F32)
    hits = row_hits(arrived[:, CAP, :])
    values = arrived.reshape(RANKS * ATMOS_SLOTS, COLS).astype(BF16)
    pushed = lax.dot_general(hits, values, (((0,), (0,)), ((), ())), preferred_element_type=F32)
    top = (base_ref[...] + pushed).astype(BF16)
    picked = jnp.dot(hits, top, preferred_element_type=F32)
    out_ref[...] = picked.astype(BF16).reshape(RANKS, ATMOS_SLOTS, COLS)


def sums_body(arrived_ref, base_ref, share_ref, out_ref, first_ref, wide):
    width = OCEAN_SLOTS * NF
    wide[...] = arrived_ref[...].astype(F32).reshape(RANKS * width, COLS)
    labels = wide[pl.ds(CAP * NF, RANKS, stride=width), :]
    by_slot = jnp.concatenate([labels, labels], axis=0).T
    row = lax.broadcasted_iota(jnp.int32, (ROWS, COLS), 0).astype(F32)
    lane = lax.broadcasted_iota(jnp.int32, (1, COLS), 1)
    pieces = []
    for s in range(0, CAP, 2):
        pair = jnp.where(lane < RANKS, by_slot[s : s + 1, :], by_slot[s + 1 : s + 2, :])
        pieces.append(jnp.where(row == pair, 1.0, 0.0).astype(BF16))
    hits = jnp.concatenate(pieces, axis=1)
    forcing = []
    for f in range(0, NF, 2):
        values = [
            jnp.concatenate(
                [wide[pl.ds(s * NF + g, RANKS, stride=width), :] for s in range(CAP)], axis=0
            )
            for g in (f, f + 1)
        ]
        both = jnp.concatenate(values, axis=1).astype(BF16)
        summed = jnp.dot(hits, both, preferred_element_type=F32)
        forcing += [summed[:, :COLS], summed[:, COLS:]]
    first_ref[...] = forcing[0]
    for l in range(LEV):
        level = base_ref[l]
        for f in range(NF):
            level += share_ref[l, f] * forcing[f]
        out_ref[l] = level


def ocean_sums(arrived, base, share):
    return pl.pallas_call(
        sums_body,
        out_shape=(
            jax.ShapeDtypeStruct((LEV, ROWS, COLS), F32),
            jax.ShapeDtypeStruct((ROWS, COLS), F32),
        ),
        in_specs=[VMEM, VMEM, SMEM],
        out_specs=(VMEM, VMEM),
        scratch_shapes=[pltpu.VMEM((RANKS * OCEAN_SLOTS * NF, COLS), F32)],
        compiler_params=pltpu.CompilerParams(vmem_limit_bytes=24 << 20),
    )(arrived, base, share)


def remap_body(pos_ref, arrived_ref, w_ref, out_ref, held, values, own, sems):
    copy = weight_copies(w_ref, held, sems, REMAP_ROWS)
    for c in range(ROWS // REMAP_ROWS):
        copy(c).start()
    slots = RANKS * ATMOS_SLOTS
    by_column = arrived_ref[...].astype(F32).reshape(slots, COLS).T.astype(BF16)
    at = lax.broadcasted_iota(jnp.int32, (slots, ROWS), 0)
    groups = ROWS // COLS
    for k in range(K):
        hits = jnp.where(at == pos_ref[K + k : K + k + 1, :], 1.0, 0.0).astype(BF16)
        found = jnp.dot(by_column, hits, preferred_element_type=F32).astype(BF16)
        for g in range(groups):
            values[g, k * COLS : (k + 1) * COLS, :] = found[:, g * COLS : (g + 1) * COLS]
    lane = lax.broadcasted_iota(jnp.int32, (COLS, COLS), 1)
    parts = COLS // REMAP_ROWS

    @pl.loop(0, ROWS // REMAP_ROWS)
    def _(c):
        copy(c).wait()
        block = held.at[pl.ds(c * REMAP_ROWS, REMAP_ROWS)]
        tiles = jnp.concatenate(
            [block[:, k].reshape(REMAP_ROWS * COLS, COLS) for k in range(K)], axis=1
        )
        crossed = jnp.dot(tiles, values[c // parts], preferred_element_type=F32)
        kept = own[c // parts]
        for i in range(REMAP_ROWS):
            mine = lane == (c % parts) * REMAP_ROWS + i
            kept = jnp.where(mine, crossed[i * COLS : (i + 1) * COLS], kept)
        own[c // parts] = kept

    for g in range(groups):
        out_ref[g * COLS : (g + 1) * COLS, :] = own[g].T


def remap(pos, arrived, weights):
    return pl.pallas_call(
        remap_body,
        out_shape=jax.ShapeDtypeStruct((ROWS, COLS), F32),
        in_specs=[VMEM, VMEM, ANY],
        out_specs=VMEM,
        scratch_shapes=WEIGHTS_HELD
        + [
            pltpu.VMEM((ROWS // COLS, K * COLS, COLS), BF16),
            pltpu.VMEM((ROWS // COLS, COLS, COLS), F32),
            pltpu.SemaphoreType.DMA((ROWS // REMAP_ROWS,)),
        ],
        compiler_params=pltpu.CompilerParams(vmem_limit_bytes=32 << 20),
    )(pos, arrived, weights)


def to_peers(payload):
    return lax.all_to_all(payload, ("gx", "gy"), split_axis=0, concat_axis=0, tiled=True)


def local(
    layered_heat_profile,
    prior_marine_heat,
    transfer_factor_table,
    depth_fraction_matrix,
    adjacent_cell_table,
    destination_water_peer,
    destination_water_line,
    interpolation_matrix_blocks,
):
    is_atmosphere_side = lax.axis_index("comp") == 0
    own = layered_heat_profile[0]
    block = jax.ShapeDtypeStruct((LEV, ROWS, COLS), F32)
    plane = jax.ShapeDtypeStruct((ROWS, COLS), F32)
    swap = [(0, 1), (1, 0)]

    cross, sides, pos, labels = first_kernel(
        lax.axis_index("comp").reshape(1), own, destination_water_peer, destination_water_line
    )
    other = lax.ppermute(cross, "comp", [(0, 1), (1, 0)])
    sides = from_mate(sides)

    def atmosphere_early():
        packed = atmos_flux(
            pos,
            labels,
            own,
            prior_marine_heat,
            transfer_factor_table,
            interpolation_matrix_blocks,
            depth_fraction_matrix,
        )
        nothing = jnp.zeros((LEV + 1, WIDE, COLS), F32)
        return packed, nothing, nothing

    def ocean_early():
        halo = from_neighbours(*edge_rows(own, sides))
        return jnp.zeros((RANKS, ATMOS_SLOTS, COLS), BF16), *halo

    packed, *ocean_rows = lax.cond(is_atmosphere_side, atmosphere_early, ocean_early)

    def atmosphere():
        mate = from_mate(other)
        edges = edge_rows(own, sides, other[0], mate[0])
        payload, *edges = lax.optimization_barrier((packed, *edges))
        before, after = from_neighbours(*edges)
        arrived = to_peers(payload)
        base = shadow_call(top_base_body, plane, [VMEM] * 5)(
            other, mate, before, after, adjacent_cell_table
        )
        picked = call(
            top_body, jax.ShapeDtypeStruct((RANKS, ATMOS_SLOTS, COLS), BF16), [VMEM, VMEM]
        )(arrived, base)
        returned = to_peers(picked)
        wide = pltpu.VMEM((LEV, EXTENDED, COLS), F32)
        final = shadow_call(
            substeps_body, block, [VMEM] * 4 + [ANY], scratch_shapes=[wide, wide]
        )(own, sides, before, after, picked)
        return final, remap(pos, returned, interpolation_matrix_blocks)

    def ocean():
        payload = ocean_flux(
            pos,
            labels,
            other,
            prior_marine_heat,
            transfer_factor_table,
            interpolation_matrix_blocks,
        )
        arrived = to_peers(payload.reshape(RANKS, OCEAN_SLOTS * NF, COLS))
        base = shadow_call(
            ocean_base_body,
            block,
            [VMEM] * 5,
            scratch_shapes=[pltpu.VMEM((len(ORDER), ROWS, COLS), F32)],
        )(own, sides, *ocean_rows, adjacent_cell_table)
        return ocean_sums(
            arrived.reshape(RANKS * OCEAN_SLOTS, NF, COLS), base, depth_fraction_matrix
        )

    state, plane_out = lax.cond(is_atmosphere_side, atmosphere, ocean)
    return state[None], plane_out[None]


def solution(mesh):
    return jax.shard_map(
        local,
        mesh=mesh,
        in_specs=(
            P("comp", None, "gx", "gy"),
            P("gx", "gy"),
            P(None, "gx", "gy"),
            P(),
            P(None, "gx", "gy"),
            P(("gx", "gy"), None),
            P(("gx", "gy"), None),
            P(("gx", "gy"), None, None, None),
        ),
        out_specs=(P("comp", None, "gx", "gy"), P("comp", "gx", "gy")),
        check_vma=False,
    )
```

```python
import functools

import jax
import jax.numpy as jnp
import numpy as np
from jax import lax
from jax.experimental import pallas as pl
from jax.experimental.pallas import tpu as pltpu
from jax.sharding import PartitionSpec as P

ATMOS_DIFFUSION = 0.01
MIXING = 0.2
OCEAN_DIFFUSION = 0.12

RANKS = 64
CAP = 18
CORES = 2
LEV = 8
NF = 8
ROWS = 256
COLS = 128
K = 2
WIDE = 8
OCEAN_SLOTS = 19
ATMOS_SLOTS = 24

VMEM = pl.BlockSpec(memory_space=pltpu.VMEM)
SMEM = pl.BlockSpec(memory_space=pltpu.SMEM)
ANY = pl.BlockSpec(memory_space=pl.ANY)
HBM = pl.BlockSpec(memory_space=pltpu.HBM)
F32 = jnp.float32
BF16 = jnp.bfloat16


def second_table():
    gll_nodes = np.array([-1.0, -1.0 / np.sqrt(5.0), 1.0 / np.sqrt(5.0), 1.0])
    poly_order = 3
    legendre = (5.0 * gll_nodes**3 - 3.0 * gll_nodes) / 2.0
    derivative = np.zeros((4, 4))
    for row_index in range(4):
        for col_index in range(4):
            if row_index != col_index:
                derivative[row_index, col_index] = legendre[row_index] / (
                    legendre[col_index] * (gll_nodes[row_index] - gll_nodes[col_index])
                )
    derivative[0, 0] = -poly_order * (poly_order + 1) / 4.0
    derivative[3, 3] = poly_order * (poly_order + 1) / 4.0
    return derivative @ derivative


SECOND = second_table()


def call(body, out_shape, specs, **params):
    return pl.pallas_call(
        body,
        out_shape=out_shape,
        in_specs=specs,
        out_specs=jax.tree.map(lambda _: VMEM, out_shape),
        compiler_params=pltpu.CompilerParams(vmem_limit_bytes=params.pop("vmem", 24 << 20)),
        **params,
    )


def shadow_call(body, out_shape, specs, us=0, **params):
    cost = pl.CostEstimate(flops=0, bytes_accessed=us * 3_690_000, transcendentals=0)
    return call(body, out_shape, specs, cost_estimate=cost, **params)


def unused(shape, dtype):
    return pl.pallas_call(lambda out_ref: None, out_shape=pltpu.HBM(shape, dtype), out_specs=HBM)()


def route(peer_ref, line_ref, pos_ref, label_ref):
    count = ROWS * K
    peer = jnp.concatenate([peer_ref[k : k + 1, :] for k in range(K)], axis=1)
    line = jnp.concatenate([line_ref[k : k + 1, :] for k in range(K)], axis=1)
    hits = lax.broadcasted_iota(jnp.int32, (RANKS, count), 0) == peer
    hits_f = jnp.where(hits, 1.0, 0.0)
    earlier = lax.broadcasted_iota(jnp.int32, (count, count), 0) < lax.broadcasted_iota(
        jnp.int32, (count, count), 1
    )
    before = jnp.dot(
        hits_f.astype(BF16),
        jnp.where(earlier, 1.0, 0.0).astype(BF16),
        preferred_element_type=F32,
    )
    slot = jnp.sum(hits_f * before, axis=0, keepdims=True).astype(jnp.int32)
    for width, at in ((OCEAN_SLOTS, 0), (ATMOS_SLOTS, K)):
        position = peer * width + slot
        for k in range(K):
            pos_ref[at + k : at + k + 1, :] = position[:, k * ROWS : (k + 1) * ROWS]
    slot_hits = lax.broadcasted_iota(jnp.int32, (COLS, count), 0) == slot
    shifted = jnp.where(hits, (line + 1).astype(F32), 0.0).astype(BF16)
    label_ref[...] = (
        lax.dot_general(
            shifted,
            jnp.where(slot_hits, 1.0, 0.0).astype(BF16),
            (((1,), (1,)), ((), ())),
            preferred_element_type=F32,
        )
        - 1.0
    )


def turned(field, lanes):
    lanes = lanes % COLS
    return field if lanes == 0 else pltpu.roll(field, lanes, 1)


def cross_body(side_ref, own_ref, out_ref, held, sem):
    copy = pltpu.make_async_copy(own_ref.at[pl.ds(0, 2)], held, sem)
    copy.start()
    copy.wait()
    top = held[0]
    high = top.astype(BF16)
    rest = top - high.astype(F32)
    out_ref[0] = high
    other = MIXING * held[1] + (1.0 - MIXING) * rest
    out_ref[1] = jnp.where(side_ref[0] == 0, rest, other).astype(BF16)


def cross_kernel(side, own):
    return call(
        cross_body,
        jax.ShapeDtypeStruct((2, ROWS, COLS), BF16),
        [SMEM, HBM],
        scratch_shapes=[pltpu.VMEM((2, ROWS, COLS), F32), pltpu.SemaphoreType.DMA],
    )(side, own)


def packed_sides(levels, lane):
    packed = jnp.zeros(lane.shape, F32)
    for l, level in enumerate(levels):
        packed = jnp.where(lane // (2 * WIDE) == l, turned(level, WIDE + 2 * WIDE * l), packed)
    return packed


def sides_body(own_ref, out_ref):
    lane = lax.broadcasted_iota(jnp.int32, (ROWS, COLS), 1)
    out_ref[...] = packed_sides([own_ref[l] for l in range(LEV)], lane)


FLUX_ROWS = 16
REMAP_ROWS = 32
CHUNKS = ROWS // FLUX_ROWS


def weight_copies(source, held, sems, per):
    def copy(c):
        part = pl.ds(c * per, per)
        return pltpu.make_async_copy(source.at[part], held.at[part], sems.at[c])

    return copy


def side_by_side(held, b):
    return jnp.concatenate([held[b, k] for k in range(K)], axis=1)


WEIGHTS_HELD = [
    pltpu.VMEM((ROWS, K, COLS, COLS), BF16),
]
ROUTING = [
    pltpu.VMEM((K, ROWS), jnp.int32),
    pltpu.VMEM((K, ROWS), jnp.int32),
    pltpu.VMEM((RANKS, COLS), F32),
    pltpu.SMEM((2 * K, ROWS), jnp.int32),
]
FIELDS = [
    pltpu.VMEM((ROWS, COLS), F32),
    pltpu.VMEM((NF, ROWS, COLS), F32),
]


def ocean_flux_body(
    peer_ref,
    line_ref,
    air_ref,
    prior_ref,
    factor_ref,
    w_ref,
    out_ref,
    held,
    peer,
    line,
    label,
    pos,
    prior,
    factor,
    pos_rows,
    packed,
    rows,
    sems,
):
    copy = weight_copies(w_ref, held, sems, FLUX_ROWS)
    index_copies = [
        pltpu.make_async_copy(peer_ref, peer, sems.at[CHUNKS]),
        pltpu.make_async_copy(line_ref, line, sems.at[CHUNKS + 1]),
    ]
    field_copies = [
        pltpu.make_async_copy(prior_ref, prior, sems.at[CHUNKS + 2]),
        pltpu.make_async_copy(factor_ref, factor, sems.at[CHUNKS + 3]),
    ]
    for started in index_copies + field_copies:
        started.start()
    for c in range(CHUNKS):
        copy(c).start()
    packed[...] = jnp.zeros_like(packed)
    for started in index_copies:
        started.wait()
    route(peer, line, pos_rows, label)
    to_scalars = pltpu.make_async_copy(pos_rows, pos, sems.at[CHUNKS + 4])
    to_scalars.start()
    for d in range(RANKS):
        packed[d * OCEAN_SLOTS + CAP] = jnp.broadcast_to(label[d : d + 1, :], (NF, COLS)).astype(
            BF16
        )
    for started in field_copies:
        started.wait()
    difference = air_ref[0].astype(F32) + air_ref[1].astype(F32) - prior[...]
    for f in range(NF):
        rows[pl.ds(f, ROWS, stride=NF), :] = factor[f] * difference
    to_scalars.wait()

    @pl.loop(0, CHUNKS)
    def _(c):
        copy(c).wait()
        for i in range(FLUX_ROWS):
            b = c * FLUX_ROWS + i
            flux = rows[pl.ds(pl.multiple_of(b * NF, NF), NF), :].astype(BF16)
            part = jnp.dot(flux, side_by_side(held, b), preferred_element_type=F32).astype(BF16)
            for k in range(K):
                packed[pos[k, b]] = part[:, k * COLS : (k + 1) * COLS]

    done = pltpu.make_async_copy(packed, out_ref, sems.at[CHUNKS + 5])
    done.start()
    done.wait()


def ocean_flux(peer, line, air, prior, factors, weights):
    return pl.pallas_call(
        ocean_flux_body,
        out_shape=pltpu.HBM((RANKS * OCEAN_SLOTS, NF, COLS), BF16),
        in_specs=[HBM, HBM, VMEM, HBM, HBM, HBM],
        out_specs=HBM,
        scratch_shapes=WEIGHTS_HELD
        + ROUTING
        + FIELDS
        + [
            pltpu.VMEM((2 * K, ROWS), jnp.int32),
            pltpu.VMEM((RANKS * OCEAN_SLOTS, NF, COLS), BF16),
            pltpu.VMEM((ROWS * NF, COLS), F32),
            pltpu.SemaphoreType.DMA((CHUNKS + 6,)),
        ],
        compiler_params=pltpu.CompilerParams(vmem_limit_bytes=32 << 20),
    )(peer.T, line.T, air, prior, factors, weights)


def atmos_flux_body(
    peer_ref,
    line_ref,
    own_ref,
    prior_ref,
    factor_ref,
    w_ref,
    share_ref,
    out_ref,
    pos_ref,
    held,
    peer,
    line,
    label,
    pos,
    prior,
    factor,
    air,
    packed,
    rows,
    sems,
):
    copy = weight_copies(w_ref, held, sems, FLUX_ROWS)
    index_copies = [
        pltpu.make_async_copy(peer_ref, peer, sems.at[CHUNKS]),
        pltpu.make_async_copy(line_ref, line, sems.at[CHUNKS + 1]),
    ]
    field_copies = [
        pltpu.make_async_copy(prior_ref, prior, sems.at[CHUNKS + 2]),
        pltpu.make_async_copy(own_ref.at[0], air, sems.at[CHUNKS + 3]),
        pltpu.make_async_copy(factor_ref, factor, sems.at[CHUNKS + 4]),
    ]
    for started in index_copies + field_copies:
        started.start()
    for c in range(CHUNKS):
        copy(c).start()
    packed[...] = jnp.zeros_like(packed)
    rows[...] = jnp.zeros_like(rows)
    for started in index_copies:
        started.wait()
    route(peer, line, pos_ref, label)
    to_scalars = pltpu.make_async_copy(pos_ref, pos, sems.at[CHUNKS + 5])
    to_scalars.start()
    for d in range(RANKS):
        packed[d * ATMOS_SLOTS + CAP : d * ATMOS_SLOTS + CAP + 1, :] = label[d : d + 1, :]
    for started in field_copies:
        started.wait()
    mixed = share_ref[0, 0] * factor[0]
    for f in range(1, NF):
        mixed += share_ref[0, f] * factor[f]
    flux = mixed * (air[...] - prior[...])
    high = flux.astype(BF16).astype(F32)
    rows[pl.ds(0, ROWS, stride=8), :] = high
    rows[pl.ds(1, ROWS, stride=8), :] = flux - high
    to_scalars.wait()

    @pl.loop(0, CHUNKS)
    def _(c):
        copy(c).wait()
        for i in range(FLUX_ROWS):
            b = c * FLUX_ROWS + i
            pair = rows[pl.ds(pl.multiple_of(b * 8, 8), 8), :].astype(BF16)
            part = jnp.dot(pair, side_by_side(held, b), preferred_element_type=F32)
            part = part[0:1, :] + part[1:2, :]
            for k in range(K):
                packed[pl.ds(pos[K + k, b], 1), :] = part[:, k * COLS : (k + 1) * COLS]

    out_ref[...] = packed[...].astype(BF16).reshape(RANKS, ATMOS_SLOTS, COLS)


def atmos_flux(peer, line, own, prior, factors, weights, share):
    return pl.pallas_call(
        atmos_flux_body,
        out_shape=(
            jax.ShapeDtypeStruct((RANKS, ATMOS_SLOTS, COLS), BF16),
            jax.ShapeDtypeStruct((2 * K, ROWS), jnp.int32),
        ),
        in_specs=[HBM, HBM, HBM, HBM, HBM, HBM, SMEM],
        out_specs=(VMEM, VMEM),
        scratch_shapes=WEIGHTS_HELD
        + ROUTING
        + FIELDS
        + [
            pltpu.VMEM((ROWS, COLS), F32),
            pltpu.VMEM((RANKS * ATMOS_SLOTS, COLS), F32),
            pltpu.VMEM((ROWS * 8, COLS), F32),
            pltpu.SemaphoreType.DMA((CHUNKS + 6,)),
        ],
        compiler_params=pltpu.CompilerParams(vmem_limit_bytes=32 << 20),
    )(peer.T, line.T, own, prior, factors, weights, share)


EXTENDED = ROWS + 2 * WIDE


def iotas(rows):
    return (
        lax.broadcasted_iota(jnp.int32, (rows, COLS), 0),
        lax.broadcasted_iota(jnp.int32, (rows, COLS), 1),
    )


def mate_ends(sides, level):
    return turned(sides, -(2 * WIDE * level + WIDE))


def column_left(field, ends, lane):
    return pltpu.roll(jnp.where(lane == COLS - 1, ends, field), 1, 1)


def column_right(field, ends, lane):
    return pltpu.roll(jnp.where(lane == 0, ends, field), COLS - 1, 1)


def second_along(field, axis, index):
    phase = index % 4
    total = None
    for shift in range(-3, 4):
        factor = jnp.zeros(index.shape, F32)
        for p in range(4):
            if 0 <= p + shift < 4:
                factor = jnp.where(phase == p, F32(SECOND[p, p + shift]), factor)
        moved = field if shift == 0 else pltpu.roll(field, (-shift) % field.shape[axis], axis)
        total = factor * moved if total is None else total + factor * moved
    return total


def diffused(field, above, below):
    groups = field.reshape(-1, 8, COLS)
    along = second_along(groups, 1, lax.broadcasted_iota(jnp.int32, (1, 8, COLS), 1))
    along = along.reshape(field.shape)
    along += second_along(field, 1, lax.broadcasted_iota(jnp.int32, (1, COLS), 1))
    return field + ATMOS_DIFFUSION * along + MIXING * (above + below - 2.0 * field)


def assembled(field, axis, phase, ahead, behind):
    return jnp.where(
        phase == 3,
        0.5 * (field + ahead),
        jnp.where(phase == 0, 0.5 * (field + behind), field),
    )


def assembled_rows(field, row):
    ahead = pltpu.roll(field, EXTENDED - 1, 0)
    return assembled(field, 0, row % 4, ahead, pltpu.roll(field, 1, 0))


def diffused_levels(levels):
    return [
        diffused(levels[l], levels[min(l + 1, LEV - 1)], levels[max(l - 1, 0)]) for l in range(LEV)
    ]


def local_body(u_ref, out_ref):
    for l, field in enumerate(diffused_levels([u_ref[l] for l in range(LEV)])):
        out_ref[l] = field


def substeps_body(
    local_ref, sides_ref, before_ref, after_ref, mate_before_ref, mate_after_ref, _, out_ref, main
):
    row, lane = iotas(EXTENDED)
    phase, part = lane % 4, lane % (2 * WIDE)
    edges = [diffused_levels([r[l] for l in range(LEV)]) for r in (before_ref, after_ref)]
    thin = lax.broadcasted_iota(jnp.int32, (WIDE, COLS), 1)
    ends = [
        packed_sides([r[l] for l in range(LEV)], thin) for r in (mate_before_ref, mate_after_ref)
    ]
    sides = jnp.concatenate([ends[0], sides_ref[...], ends[1]], axis=0)
    for substep in range(2):
        over = jnp.where(lane < COLS - 2 * WIDE, turned(sides, -2 * WIDE), sides)
        under = jnp.where(lane >= 2 * WIDE, turned(sides, 2 * WIDE), sides)
        sides = assembled_rows(diffused(sides, over, under), row)
        near = jnp.zeros((EXTENDED, COLS), F32)
        for l in range(LEV):
            if substep == 0:
                half = jnp.concatenate([edges[0][l], local_ref[l], edges[1][l]], axis=0)
            else:
                half = diffused(main[l], main[min(l + 1, LEV - 1)], main[max(l - 1, 0)])
            half = assembled_rows(half, row)
            if substep == 0:
                first = turned(half, 2 * WIDE * l + WIDE - 1)
                last = turned(half, 2 * WIDE * l + WIDE + 1)
                own_level = lane // (2 * WIDE) == l
                near = jnp.where(own_level, jnp.where(part < WIDE, first, last), near)
            ends = mate_ends(sides, l)
            whole = assembled(
                half, 1, phase, column_right(half, ends, lane), column_left(half, ends, lane)
            )
            if substep == 0:
                main[l] = whole
            else:
                out_ref[l] = whole[WIDE : WIDE + ROWS]
        if substep == 0:
            ahead = jnp.where(part == WIDE - 1, near, turned(sides, -1))
            behind = jnp.where(part == WIDE, near, turned(sides, 1))
            sides = assembled(sides, 1, phase, ahead, behind)


ORDER = [(dr, dc) for dr in (-1, 0, 1) for dc in (-1, 0, 1) if dr or dc]


def neighbour_counts(table_ref, row, lane):
    own = (row + 1) * (COLS + 2) + lane + 1
    counts = []
    for dr, dc in ORDER:
        target = own + (dr * (COLS + 2) + dc)
        count = jnp.zeros((ROWS, COLS), F32)
        for e in range(table_ref.shape[0]):
            count += jnp.where(table_ref[e] == target, 1.0, 0.0)
        counts.append(count)
    return counts


def neighbour_spread(field, ends, before, after, ends_before, ends_after, counts, row, lane):
    total = jnp.zeros((ROWS, COLS), F32)
    lines = {
        0: (field, ends),
        -1: tuple(
            jnp.where(row == 0, edge, pltpu.roll(v, 1, 0))
            for v, edge in ((field, before), (ends, ends_before))
        ),
        1: tuple(
            jnp.where(row == ROWS - 1, edge, pltpu.roll(v, ROWS - 1, 0))
            for v, edge in ((field, after), (ends, ends_after))
        ),
    }
    for (dr, dc), count in zip(ORDER, counts):
        line, line_ends = lines[dr]
        if dc == -1:
            line = column_left(line, line_ends, lane)
        elif dc == 1:
            line = column_right(line, line_ends, lane)
        total += count * (line - field)
    return total


def top_base_body(other_ref, mate_ref, table_ref, out_ref, weight_ref):
    row, lane = iotas(ROWS)
    top = other_ref[0].astype(F32)
    counts = neighbour_counts(table_ref, row, lane)
    none = jnp.zeros((1, COLS), F32)
    spread = neighbour_spread(
        top, mate_ref[0].astype(F32), none, none, none, none, counts, row, lane
    )
    out_ref[...] = (1.0 - MIXING) * top + other_ref[1].astype(F32) + OCEAN_DIFFUSION * spread
    weight_ref[...] = jnp.zeros_like(weight_ref)
    for n, (dr, _) in enumerate(ORDER):
        if dr:
            edge = 0 if dr < 0 else ROWS - 1
            weight_ref[n : n + 1, :] = counts[n][edge : edge + 1, :]


def edge_terms(line, ends, weights):
    lane = lax.broadcasted_iota(jnp.int32, (1, COLS), 1)
    total = weights[0] * column_left(line, ends, lane) + weights[1] * line
    return OCEAN_DIFFUSION * (total + weights[2] * column_right(line, ends, lane))


def ocean_base_body(
    o_ref,
    sides_ref,
    before_ref,
    after_ref,
    mate_before_ref,
    mate_after_ref,
    table_ref,
    out_ref,
    counts_ref,
):
    row, lane = iotas(ROWS)
    for n, count in enumerate(neighbour_counts(table_ref, row, lane)):
        counts_ref[n] = count
    for l in range(LEV):
        field = o_ref[l]
        spread = neighbour_spread(
            field,
            mate_ends(sides_ref[...], l),
            before_ref[l, WIDE - 1 :, :],
            after_ref[l, :1, :],
            mate_before_ref[l, WIDE - 1 :, :],
            mate_after_ref[l, :1, :],
            [counts_ref[n] for n in range(len(ORDER))],
            row,
            lane,
        )
        below, above = o_ref[max(l - 1, 0)], o_ref[min(l + 1, LEV - 1)]
        out_ref[l] = field + OCEAN_DIFFUSION * spread + MIXING * (above + below - 2.0 * field)


def edge_rows(*fields):
    last = [v[..., ROWS - WIDE :, :].reshape(-1, WIDE, COLS).astype(F32) for v in fields]
    first = [v[..., :WIDE, :].reshape(-1, WIDE, COLS).astype(F32) for v in fields]
    return jnp.concatenate(last, axis=0), jnp.concatenate(first, axis=0)


def from_neighbours(last, first):
    size = lax.axis_size("gx")
    up = [(i, (i + 1) % size) for i in range(size)]
    down = [(j, i) for i, j in up]
    return lax.ppermute(last, "gx", up), lax.ppermute(first, "gx", down)


def from_mate(field):
    return lax.ppermute(field, "gy", [(0, 1), (1, 0)])


def row_hits(labels):
    blocks, width = labels.shape[0], ATMOS_SLOTS
    shape = (blocks, width, COLS)
    diagonal = lax.broadcasted_iota(jnp.int32, shape, 1) == lax.broadcasted_iota(jnp.int32, shape, 2)
    spread = jnp.where(diagonal, labels[:, None, :], 0.0)
    column = jnp.sum(spread, axis=2, keepdims=True).reshape(blocks * width, 1)
    slot = lax.broadcasted_iota(jnp.int32, (blocks, width, 1), 1).reshape(blocks * width, 1)
    column = jnp.where(slot < CAP, column, -1.0).astype(jnp.int32)
    rows = lax.broadcasted_iota(jnp.int32, (blocks * width, ROWS), 1)
    return jnp.where(column == rows, 1.0, 0.0).astype(BF16)


def push_body(
    core_ref,
    arrived_ref,
    base_ref,
    weight_ref,
    before_ref,
    after_ref,
    mate_before_ref,
    mate_after_ref,
    _,
    out_ref,
    hits_ref,
):
    weights = [weight_ref[n : n + 1, :] for n in range(len(ORDER))]
    row = lax.broadcasted_iota(jnp.int32, (ROWS, COLS), 0)
    above = edge_terms(
        before_ref[LEV, WIDE - 1 :, :], mate_before_ref[LEV, WIDE - 1 :, :], weights[:3]
    )
    below = edge_terms(after_ref[LEV, :1, :], mate_after_ref[LEV, :1, :], weights[5:])
    base = base_ref[...] + jnp.where(row == 0, above, 0.0) + jnp.where(row == ROWS - 1, below, 0.0)
    blocks = RANKS // CORES
    arrived = arrived_ref[...].astype(F32).reshape(blocks, CORES, ATMOS_SLOTS, COLS)
    for core in range(CORES):
        part = arrived[:, core]
        hits = row_hits(part[:, CAP, :])
        hits_ref[core] = hits
        values = part.reshape(blocks * ATMOS_SLOTS, COLS).astype(BF16)
        pushed = lax.dot_general(
            hits, values, (((0,), (0,)), ((), ())), preferred_element_type=F32
        )
        out_ref[core] = pushed + jnp.where(core_ref[0] == core, base, 0.0)


def pick_body(mine_ref, mate_ref, hits_ref, out_ref):
    blocks = RANKS // CORES
    for core in range(CORES):
        top = (mine_ref[core] + mate_ref[core]).astype(BF16)
        picked = jnp.dot(hits_ref[core], top, preferred_element_type=F32)
        out_ref[:, core] = picked.astype(BF16).reshape(blocks, ATMOS_SLOTS, COLS)


def sums_body(arrived_ref, base_ref, share_ref, out_ref, first_ref, wide):
    width = OCEAN_SLOTS * NF
    wide[...] = arrived_ref[...].astype(F32).reshape(RANKS * width, COLS)
    labels = wide[pl.ds(CAP * NF, RANKS, stride=width), :]
    by_slot = jnp.concatenate([labels, labels], axis=0).T
    row = lax.broadcasted_iota(jnp.int32, (ROWS, COLS), 0).astype(F32)
    lane = lax.broadcasted_iota(jnp.int32, (1, COLS), 1)
    pieces = []
    for s in range(0, CAP, 2):
        pair = jnp.where(lane < RANKS, by_slot[s : s + 1, :], by_slot[s + 1 : s + 2, :])
        pieces.append(jnp.where(row == pair, 1.0, 0.0).astype(BF16))
    hits = jnp.concatenate(pieces, axis=1)
    forcing = []
    for f in range(0, NF, 2):
        values = [
            jnp.concatenate(
                [wide[pl.ds(s * NF + g, RANKS, stride=width), :] for s in range(CAP)], axis=0
            )
            for g in (f, f + 1)
        ]
        both = jnp.concatenate(values, axis=1).astype(BF16)
        summed = jnp.dot(hits, both, preferred_element_type=F32)
        forcing += [summed[:, :COLS], summed[:, COLS:]]
    first_ref[...] = forcing[0]
    for l in range(LEV):
        level = base_ref[l]
        for f in range(NF):
            level += share_ref[l, f] * forcing[f]
        out_ref[l] = level


def ocean_sums(arrived, base, share):
    return pl.pallas_call(
        sums_body,
        out_shape=(
            jax.ShapeDtypeStruct((LEV, ROWS, COLS), F32),
            jax.ShapeDtypeStruct((ROWS, COLS), F32),
        ),
        in_specs=[VMEM, VMEM, SMEM],
        out_specs=(VMEM, VMEM),
        scratch_shapes=[pltpu.VMEM((RANKS * OCEAN_SLOTS * NF, COLS), F32)],
        compiler_params=pltpu.CompilerParams(vmem_limit_bytes=24 << 20),
    )(arrived, base, share)


def remap_body(pos_ref, arrived_ref, w_ref, out_ref, held, values, own, sems):
    copy = weight_copies(w_ref, held, sems, REMAP_ROWS)
    for c in range(ROWS // REMAP_ROWS):
        copy(c).start()
    slots = RANKS * ATMOS_SLOTS
    by_column = arrived_ref[...].astype(F32).reshape(slots, COLS).T.astype(BF16)
    at = lax.broadcasted_iota(jnp.int32, (slots, ROWS), 0)
    groups = ROWS // COLS
    for k in range(K):
        hits = jnp.where(at == pos_ref[K + k : K + k + 1, :], 1.0, 0.0).astype(BF16)
        found = jnp.dot(by_column, hits, preferred_element_type=F32).astype(BF16)
        for g in range(groups):
            values[g, k * COLS : (k + 1) * COLS, :] = found[:, g * COLS : (g + 1) * COLS]
    lane = lax.broadcasted_iota(jnp.int32, (COLS, COLS), 1)
    parts = COLS // REMAP_ROWS

    @pl.loop(0, ROWS // REMAP_ROWS)
    def _(c):
        copy(c).wait()
        block = held.at[pl.ds(c * REMAP_ROWS, REMAP_ROWS)]
        tiles = jnp.concatenate(
            [block[:, k].reshape(REMAP_ROWS * COLS, COLS) for k in range(K)], axis=1
        )
        crossed = jnp.dot(tiles, values[c // parts], preferred_element_type=F32)
        kept = own[c // parts]
        for i in range(REMAP_ROWS):
            mine = lane == (c % parts) * REMAP_ROWS + i
            kept = jnp.where(mine, crossed[i * COLS : (i + 1) * COLS], kept)
        own[c // parts] = kept

    for g in range(groups):
        out_ref[g * COLS : (g + 1) * COLS, :] = own[g].T


def remap(pos, arrived, weights):
    return pl.pallas_call(
        remap_body,
        out_shape=jax.ShapeDtypeStruct((ROWS, COLS), F32),
        in_specs=[VMEM, VMEM, HBM],
        out_specs=VMEM,
        scratch_shapes=WEIGHTS_HELD
        + [
            pltpu.VMEM((ROWS // COLS, K * COLS, COLS), BF16),
            pltpu.VMEM((ROWS // COLS, COLS, COLS), F32),
            pltpu.SemaphoreType.DMA((ROWS // REMAP_ROWS,)),
        ],
        compiler_params=pltpu.CompilerParams(vmem_limit_bytes=32 << 20),
    )(pos, arrived, weights)


def to_peers(payload, axes):
    return lax.all_to_all(payload, axes, split_axis=0, concat_axis=0, tiled=True)


def local(
    layered_heat_profile,
    prior_marine_heat,
    transfer_factor_table,
    depth_fraction_matrix,
    adjacent_cell_table,
    destination_water_peer,
    destination_water_line,
    interpolation_matrix_blocks,
):
    is_atmosphere_side = lax.axis_index("comp") == 0
    own = layered_heat_profile[0]
    block = jax.ShapeDtypeStruct((LEV, ROWS, COLS), F32)
    plane = jax.ShapeDtypeStruct((ROWS, COLS), F32)
    swap = [(0, 1), (1, 0)]

    cross = cross_kernel(lax.axis_index("comp").reshape(1), own)
    other = lax.ppermute(cross, "comp", [(0, 1), (1, 0)])

    def atmosphere_early():
        packed, pos = atmos_flux(
            destination_water_peer,
            destination_water_line,
            own,
            prior_marine_heat,
            transfer_factor_table,
            interpolation_matrix_blocks,
            depth_fraction_matrix,
        )
        nothing = jnp.zeros((LEV, WIDE, COLS), F32)
        return packed, pos, nothing, nothing

    def ocean_early():
        before, after = from_neighbours(*edge_rows(own))
        packed = unused((RANKS, ATMOS_SLOTS, COLS), BF16)
        return packed, jnp.zeros((2 * K, ROWS), jnp.int32), before, after

    packed, pos, *ocean_rows = lax.cond(is_atmosphere_side, atmosphere_early, ocean_early)

    def atmosphere():
        by_chip = (RANKS // CORES, CORES * ATMOS_SLOTS, COLS)
        payload, *edges = lax.optimization_barrier((packed, *edge_rows(own, other[:1])))
        rows = from_neighbours(*edges)
        arrived = to_peers(payload.reshape(by_chip), "gx")
        sides = from_mate(shadow_call(sides_body, plane, [VMEM])(own))
        moved = shadow_call(local_body, block, [VMEM], us=3)(own)
        base, weights = shadow_call(
            top_base_body, (plane, jax.ShapeDtypeStruct((len(ORDER), COLS), F32)), [VMEM] * 3, us=2
        )(other, from_mate(other), adjacent_cell_table)
        *rows, moved, base = lax.optimization_barrier((*rows, moved, base))
        rows = [*rows, *map(from_mate, rows)]
        mine, hits = call(
            push_body,
            (
                jax.ShapeDtypeStruct((CORES, ROWS, COLS), F32),
                jax.ShapeDtypeStruct((CORES, RANKS // CORES * ATMOS_SLOTS, ROWS), BF16),
            ),
            [SMEM] + [VMEM] * 7 + [ANY],
        )(
            lax.axis_index("gy").reshape(1),
            arrived.reshape(RANKS, ATMOS_SLOTS, COLS),
            base,
            weights,
            *rows,
            moved,
        )
        picked = call(
            pick_body,
            jax.ShapeDtypeStruct((RANKS // CORES, CORES, ATMOS_SLOTS, COLS), BF16),
            [VMEM] * 3,
        )(mine, from_mate(mine), hits)
        returned = to_peers(picked.reshape(by_chip), "gx")
        wide = pltpu.VMEM((LEV, EXTENDED, COLS), F32)
        final = shadow_call(
            substeps_body, block, [VMEM] * 6 + [ANY], scratch_shapes=[wide]
        )(moved, sides, *rows, picked)
        return final, remap(
            pos, returned.reshape(RANKS, ATMOS_SLOTS, COLS), interpolation_matrix_blocks
        )

    def ocean():
        payload = ocean_flux(
            destination_water_peer,
            destination_water_line,
            other,
            prior_marine_heat,
            transfer_factor_table,
            interpolation_matrix_blocks,
        )
        arrived = to_peers(payload.reshape(RANKS, OCEAN_SLOTS * NF, COLS), ("gx", "gy"))
        sides = from_mate(shadow_call(sides_body, plane, [VMEM])(own))
        base = shadow_call(
            ocean_base_body,
            block,
            [VMEM] * 7,
            scratch_shapes=[pltpu.VMEM((len(ORDER), ROWS, COLS), F32)],
        )(own, sides, *ocean_rows, *map(from_mate, ocean_rows), adjacent_cell_table)
        return ocean_sums(
            arrived.reshape(RANKS * OCEAN_SLOTS, NF, COLS), base, depth_fraction_matrix
        )

    state, plane_out = lax.cond(is_atmosphere_side, atmosphere, ocean)
    return state[None], plane_out[None]


def solution(mesh):
    return jax.shard_map(
        local,
        mesh=mesh,
        in_specs=(
            P("comp", None, "gx", "gy"),
            P("gx", "gy"),
            P(None, "gx", "gy"),
            P(),
            P(None, "gx", "gy"),
            P(("gx", "gy"), None),
            P(("gx", "gy"), None),
            P(("gx", "gy"), None, None, None),
        ),
        out_specs=(P("comp", None, "gx", "gy"), P("comp", "gx", "gy")),
        check_vma=False,
    )
```

```python
import functools

import jax
import jax.numpy as jnp
import numpy as np
from jax import lax
from jax.experimental import pallas as pl
from jax.experimental.pallas import tpu as pltpu
from jax.sharding import PartitionSpec as P

ATMOS_DIFFUSION = 0.01
MIXING = 0.2
OCEAN_DIFFUSION = 0.12

RANKS = 64
CAP = 18
CORES = 2
LEV = 8
NF = 8
ROWS = 256
COLS = 128
K = 2
WIDE = 8
OCEAN_SLOTS = 19
ATMOS_SLOTS = 24

VMEM = pl.BlockSpec(memory_space=pltpu.VMEM)
SMEM = pl.BlockSpec(memory_space=pltpu.SMEM)
ANY = pl.BlockSpec(memory_space=pl.ANY)
HBM = pl.BlockSpec(memory_space=pltpu.HBM)
F32 = jnp.float32
BF16 = jnp.bfloat16


def second_table():
    gll_nodes = np.array([-1.0, -1.0 / np.sqrt(5.0), 1.0 / np.sqrt(5.0), 1.0])
    poly_order = 3
    legendre = (5.0 * gll_nodes**3 - 3.0 * gll_nodes) / 2.0
    derivative = np.zeros((4, 4))
    for row_index in range(4):
        for col_index in range(4):
            if row_index != col_index:
                derivative[row_index, col_index] = legendre[row_index] / (
                    legendre[col_index] * (gll_nodes[row_index] - gll_nodes[col_index])
                )
    derivative[0, 0] = -poly_order * (poly_order + 1) / 4.0
    derivative[3, 3] = poly_order * (poly_order + 1) / 4.0
    return derivative @ derivative


SECOND = second_table()


def call(body, out_shape, specs, **params):
    return pl.pallas_call(
        body,
        out_shape=out_shape,
        in_specs=specs,
        out_specs=jax.tree.map(lambda _: VMEM, out_shape),
        compiler_params=pltpu.CompilerParams(vmem_limit_bytes=params.pop("vmem", 24 << 20)),
        **params,
    )


def shadow_call(body, out_shape, specs, us=0, **params):
    cost = pl.CostEstimate(flops=0, bytes_accessed=us * 3_690_000, transcendentals=0)
    return call(body, out_shape, specs, cost_estimate=cost, **params)


def unused(shape, dtype):
    return pl.pallas_call(lambda out_ref: None, out_shape=pltpu.HBM(shape, dtype), out_specs=HBM)()


def route(peer_ref, line_ref, pos_ref, label_ref):
    count = ROWS * K
    peer = jnp.concatenate([peer_ref[k : k + 1, :] for k in range(K)], axis=1)
    line = jnp.concatenate([line_ref[k : k + 1, :] for k in range(K)], axis=1)
    hits = lax.broadcasted_iota(jnp.int32, (RANKS, count), 0) == peer
    hits_f = jnp.where(hits, 1.0, 0.0)
    earlier = lax.broadcasted_iota(jnp.int32, (count, count), 0) < lax.broadcasted_iota(
        jnp.int32, (count, count), 1
    )
    before = jnp.dot(
        hits_f.astype(BF16),
        jnp.where(earlier, 1.0, 0.0).astype(BF16),
        preferred_element_type=F32,
    )
    slot = jnp.sum(hits_f * before, axis=0, keepdims=True).astype(jnp.int32)
    for width, at in ((OCEAN_SLOTS, 0), (ATMOS_SLOTS, K)):
        position = peer * width + slot
        for k in range(K):
            pos_ref[at + k : at + k + 1, :] = position[:, k * ROWS : (k + 1) * ROWS]
    slot_hits = lax.broadcasted_iota(jnp.int32, (COLS, count), 0) == slot
    shifted = jnp.where(hits, (line + 1).astype(F32), 0.0).astype(BF16)
    label_ref[...] = (
        lax.dot_general(
            shifted,
            jnp.where(slot_hits, 1.0, 0.0).astype(BF16),
            (((1,), (1,)), ((), ())),
            preferred_element_type=F32,
        )
        - 1.0
    )


def turned(field, lanes):
    lanes = lanes % COLS
    return field if lanes == 0 else pltpu.roll(field, lanes, 1)


def cross_body(side_ref, own_ref, out_ref, last_ref, first_ref, held, edges, sems):
    copies = [
        pltpu.make_async_copy(own_ref.at[pl.ds(0, 2)], held, sems.at[0]),
        pltpu.make_async_copy(own_ref.at[:, pl.ds(ROWS - WIDE, WIDE)], edges.at[0], sems.at[1]),
        pltpu.make_async_copy(own_ref.at[:, pl.ds(0, WIDE)], edges.at[1], sems.at[2]),
    ]
    for copy in copies:
        copy.start()
    copies[0].wait()
    top = held[0]
    high = top.astype(BF16)
    rest = top - high.astype(F32)
    out_ref[0] = high
    other = MIXING * held[1] + (1.0 - MIXING) * rest
    out_ref[1] = jnp.where(side_ref[0] == 0, rest, other).astype(BF16)
    for copy in copies[1:]:
        copy.wait()
    for l in range(LEV):
        last_ref[l : l + 1, :] = edges[0, l, WIDE - 1 :, :]
        first_ref[l : l + 1, :] = edges[1, l, :1, :]


def cross_kernel(side, own):
    edge = jax.ShapeDtypeStruct((LEV, COLS), F32)
    return call(
        cross_body,
        (jax.ShapeDtypeStruct((2, ROWS, COLS), BF16), edge, edge),
        [SMEM, HBM],
        scratch_shapes=[
            pltpu.VMEM((2, ROWS, COLS), F32),
            pltpu.VMEM((2, LEV, WIDE, COLS), F32),
            pltpu.SemaphoreType.DMA((3,)),
        ],
    )(side, own)


def packed_sides(levels, lane):
    packed = jnp.zeros(lane.shape, F32)
    for l, level in enumerate(levels):
        packed = jnp.where(lane // (2 * WIDE) == l, turned(level, WIDE + 2 * WIDE * l), packed)
    return packed


def sides_body(own_ref, out_ref):
    lane = lax.broadcasted_iota(jnp.int32, (ROWS, COLS), 1)
    out_ref[...] = packed_sides([own_ref[l] for l in range(LEV)], lane)


FLUX_ROWS = 16
REMAP_ROWS = 32
CHUNKS = ROWS // FLUX_ROWS


def weight_copies(source, held, sems, per):
    def copy(c):
        part = pl.ds(c * per, per)
        return pltpu.make_async_copy(source.at[part], held.at[part], sems.at[c])

    return copy


def side_by_side(held, b):
    return jnp.concatenate([held[b, k] for k in range(K)], axis=1)


WEIGHTS_HELD = [
    pltpu.VMEM((ROWS, K, COLS, COLS), BF16),
]
ROUTING = [
    pltpu.VMEM((K, ROWS), jnp.int32),
    pltpu.VMEM((K, ROWS), jnp.int32),
    pltpu.VMEM((RANKS, COLS), F32),
    pltpu.SMEM((2 * K, ROWS), jnp.int32),
]
FIELDS = [
    pltpu.VMEM((ROWS, COLS), F32),
    pltpu.VMEM((NF, ROWS, COLS), F32),
]


def ocean_flux_body(
    peer_ref,
    line_ref,
    air_hbm_ref,
    prior_ref,
    factor_ref,
    w_ref,
    out_ref,
    held,
    peer,
    line,
    label,
    pos,
    prior,
    factor,
    air_ref,
    pos_rows,
    packed,
    rows,
    sems,
):
    copy = weight_copies(w_ref, held, sems, FLUX_ROWS)
    index_copies = [
        pltpu.make_async_copy(peer_ref, peer, sems.at[CHUNKS]),
        pltpu.make_async_copy(line_ref, line, sems.at[CHUNKS + 1]),
    ]
    field_copies = [
        pltpu.make_async_copy(prior_ref, prior, sems.at[CHUNKS + 2]),
        pltpu.make_async_copy(air_hbm_ref, air_ref, sems.at[CHUNKS + 6]),
        pltpu.make_async_copy(factor_ref, factor, sems.at[CHUNKS + 3]),
    ]
    for started in index_copies + field_copies:
        started.start()
    for c in range(CHUNKS):
        copy(c).start()
    packed[...] = jnp.zeros_like(packed)
    for started in index_copies:
        started.wait()
    route(peer, line, pos_rows, label)
    to_scalars = pltpu.make_async_copy(pos_rows, pos, sems.at[CHUNKS + 4])
    to_scalars.start()
    for d in range(RANKS):
        packed[d * OCEAN_SLOTS + CAP] = jnp.broadcast_to(label[d : d + 1, :], (NF, COLS)).astype(
            BF16
        )
    for started in field_copies:
        started.wait()
    difference = air_ref[0].astype(F32) + air_ref[1].astype(F32) - prior[...]
    for f in range(NF):
        rows[pl.ds(f, ROWS, stride=NF), :] = factor[f] * difference
    to_scalars.wait()

    @pl.loop(0, CHUNKS)
    def _(c):
        copy(c).wait()
        for i in range(FLUX_ROWS):
            b = c * FLUX_ROWS + i
            flux = rows[pl.ds(pl.multiple_of(b * NF, NF), NF), :].astype(BF16)
            part = jnp.dot(flux, side_by_side(held, b), preferred_element_type=F32).astype(BF16)
            for k in range(K):
                packed[pos[k, b]] = part[:, k * COLS : (k + 1) * COLS]

    done = pltpu.make_async_copy(packed, out_ref, sems.at[CHUNKS + 5])
    done.start()
    done.wait()


def ocean_flux(peer, line, air, prior, factors, weights):
    return pl.pallas_call(
        ocean_flux_body,
        out_shape=pltpu.HBM((RANKS * OCEAN_SLOTS, NF, COLS), BF16),
        in_specs=[HBM, HBM, ANY, HBM, HBM, HBM],
        out_specs=HBM,
        scratch_shapes=WEIGHTS_HELD
        + ROUTING
        + FIELDS
        + [
            pltpu.VMEM((2, ROWS, COLS), BF16),
            pltpu.VMEM((2 * K, ROWS), jnp.int32),
            pltpu.VMEM((RANKS * OCEAN_SLOTS, NF, COLS), BF16),
            pltpu.VMEM((ROWS * NF, COLS), F32),
            pltpu.SemaphoreType.DMA((CHUNKS + 7,)),
        ],
        compiler_params=pltpu.CompilerParams(vmem_limit_bytes=32 << 20),
    )(peer.T, line.T, air, prior, factors, weights)


def atmos_flux_body(
    peer_ref,
    line_ref,
    own_ref,
    prior_ref,
    factor_ref,
    w_ref,
    share_ref,
    out_ref,
    pos_ref,
    held,
    peer,
    line,
    label,
    pos,
    prior,
    factor,
    air,
    packed,
    rows,
    sems,
):
    copy = weight_copies(w_ref, held, sems, FLUX_ROWS)
    index_copies = [
        pltpu.make_async_copy(peer_ref, peer, sems.at[CHUNKS]),
        pltpu.make_async_copy(line_ref, line, sems.at[CHUNKS + 1]),
    ]
    field_copies = [
        pltpu.make_async_copy(prior_ref, prior, sems.at[CHUNKS + 2]),
        pltpu.make_async_copy(own_ref.at[0], air, sems.at[CHUNKS + 3]),
        pltpu.make_async_copy(factor_ref, factor, sems.at[CHUNKS + 4]),
    ]
    for started in index_copies + field_copies:
        started.start()
    for c in range(CHUNKS):
        copy(c).start()
    packed[...] = jnp.zeros_like(packed)
    rows[...] = jnp.zeros_like(rows)
    for started in index_copies:
        started.wait()
    route(peer, line, pos_ref, label)
    to_scalars = pltpu.make_async_copy(pos_ref, pos, sems.at[CHUNKS + 5])
    to_scalars.start()
    for d in range(RANKS):
        packed[d * ATMOS_SLOTS + CAP : d * ATMOS_SLOTS + CAP + 1, :] = label[d : d + 1, :]
    for started in field_copies:
        started.wait()
    mixed = share_ref[0, 0] * factor[0]
    for f in range(1, NF):
        mixed += share_ref[0, f] * factor[f]
    flux = mixed * (air[...] - prior[...])
    high = flux.astype(BF16).astype(F32)
    rows[pl.ds(0, ROWS, stride=8), :] = high
    rows[pl.ds(1, ROWS, stride=8), :] = flux - high
    to_scalars.wait()

    @pl.loop(0, CHUNKS)
    def _(c):
        copy(c).wait()
        for i in range(FLUX_ROWS):
            b = c * FLUX_ROWS + i
            pair = rows[pl.ds(pl.multiple_of(b * 8, 8), 8), :].astype(BF16)
            part = jnp.dot(pair, side_by_side(held, b), preferred_element_type=F32)
            part = part[0:1, :] + part[1:2, :]
            for k in range(K):
                packed[pl.ds(pos[K + k, b], 1), :] = part[:, k * COLS : (k + 1) * COLS]

    out_ref[...] = packed[...].astype(BF16).reshape(RANKS, ATMOS_SLOTS, COLS)


def atmos_flux(peer, line, own, prior, factors, weights, share):
    return pl.pallas_call(
        atmos_flux_body,
        out_shape=(
            jax.ShapeDtypeStruct((RANKS, ATMOS_SLOTS, COLS), BF16),
            jax.ShapeDtypeStruct((2 * K, ROWS), jnp.int32),
        ),
        in_specs=[HBM, HBM, HBM, HBM, HBM, HBM, SMEM],
        out_specs=(VMEM, VMEM),
        scratch_shapes=WEIGHTS_HELD
        + ROUTING
        + FIELDS
        + [
            pltpu.VMEM((ROWS, COLS), F32),
            pltpu.VMEM((RANKS * ATMOS_SLOTS, COLS), F32),
            pltpu.VMEM((ROWS * 8, COLS), F32),
            pltpu.SemaphoreType.DMA((CHUNKS + 6,)),
        ],
        compiler_params=pltpu.CompilerParams(vmem_limit_bytes=32 << 20),
    )(peer.T, line.T, own, prior, factors, weights, share)


EXTENDED = ROWS + 2 * WIDE


def iotas(rows):
    return (
        lax.broadcasted_iota(jnp.int32, (rows, COLS), 0),
        lax.broadcasted_iota(jnp.int32, (rows, COLS), 1),
    )


def mate_ends(sides, level):
    return turned(sides, -(2 * WIDE * level + WIDE))


def column_left(field, ends, lane):
    return pltpu.roll(jnp.where(lane == COLS - 1, ends, field), 1, 1)


def column_right(field, ends, lane):
    return pltpu.roll(jnp.where(lane == 0, ends, field), COLS - 1, 1)


def second_along(field, axis, index):
    phase = index % 4
    total = None
    for shift in range(-3, 4):
        factor = jnp.zeros(index.shape, F32)
        for p in range(4):
            if 0 <= p + shift < 4:
                factor = jnp.where(phase == p, F32(SECOND[p, p + shift]), factor)
        moved = field if shift == 0 else pltpu.roll(field, (-shift) % field.shape[axis], axis)
        total = factor * moved if total is None else total + factor * moved
    return total


def diffused(field, above, below):
    groups = field.reshape(-1, 8, COLS)
    along = second_along(groups, 1, lax.broadcasted_iota(jnp.int32, (1, 8, COLS), 1))
    along = along.reshape(field.shape)
    along += second_along(field, 1, lax.broadcasted_iota(jnp.int32, (1, COLS), 1))
    return field + ATMOS_DIFFUSION * along + MIXING * (above + below - 2.0 * field)


def assembled(field, axis, phase, ahead, behind):
    return jnp.where(
        phase == 3,
        0.5 * (field + ahead),
        jnp.where(phase == 0, 0.5 * (field + behind), field),
    )


def assembled_rows(field, row):
    ahead = pltpu.roll(field, EXTENDED - 1, 0)
    return assembled(field, 0, row % 4, ahead, pltpu.roll(field, 1, 0))


def diffused_levels(levels):
    return [
        diffused(levels[l], levels[min(l + 1, LEV - 1)], levels[max(l - 1, 0)]) for l in range(LEV)
    ]


def local_body(u_ref, out_ref):
    for l, field in enumerate(diffused_levels([u_ref[l] for l in range(LEV)])):
        out_ref[l] = field


def substeps_body(
    local_ref, sides_ref, before_ref, after_ref, mate_before_ref, mate_after_ref, _, out_ref, main
):
    row, lane = iotas(EXTENDED)
    phase, part = lane % 4, lane % (2 * WIDE)
    edges = [diffused_levels([r[l] for l in range(LEV)]) for r in (before_ref, after_ref)]
    thin = lax.broadcasted_iota(jnp.int32, (WIDE, COLS), 1)
    ends = [
        packed_sides([r[l] for l in range(LEV)], thin) for r in (mate_before_ref, mate_after_ref)
    ]
    sides = jnp.concatenate([ends[0], sides_ref[...], ends[1]], axis=0)
    for substep in range(2):
        over = jnp.where(lane < COLS - 2 * WIDE, turned(sides, -2 * WIDE), sides)
        under = jnp.where(lane >= 2 * WIDE, turned(sides, 2 * WIDE), sides)
        sides = assembled_rows(diffused(sides, over, under), row)
        near = jnp.zeros((EXTENDED, COLS), F32)
        for l in range(LEV):
            if substep == 0:
                half = jnp.concatenate([edges[0][l], local_ref[l], edges[1][l]], axis=0)
            else:
                half = diffused(main[l], main[min(l + 1, LEV - 1)], main[max(l - 1, 0)])
            half = assembled_rows(half, row)
            if substep == 0:
                first = turned(half, 2 * WIDE * l + WIDE - 1)
                last = turned(half, 2 * WIDE * l + WIDE + 1)
                own_level = lane // (2 * WIDE) == l
                near = jnp.where(own_level, jnp.where(part < WIDE, first, last), near)
            ends = mate_ends(sides, l)
            whole = assembled(
                half, 1, phase, column_right(half, ends, lane), column_left(half, ends, lane)
            )
            if substep == 0:
                main[l] = whole
            else:
                out_ref[l] = whole[WIDE : WIDE + ROWS]
        if substep == 0:
            ahead = jnp.where(part == WIDE - 1, near, turned(sides, -1))
            behind = jnp.where(part == WIDE, near, turned(sides, 1))
            sides = assembled(sides, 1, phase, ahead, behind)


ORDER = [(dr, dc) for dr in (-1, 0, 1) for dc in (-1, 0, 1) if dr or dc]


def neighbour_counts(table_ref, row, lane):
    own = (row + 1) * (COLS + 2) + lane + 1
    counts = []
    for dr, dc in ORDER:
        target = own + (dr * (COLS + 2) + dc)
        count = jnp.zeros((ROWS, COLS), F32)
        for e in range(table_ref.shape[0]):
            count += jnp.where(table_ref[e] == target, 1.0, 0.0)
        counts.append(count)
    return counts


def neighbour_spread(field, ends, before, after, ends_before, ends_after, counts, row, lane):
    total = jnp.zeros((ROWS, COLS), F32)
    lines = {
        0: (field, ends),
        -1: tuple(
            jnp.where(row == 0, edge, pltpu.roll(v, 1, 0))
            for v, edge in ((field, before), (ends, ends_before))
        ),
        1: tuple(
            jnp.where(row == ROWS - 1, edge, pltpu.roll(v, ROWS - 1, 0))
            for v, edge in ((field, after), (ends, ends_after))
        ),
    }
    for (dr, dc), count in zip(ORDER, counts):
        line, line_ends = lines[dr]
        if dc == -1:
            line = column_left(line, line_ends, lane)
        elif dc == 1:
            line = column_right(line, line_ends, lane)
        total += count * (line - field)
    return total


def edge_weights(counts, weight_ref):
    weight_ref[...] = jnp.zeros_like(weight_ref)
    for n, (dr, _) in enumerate(ORDER):
        if dr:
            edge = 0 if dr < 0 else ROWS - 1
            weight_ref[n : n + 1, :] = counts[n][edge : edge + 1, :]


def top_base_body(other_ref, mate_ref, table_ref, out_ref, weight_ref):
    row, lane = iotas(ROWS)
    top = other_ref[0].astype(F32)
    counts = neighbour_counts(table_ref, row, lane)
    none = jnp.zeros((1, COLS), F32)
    spread = neighbour_spread(
        top, mate_ref[0].astype(F32), none, none, none, none, counts, row, lane
    )
    out_ref[...] = (1.0 - MIXING) * top + other_ref[1].astype(F32) + OCEAN_DIFFUSION * spread
    edge_weights(counts, weight_ref)


def edge_terms(line, ends, weights):
    lane = lax.broadcasted_iota(jnp.int32, (1, COLS), 1)
    total = weights[0] * column_left(line, ends, lane) + weights[1] * line
    return OCEAN_DIFFUSION * (total + weights[2] * column_right(line, ends, lane))


def both_edges(before, before_ends, after, after_ends, weight_ref):
    weights = [weight_ref[n : n + 1, :] for n in range(len(ORDER))]
    return edge_terms(before, before_ends, weights[:3]), edge_terms(after, after_ends, weights[5:])


def ocean_base_body(
    o_ref,
    sides_ref,
    before_ref,
    after_ref,
    mate_before_ref,
    mate_after_ref,
    table_ref,
    out_ref,
    counts_ref,
):
    row, lane = iotas(ROWS)
    for n, count in enumerate(neighbour_counts(table_ref, row, lane)):
        counts_ref[n] = count
    for l in range(LEV):
        field = o_ref[l]
        spread = neighbour_spread(
            field,
            mate_ends(sides_ref[...], l),
            before_ref[l : l + 1, :],
            after_ref[l : l + 1, :],
            mate_before_ref[l : l + 1, :],
            mate_after_ref[l : l + 1, :],
            [counts_ref[n] for n in range(len(ORDER))],
            row,
            lane,
        )
        below, above = o_ref[max(l - 1, 0)], o_ref[min(l + 1, LEV - 1)]
        out_ref[l] = field + OCEAN_DIFFUSION * spread + MIXING * (above + below - 2.0 * field)


def edge_rows(*fields):
    last = [v[..., ROWS - WIDE :, :].reshape(-1, WIDE, COLS).astype(F32) for v in fields]
    first = [v[..., :WIDE, :].reshape(-1, WIDE, COLS).astype(F32) for v in fields]
    return jnp.concatenate(last, axis=0), jnp.concatenate(first, axis=0)


def from_neighbours(last, first):
    size = lax.axis_size("gx")
    up = [(i, (i + 1) % size) for i in range(size)]
    down = [(j, i) for i, j in up]
    return lax.ppermute(last, "gx", up), lax.ppermute(first, "gx", down)


def from_mate(field):
    return lax.ppermute(field, "gy", [(0, 1), (1, 0)])


def row_hits(labels):
    blocks, width = labels.shape[0], ATMOS_SLOTS
    shape = (blocks, width, COLS)
    diagonal = lax.broadcasted_iota(jnp.int32, shape, 1) == lax.broadcasted_iota(jnp.int32, shape, 2)
    spread = jnp.where(diagonal, labels[:, None, :], 0.0)
    column = jnp.sum(spread, axis=2, keepdims=True).reshape(blocks * width, 1)
    slot = lax.broadcasted_iota(jnp.int32, (blocks, width, 1), 1).reshape(blocks * width, 1)
    column = jnp.where(slot < CAP, column, -1.0).astype(jnp.int32)
    rows = lax.broadcasted_iota(jnp.int32, (blocks * width, ROWS), 1)
    return jnp.where(column == rows, 1.0, 0.0).astype(BF16)


def push_body(core_ref, arrived_ref, base_ref, out_ref, hits_ref):
    blocks = RANKS // CORES
    arrived = arrived_ref[...].astype(F32).reshape(blocks, CORES, ATMOS_SLOTS, COLS)
    for core in range(CORES):
        part = arrived[:, core]
        hits = row_hits(part[:, CAP, :])
        hits_ref[core] = hits
        values = part.reshape(blocks * ATMOS_SLOTS, COLS).astype(BF16)
        pushed = lax.dot_general(
            hits, values, (((0,), (0,)), ((), ())), preferred_element_type=F32
        )
        out_ref[core] = pushed + jnp.where(core_ref[0] == core, base_ref[...], 0.0)


def pick_body(
    core_ref,
    mine_ref,
    mate_ref,
    weight_ref,
    mate_weight_ref,
    before_ref,
    after_ref,
    mate_before_ref,
    mate_after_ref,
    hits_ref,
    out_ref,
):
    blocks = RANKS // CORES
    row = lax.broadcasted_iota(jnp.int32, (ROWS, COLS), 0)
    own_rows = [before_ref[LEV, WIDE - 1 :, :], after_ref[LEV, :1, :]]
    mate_rows = [mate_before_ref[LEV, WIDE - 1 :, :], mate_after_ref[LEV, :1, :]]
    own = both_edges(own_rows[0], mate_rows[0], own_rows[1], mate_rows[1], weight_ref)
    mate = both_edges(mate_rows[0], own_rows[0], mate_rows[1], own_rows[1], mate_weight_ref)
    for core in range(CORES):
        above, below = (jnp.where(core_ref[0] == core, o, m) for o, m in zip(own, mate))
        top = mine_ref[core] + mate_ref[core]
        top += jnp.where(row == 0, above, 0.0) + jnp.where(row == ROWS - 1, below, 0.0)
        picked = jnp.dot(hits_ref[core], top.astype(BF16), preferred_element_type=F32)
        out_ref[:, core] = picked.astype(BF16).reshape(blocks, ATMOS_SLOTS, COLS)


def sums_body(arrived_ref, base_ref, share_ref, out_ref, first_ref, wide):
    width = OCEAN_SLOTS * NF
    wide[...] = arrived_ref[...].astype(F32).reshape(RANKS * width, COLS)
    labels = wide[pl.ds(CAP * NF, RANKS, stride=width), :]
    by_slot = jnp.concatenate([labels, labels], axis=0).T
    row = lax.broadcasted_iota(jnp.int32, (ROWS, COLS), 0).astype(F32)
    lane = lax.broadcasted_iota(jnp.int32, (1, COLS), 1)
    pieces = []
    for s in range(0, CAP, 2):
        pair = jnp.where(lane < RANKS, by_slot[s : s + 1, :], by_slot[s + 1 : s + 2, :])
        pieces.append(jnp.where(row == pair, 1.0, 0.0).astype(BF16))
    hits = jnp.concatenate(pieces, axis=1)
    forcing = []
    for f in range(0, NF, 2):
        values = [
            jnp.concatenate(
                [wide[pl.ds(s * NF + g, RANKS, stride=width), :] for s in range(CAP)], axis=0
            )
            for g in (f, f + 1)
        ]
        both = jnp.concatenate(values, axis=1).astype(BF16)
        summed = jnp.dot(hits, both, preferred_element_type=F32)
        forcing += [summed[:, :COLS], summed[:, COLS:]]
    first_ref[...] = forcing[0]
    for l in range(LEV):
        level = base_ref[l]
        for f in range(NF):
            level += share_ref[l, f] * forcing[f]
        out_ref[l] = level


def ocean_sums(arrived, base, share):
    return pl.pallas_call(
        sums_body,
        out_shape=(
            jax.ShapeDtypeStruct((LEV, ROWS, COLS), F32),
            jax.ShapeDtypeStruct((ROWS, COLS), F32),
        ),
        in_specs=[VMEM, VMEM, SMEM],
        out_specs=(VMEM, VMEM),
        scratch_shapes=[pltpu.VMEM((RANKS * OCEAN_SLOTS * NF, COLS), F32)],
        compiler_params=pltpu.CompilerParams(vmem_limit_bytes=24 << 20),
    )(arrived, base, share)


def remap_body(pos_hbm_ref, arrived_ref, w_ref, out_ref, held, pos_ref, values, own, sems):
    pos_copy = pltpu.make_async_copy(pos_hbm_ref, pos_ref, sems.at[ROWS // REMAP_ROWS])
    pos_copy.start()
    copy = weight_copies(w_ref, held, sems, REMAP_ROWS)
    for c in range(ROWS // REMAP_ROWS):
        copy(c).start()
    slots = RANKS * ATMOS_SLOTS
    by_column = arrived_ref[...].astype(F32).reshape(slots, COLS).T.astype(BF16)
    at = lax.broadcasted_iota(jnp.int32, (slots, ROWS), 0)
    groups = ROWS // COLS
    pos_copy.wait()
    for k in range(K):
        hits = jnp.where(at == pos_ref[K + k : K + k + 1, :], 1.0, 0.0).astype(BF16)
        found = jnp.dot(by_column, hits, preferred_element_type=F32).astype(BF16)
        for g in range(groups):
            values[g, k * COLS : (k + 1) * COLS, :] = found[:, g * COLS : (g + 1) * COLS]
    lane = lax.broadcasted_iota(jnp.int32, (COLS, COLS), 1)
    parts = COLS // REMAP_ROWS

    @pl.loop(0, ROWS // REMAP_ROWS)
    def _(c):
        copy(c).wait()
        block = held.at[pl.ds(c * REMAP_ROWS, REMAP_ROWS)]
        tiles = jnp.concatenate(
            [block[:, k].reshape(REMAP_ROWS * COLS, COLS) for k in range(K)], axis=1
        )
        crossed = jnp.dot(tiles, values[c // parts], preferred_element_type=F32)
        kept = own[c // parts]
        for i in range(REMAP_ROWS):
            mine = lane == (c % parts) * REMAP_ROWS + i
            kept = jnp.where(mine, crossed[i * COLS : (i + 1) * COLS], kept)
        own[c // parts] = kept

    for g in range(groups):
        out_ref[g * COLS : (g + 1) * COLS, :] = own[g].T


def remap(pos, arrived, weights):
    return pl.pallas_call(
        remap_body,
        out_shape=jax.ShapeDtypeStruct((ROWS, COLS), F32),
        in_specs=[ANY, VMEM, HBM],
        out_specs=VMEM,
        scratch_shapes=WEIGHTS_HELD
        + [
            pltpu.VMEM((2 * K, ROWS), jnp.int32),
            pltpu.VMEM((ROWS // COLS, K * COLS, COLS), BF16),
            pltpu.VMEM((ROWS // COLS, COLS, COLS), F32),
            pltpu.SemaphoreType.DMA((ROWS // REMAP_ROWS + 1,)),
        ],
        compiler_params=pltpu.CompilerParams(vmem_limit_bytes=32 << 20),
    )(pos, arrived, weights)


def to_peers(payload, axes):
    return lax.all_to_all(payload, axes, split_axis=0, concat_axis=0, tiled=True)


def local(
    layered_heat_profile,
    prior_marine_heat,
    transfer_factor_table,
    depth_fraction_matrix,
    adjacent_cell_table,
    destination_water_peer,
    destination_water_line,
    interpolation_matrix_blocks,
):
    is_atmosphere_side = lax.axis_index("comp") == 0
    own = layered_heat_profile[0]
    block = jax.ShapeDtypeStruct((LEV, ROWS, COLS), F32)
    plane = jax.ShapeDtypeStruct((ROWS, COLS), F32)
    swap = [(0, 1), (1, 0)]

    cross, last, first = cross_kernel(lax.axis_index("comp").reshape(1), own)
    other = lax.ppermute(cross, "comp", [(0, 1), (1, 0)])

    def atmosphere_early():
        packed, pos = atmos_flux(
            destination_water_peer,
            destination_water_line,
            own,
            prior_marine_heat,
            transfer_factor_table,
            interpolation_matrix_blocks,
            depth_fraction_matrix,
        )
        return packed, pos, unused((LEV, COLS), F32), unused((1, LEV, COLS), F32)

    def ocean_early():
        before, after = from_neighbours(last, first)
        packed = unused((RANKS, ATMOS_SLOTS, COLS), BF16)
        return packed, unused((2 * K, ROWS), jnp.int32), before, after[None]

    packed, pos, before, after = lax.cond(is_atmosphere_side, atmosphere_early, ocean_early)
    ocean_rows = (before, after[0])
    edge_shape = jax.ShapeDtypeStruct((len(ORDER), COLS), F32)

    def atmosphere():
        by_chip = (RANKS // CORES, CORES * ATMOS_SLOTS, COLS)
        rows = from_neighbours(*edge_rows(own, other[:1]))
        arrived = to_peers(packed.reshape(by_chip), "gx")
        sides = from_mate(shadow_call(sides_body, plane, [VMEM])(own))
        moved = shadow_call(local_body, block, [VMEM], us=3)(own)
        base, weights = shadow_call(top_base_body, (plane, edge_shape), [VMEM] * 3, us=2)(
            other, from_mate(other), adjacent_cell_table
        )
        *rows, moved, base = lax.optimization_barrier((*rows, moved, base))
        rows = [*rows, *map(from_mate, rows)]
        core = lax.axis_index("gy").reshape(1)
        mine, hits = call(
            push_body,
            (
                jax.ShapeDtypeStruct((CORES, ROWS, COLS), F32),
                jax.ShapeDtypeStruct((CORES, RANKS // CORES * ATMOS_SLOTS, ROWS), BF16),
            ),
            [SMEM, VMEM, VMEM],
        )(core, arrived.reshape(RANKS, ATMOS_SLOTS, COLS), base)
        picked = call(
            pick_body,
            jax.ShapeDtypeStruct((RANKS // CORES, CORES, ATMOS_SLOTS, COLS), BF16),
            [SMEM] + [VMEM] * 9,
        )(core, mine, from_mate(mine), weights, from_mate(weights), *rows, hits)
        returned = to_peers(picked.reshape(by_chip), "gx")
        wide = pltpu.VMEM((LEV, EXTENDED, COLS), F32)
        final = shadow_call(
            substeps_body, block, [VMEM] * 6 + [ANY], scratch_shapes=[wide]
        )(moved, sides, *rows, picked)
        return final, remap(
            pos, returned.reshape(RANKS, ATMOS_SLOTS, COLS), interpolation_matrix_blocks
        )

    def ocean():
        payload = ocean_flux(
            destination_water_peer,
            destination_water_line,
            other,
            prior_marine_heat,
            transfer_factor_table,
            interpolation_matrix_blocks,
        )
        arrived = to_peers(payload.reshape(RANKS, OCEAN_SLOTS * NF, COLS), ("gx", "gy"))
        sides = from_mate(shadow_call(sides_body, plane, [VMEM])(own))
        base = shadow_call(
            ocean_base_body,
            block,
            [VMEM] * 7,
            scratch_shapes=[pltpu.VMEM((len(ORDER), ROWS, COLS), F32)],
        )(own, sides, *ocean_rows, *map(from_mate, ocean_rows), adjacent_cell_table)
        return ocean_sums(
            arrived.reshape(RANKS * OCEAN_SLOTS, NF, COLS), base, depth_fraction_matrix
        )

    state, plane_out = lax.cond(is_atmosphere_side, atmosphere, ocean)
    return state[None], plane_out[None]


def solution(mesh):
    return jax.shard_map(
        local,
        mesh=mesh,
        in_specs=(
            P("comp", None, "gx", "gy"),
            P("gx", "gy"),
            P(None, "gx", "gy"),
            P(),
            P(None, "gx", "gy"),
            P(("gx", "gy"), None),
            P(("gx", "gy"), None),
            P(("gx", "gy"), None, None, None),
        ),
        out_specs=(P("comp", None, "gx", "gy"), P("comp", "gx", "gy")),
        check_vma=False,
    )
```

```python
import functools

import jax
import jax.numpy as jnp
import numpy as np
from jax import lax
from jax.experimental import pallas as pl
from jax.experimental.pallas import tpu as pltpu
from jax.sharding import PartitionSpec as P

ATMOS_DIFFUSION = 0.01
MIXING = 0.2
OCEAN_DIFFUSION = 0.12

RANKS = 64
CAP = 18
CORES = 2
LEV = 8
NF = 8
ROWS = 256
COLS = 128
K = 2
WIDE = 8
OCEAN_SLOTS = 19
ATMOS_SLOTS = 24

VMEM = pl.BlockSpec(memory_space=pltpu.VMEM)
SMEM = pl.BlockSpec(memory_space=pltpu.SMEM)
ANY = pl.BlockSpec(memory_space=pl.ANY)
HBM = pl.BlockSpec(memory_space=pltpu.HBM)
F32 = jnp.float32
BF16 = jnp.bfloat16


def second_table():
    gll_nodes = np.array([-1.0, -1.0 / np.sqrt(5.0), 1.0 / np.sqrt(5.0), 1.0])
    poly_order = 3
    legendre = (5.0 * gll_nodes**3 - 3.0 * gll_nodes) / 2.0
    derivative = np.zeros((4, 4))
    for row_index in range(4):
        for col_index in range(4):
            if row_index != col_index:
                derivative[row_index, col_index] = legendre[row_index] / (
                    legendre[col_index] * (gll_nodes[row_index] - gll_nodes[col_index])
                )
    derivative[0, 0] = -poly_order * (poly_order + 1) / 4.0
    derivative[3, 3] = poly_order * (poly_order + 1) / 4.0
    return derivative @ derivative


SECOND = second_table()


def call(body, out_shape, specs, **params):
    return pl.pallas_call(
        body,
        out_shape=out_shape,
        in_specs=specs,
        out_specs=jax.tree.map(lambda _: VMEM, out_shape),
        compiler_params=pltpu.CompilerParams(vmem_limit_bytes=params.pop("vmem", 24 << 20)),
        **params,
    )


def shadow_call(body, out_shape, specs, us=0, **params):
    cost = pl.CostEstimate(flops=0, bytes_accessed=us * 3_690_000, transcendentals=0)
    return call(body, out_shape, specs, cost_estimate=cost, **params)


def unused(shape, dtype):
    return pl.pallas_call(lambda out_ref: None, out_shape=pltpu.HBM(shape, dtype), out_specs=HBM)()


def route(peer_ref, line_ref, pos_ref, label_ref):
    count = ROWS * K
    peer = jnp.concatenate([peer_ref[k : k + 1, :] for k in range(K)], axis=1)
    line = jnp.concatenate([line_ref[k : k + 1, :] for k in range(K)], axis=1)
    hits = lax.broadcasted_iota(jnp.int32, (RANKS, count), 0) == peer
    hits_f = jnp.where(hits, 1.0, 0.0)
    earlier = lax.broadcasted_iota(jnp.int32, (count, count), 0) < lax.broadcasted_iota(
        jnp.int32, (count, count), 1
    )
    before = jnp.dot(
        hits_f.astype(BF16),
        jnp.where(earlier, 1.0, 0.0).astype(BF16),
        preferred_element_type=F32,
    )
    slot = jnp.sum(hits_f * before, axis=0, keepdims=True).astype(jnp.int32)
    for width, at in ((OCEAN_SLOTS, 0), (ATMOS_SLOTS, K)):
        position = peer * width + slot
        for k in range(K):
            pos_ref[at + k : at + k + 1, :] = position[:, k * ROWS : (k + 1) * ROWS]
    slot_hits = lax.broadcasted_iota(jnp.int32, (COLS, count), 0) == slot
    shifted = jnp.where(hits, (line + 1).astype(F32), 0.0).astype(BF16)
    label_ref[...] = (
        lax.dot_general(
            shifted,
            jnp.where(slot_hits, 1.0, 0.0).astype(BF16),
            (((1,), (1,)), ((), ())),
            preferred_element_type=F32,
        )
        - 1.0
    )


def turned(field, lanes):
    lanes = lanes % COLS
    return field if lanes == 0 else pltpu.roll(field, lanes, 1)


def cross_body(side_ref, own_ref, out_ref, last_ref, first_ref, held, edges, sems):
    copies = [
        pltpu.make_async_copy(own_ref.at[pl.ds(0, 2)], held, sems.at[0]),
        pltpu.make_async_copy(own_ref.at[:, pl.ds(ROWS - WIDE, WIDE)], edges.at[0], sems.at[1]),
        pltpu.make_async_copy(own_ref.at[:, pl.ds(0, WIDE)], edges.at[1], sems.at[2]),
    ]
    for copy in copies:
        copy.start()
    copies[0].wait()
    top = held[0]
    high = top.astype(BF16)
    rest = top - high.astype(F32)
    out_ref[0] = high
    other = MIXING * held[1] + (1.0 - MIXING) * rest
    out_ref[1] = jnp.where(side_ref[0] == 0, rest, other).astype(BF16)
    for copy in copies[1:]:
        copy.wait()
    for l in range(LEV):
        last_ref[l : l + 1, :] = edges[0, l, WIDE - 1 :, :]
        first_ref[l : l + 1, :] = edges[1, l, :1, :]


def cross_kernel(side, own):
    edge = jax.ShapeDtypeStruct((LEV, COLS), F32)
    return call(
        cross_body,
        (jax.ShapeDtypeStruct((2, ROWS, COLS), BF16), edge, edge),
        [SMEM, HBM],
        scratch_shapes=[
            pltpu.VMEM((2, ROWS, COLS), F32),
            pltpu.VMEM((2, LEV, WIDE, COLS), F32),
            pltpu.SemaphoreType.DMA((3,)),
        ],
    )(side, own)


def packed_sides(levels, lane):
    packed = jnp.zeros(lane.shape, F32)
    for l, level in enumerate(levels):
        packed = jnp.where(lane // (2 * WIDE) == l, turned(level, WIDE + 2 * WIDE * l), packed)
    return packed


def sides_body(own_ref, out_ref):
    lane = lax.broadcasted_iota(jnp.int32, (ROWS, COLS), 1)
    out_ref[...] = packed_sides([own_ref[l] for l in range(LEV)], lane)


FLUX_ROWS = 16
REMAP_ROWS = 32
CHUNKS = ROWS // FLUX_ROWS


def weight_copies(source, held, sems, per):
    def copy(c):
        part = pl.ds(c * per, per)
        return pltpu.make_async_copy(source.at[part], held.at[part], sems.at[c])

    return copy


def side_by_side(held, b):
    return jnp.concatenate([held[b, k] for k in range(K)], axis=1)


WEIGHTS_HELD = [
    pltpu.VMEM((ROWS, K, COLS, COLS), BF16),
]
ROUTING = [
    pltpu.VMEM((K, ROWS), jnp.int32),
    pltpu.VMEM((K, ROWS), jnp.int32),
    pltpu.VMEM((RANKS, COLS), F32),
    pltpu.SMEM((2 * K, ROWS), jnp.int32),
]
FIELDS = [
    pltpu.VMEM((ROWS, COLS), F32),
    pltpu.VMEM((NF, ROWS, COLS), F32),
]


def ocean_flux_body(
    peer_ref,
    line_ref,
    air_hbm_ref,
    prior_ref,
    factor_ref,
    w_ref,
    out_ref,
    held,
    peer,
    line,
    label,
    pos,
    prior,
    factor,
    air_ref,
    pos_rows,
    packed,
    rows,
    sems,
):
    copy = weight_copies(w_ref, held, sems, FLUX_ROWS)
    index_copies = [
        pltpu.make_async_copy(peer_ref, peer, sems.at[CHUNKS]),
        pltpu.make_async_copy(line_ref, line, sems.at[CHUNKS + 1]),
    ]
    field_copies = [
        pltpu.make_async_copy(prior_ref, prior, sems.at[CHUNKS + 2]),
        pltpu.make_async_copy(air_hbm_ref, air_ref, sems.at[CHUNKS + 6]),
        pltpu.make_async_copy(factor_ref, factor, sems.at[CHUNKS + 3]),
    ]
    for started in index_copies + field_copies:
        started.start()
    for c in range(CHUNKS):
        copy(c).start()
    packed[...] = jnp.zeros_like(packed)
    for started in index_copies:
        started.wait()
    route(peer, line, pos_rows, label)
    to_scalars = pltpu.make_async_copy(pos_rows, pos, sems.at[CHUNKS + 4])
    to_scalars.start()
    for d in range(RANKS):
        packed[d * OCEAN_SLOTS + CAP] = jnp.broadcast_to(label[d : d + 1, :], (NF, COLS)).astype(
            BF16
        )
    for started in field_copies:
        started.wait()
    difference = air_ref[0].astype(F32) + air_ref[1].astype(F32) - prior[...]
    for f in range(NF):
        rows[pl.ds(f, ROWS, stride=NF), :] = factor[f] * difference
    to_scalars.wait()

    @pl.loop(0, CHUNKS)
    def _(c):
        copy(c).wait()
        for i in range(FLUX_ROWS):
            b = c * FLUX_ROWS + i
            flux = rows[pl.ds(pl.multiple_of(b * NF, NF), NF), :].astype(BF16)
            part = jnp.dot(flux, side_by_side(held, b), preferred_element_type=F32).astype(BF16)
            for k in range(K):
                packed[pos[k, b]] = part[:, k * COLS : (k + 1) * COLS]

    done = pltpu.make_async_copy(packed, out_ref, sems.at[CHUNKS + 5])
    done.start()
    done.wait()


def ocean_flux(peer, line, air, prior, factors, weights):
    return pl.pallas_call(
        ocean_flux_body,
        out_shape=pltpu.HBM((RANKS * OCEAN_SLOTS, NF, COLS), BF16),
        in_specs=[HBM, HBM, ANY, HBM, HBM, HBM],
        out_specs=HBM,
        scratch_shapes=WEIGHTS_HELD
        + ROUTING
        + FIELDS
        + [
            pltpu.VMEM((2, ROWS, COLS), BF16),
            pltpu.VMEM((2 * K, ROWS), jnp.int32),
            pltpu.VMEM((RANKS * OCEAN_SLOTS, NF, COLS), BF16),
            pltpu.VMEM((ROWS * NF, COLS), F32),
            pltpu.SemaphoreType.DMA((CHUNKS + 7,)),
        ],
        compiler_params=pltpu.CompilerParams(vmem_limit_bytes=32 << 20),
    )(peer.T, line.T, air, prior, factors, weights)


def atmos_flux_body(
    peer_ref,
    line_ref,
    own_ref,
    prior_ref,
    factor_ref,
    w_ref,
    share_ref,
    out_ref,
    pos_ref,
    held,
    peer,
    line,
    label,
    pos,
    prior,
    factor,
    air,
    packed,
    rows,
    sems,
):
    copy = weight_copies(w_ref, held, sems, FLUX_ROWS)
    index_copies = [
        pltpu.make_async_copy(peer_ref, peer, sems.at[CHUNKS]),
        pltpu.make_async_copy(line_ref, line, sems.at[CHUNKS + 1]),
    ]
    field_copies = [
        pltpu.make_async_copy(prior_ref, prior, sems.at[CHUNKS + 2]),
        pltpu.make_async_copy(own_ref.at[0], air, sems.at[CHUNKS + 3]),
        pltpu.make_async_copy(factor_ref, factor, sems.at[CHUNKS + 4]),
    ]
    for started in index_copies + field_copies:
        started.start()
    for c in range(CHUNKS):
        copy(c).start()
    packed[...] = jnp.zeros_like(packed)
    rows[...] = jnp.zeros_like(rows)
    for started in index_copies:
        started.wait()
    route(peer, line, pos_ref, label)
    to_scalars = pltpu.make_async_copy(pos_ref, pos, sems.at[CHUNKS + 5])
    to_scalars.start()
    for d in range(RANKS):
        packed[d * ATMOS_SLOTS + CAP : d * ATMOS_SLOTS + CAP + 1, :] = label[d : d + 1, :]
    for started in field_copies:
        started.wait()
    mixed = share_ref[0, 0] * factor[0]
    for f in range(1, NF):
        mixed += share_ref[0, f] * factor[f]
    flux = mixed * (air[...] - prior[...])
    high = flux.astype(BF16).astype(F32)
    rows[pl.ds(0, ROWS, stride=8), :] = high
    rows[pl.ds(1, ROWS, stride=8), :] = flux - high
    to_scalars.wait()

    @pl.loop(0, CHUNKS)
    def _(c):
        copy(c).wait()
        for i in range(FLUX_ROWS):
            b = c * FLUX_ROWS + i
            pair = rows[pl.ds(pl.multiple_of(b * 8, 8), 8), :].astype(BF16)
            part = jnp.dot(pair, side_by_side(held, b), preferred_element_type=F32)
            part = part[0:1, :] + part[1:2, :]
            for k in range(K):
                packed[pl.ds(pos[K + k, b], 1), :] = part[:, k * COLS : (k + 1) * COLS]

    out_ref[...] = packed[...].astype(BF16).reshape(RANKS, ATMOS_SLOTS, COLS)


def atmos_flux(peer, line, own, prior, factors, weights, share):
    return pl.pallas_call(
        atmos_flux_body,
        out_shape=(
            jax.ShapeDtypeStruct((RANKS, ATMOS_SLOTS, COLS), BF16),
            jax.ShapeDtypeStruct((2 * K, ROWS), jnp.int32),
        ),
        in_specs=[HBM, HBM, HBM, HBM, HBM, HBM, SMEM],
        out_specs=(VMEM, VMEM),
        scratch_shapes=WEIGHTS_HELD
        + ROUTING
        + FIELDS
        + [
            pltpu.VMEM((ROWS, COLS), F32),
            pltpu.VMEM((RANKS * ATMOS_SLOTS, COLS), F32),
            pltpu.VMEM((ROWS * 8, COLS), F32),
            pltpu.SemaphoreType.DMA((CHUNKS + 6,)),
        ],
        compiler_params=pltpu.CompilerParams(vmem_limit_bytes=32 << 20),
    )(peer.T, line.T, own, prior, factors, weights, share)


EXTENDED = ROWS + 2 * WIDE


def iotas(rows):
    return (
        lax.broadcasted_iota(jnp.int32, (rows, COLS), 0),
        lax.broadcasted_iota(jnp.int32, (rows, COLS), 1),
    )


def mate_ends(sides, level):
    return turned(sides, -(2 * WIDE * level + WIDE))


def column_left(field, ends, lane):
    return pltpu.roll(jnp.where(lane == COLS - 1, ends, field), 1, 1)


def column_right(field, ends, lane):
    return pltpu.roll(jnp.where(lane == 0, ends, field), COLS - 1, 1)


def second_along(field, axis, index):
    phase = index % 4
    total = None
    for shift in range(-3, 4):
        factor = jnp.zeros(index.shape, F32)
        for p in range(4):
            if 0 <= p + shift < 4:
                factor = jnp.where(phase == p, F32(SECOND[p, p + shift]), factor)
        moved = field if shift == 0 else pltpu.roll(field, (-shift) % field.shape[axis], axis)
        total = factor * moved if total is None else total + factor * moved
    return total


def diffused(field, above, below):
    groups = field.reshape(-1, 8, COLS)
    along = second_along(groups, 1, lax.broadcasted_iota(jnp.int32, (1, 8, COLS), 1))
    along = along.reshape(field.shape)
    along += second_along(field, 1, lax.broadcasted_iota(jnp.int32, (1, COLS), 1))
    return field + ATMOS_DIFFUSION * along + MIXING * (above + below - 2.0 * field)


def assembled(field, axis, phase, ahead, behind):
    return jnp.where(
        phase == 3,
        0.5 * (field + ahead),
        jnp.where(phase == 0, 0.5 * (field + behind), field),
    )


def assembled_rows(field, row):
    ahead = pltpu.roll(field, EXTENDED - 1, 0)
    return assembled(field, 0, row % 4, ahead, pltpu.roll(field, 1, 0))


def diffused_levels(levels):
    return [
        diffused(levels[l], levels[min(l + 1, LEV - 1)], levels[max(l - 1, 0)]) for l in range(LEV)
    ]


def local_body(u_ref, out_ref):
    for l, field in enumerate(diffused_levels([u_ref[l] for l in range(LEV)])):
        out_ref[l] = field


def substeps_body(
    local_ref, sides_ref, before_ref, after_ref, mate_before_ref, mate_after_ref, _, out_ref, main
):
    row, lane = iotas(EXTENDED)
    phase, part = lane % 4, lane % (2 * WIDE)
    edges = [diffused_levels([r[l] for l in range(LEV)]) for r in (before_ref, after_ref)]
    thin = lax.broadcasted_iota(jnp.int32, (WIDE, COLS), 1)
    ends = [
        packed_sides([r[l] for l in range(LEV)], thin) for r in (mate_before_ref, mate_after_ref)
    ]
    sides = jnp.concatenate([ends[0], sides_ref[...], ends[1]], axis=0)
    for substep in range(2):
        over = jnp.where(lane < COLS - 2 * WIDE, turned(sides, -2 * WIDE), sides)
        under = jnp.where(lane >= 2 * WIDE, turned(sides, 2 * WIDE), sides)
        sides = assembled_rows(diffused(sides, over, under), row)
        near = jnp.zeros((EXTENDED, COLS), F32)
        for l in range(LEV):
            if substep == 0:
                half = jnp.concatenate([edges[0][l], local_ref[l], edges[1][l]], axis=0)
            else:
                half = diffused(main[l], main[min(l + 1, LEV - 1)], main[max(l - 1, 0)])
            half = assembled_rows(half, row)
            if substep == 0:
                first = turned(half, 2 * WIDE * l + WIDE - 1)
                last = turned(half, 2 * WIDE * l + WIDE + 1)
                own_level = lane // (2 * WIDE) == l
                near = jnp.where(own_level, jnp.where(part < WIDE, first, last), near)
            ends = mate_ends(sides, l)
            whole = assembled(
                half, 1, phase, column_right(half, ends, lane), column_left(half, ends, lane)
            )
            if substep == 0:
                main[l] = whole
            else:
                out_ref[l] = whole[WIDE : WIDE + ROWS]
        if substep == 0:
            ahead = jnp.where(part == WIDE - 1, near, turned(sides, -1))
            behind = jnp.where(part == WIDE, near, turned(sides, 1))
            sides = assembled(sides, 1, phase, ahead, behind)


ORDER = [(dr, dc) for dr in (-1, 0, 1) for dc in (-1, 0, 1) if dr or dc]


def neighbour_counts(table_ref, row, lane):
    own = (row + 1) * (COLS + 2) + lane + 1
    counts = []
    for dr, dc in ORDER:
        target = own + (dr * (COLS + 2) + dc)
        count = jnp.zeros((ROWS, COLS), F32)
        for e in range(table_ref.shape[0]):
            count += jnp.where(table_ref[e] == target, 1.0, 0.0)
        counts.append(count)
    return counts


def neighbour_spread(field, ends, before, after, ends_before, ends_after, counts, row, lane):
    total = jnp.zeros((ROWS, COLS), F32)
    lines = {
        0: (field, ends),
        -1: tuple(
            jnp.where(row == 0, edge, pltpu.roll(v, 1, 0))
            for v, edge in ((field, before), (ends, ends_before))
        ),
        1: tuple(
            jnp.where(row == ROWS - 1, edge, pltpu.roll(v, ROWS - 1, 0))
            for v, edge in ((field, after), (ends, ends_after))
        ),
    }
    for (dr, dc), count in zip(ORDER, counts):
        line, line_ends = lines[dr]
        if dc == -1:
            line = column_left(line, line_ends, lane)
        elif dc == 1:
            line = column_right(line, line_ends, lane)
        total += count * (line - field)
    return total


def edge_weights(counts, weight_ref):
    weight_ref[...] = jnp.zeros_like(weight_ref)
    for n, (dr, _) in enumerate(ORDER):
        if dr:
            edge = 0 if dr < 0 else ROWS - 1
            weight_ref[n : n + 1, :] = counts[n][edge : edge + 1, :]


def top_base_body(other_ref, mate_ref, table_ref, out_ref, weight_ref):
    row, lane = iotas(ROWS)
    top = other_ref[0].astype(F32)
    counts = neighbour_counts(table_ref, row, lane)
    none = jnp.zeros((1, COLS), F32)
    spread = neighbour_spread(
        top, mate_ref[0].astype(F32), none, none, none, none, counts, row, lane
    )
    out_ref[...] = (1.0 - MIXING) * top + other_ref[1].astype(F32) + OCEAN_DIFFUSION * spread
    edge_weights(counts, weight_ref)


def edge_terms(line, ends, weights):
    lane = lax.broadcasted_iota(jnp.int32, (1, COLS), 1)
    total = weights[0] * column_left(line, ends, lane) + weights[1] * line
    return OCEAN_DIFFUSION * (total + weights[2] * column_right(line, ends, lane))


def both_edges(before, before_ends, after, after_ends, weight_ref):
    weights = [weight_ref[n : n + 1, :] for n in range(len(ORDER))]
    return edge_terms(before, before_ends, weights[:3]), edge_terms(after, after_ends, weights[5:])


def ocean_base_body(
    o_ref,
    sides_ref,
    before_ref,
    after_ref,
    mate_before_ref,
    mate_after_ref,
    table_ref,
    out_ref,
    counts_ref,
):
    row, lane = iotas(ROWS)
    for n, count in enumerate(neighbour_counts(table_ref, row, lane)):
        counts_ref[n] = count
    for l in range(LEV):
        field = o_ref[l]
        spread = neighbour_spread(
            field,
            mate_ends(sides_ref[...], l),
            before_ref[l : l + 1, :],
            after_ref[l : l + 1, :],
            mate_before_ref[l : l + 1, :],
            mate_after_ref[l : l + 1, :],
            [counts_ref[n] for n in range(len(ORDER))],
            row,
            lane,
        )
        below, above = o_ref[max(l - 1, 0)], o_ref[min(l + 1, LEV - 1)]
        out_ref[l] = field + OCEAN_DIFFUSION * spread + MIXING * (above + below - 2.0 * field)


def edge_rows(*fields):
    last = [v[..., ROWS - WIDE :, :].reshape(-1, WIDE, COLS).astype(F32) for v in fields]
    first = [v[..., :WIDE, :].reshape(-1, WIDE, COLS).astype(F32) for v in fields]
    return jnp.concatenate(last, axis=0), jnp.concatenate(first, axis=0)


def from_neighbours(last, first):
    size = lax.axis_size("gx")
    up = [(i, (i + 1) % size) for i in range(size)]
    down = [(j, i) for i, j in up]
    return lax.ppermute(last, "gx", up), lax.ppermute(first, "gx", down)


def from_mate(field):
    return lax.ppermute(field, "gy", [(0, 1), (1, 0)])


def row_hits(labels):
    blocks, width = labels.shape[0], ATMOS_SLOTS
    shape = (blocks, width, COLS)
    diagonal = lax.broadcasted_iota(jnp.int32, shape, 1) == lax.broadcasted_iota(jnp.int32, shape, 2)
    spread = jnp.where(diagonal, labels[:, None, :], 0.0)
    column = jnp.sum(spread, axis=2, keepdims=True).reshape(blocks * width, 1)
    slot = lax.broadcasted_iota(jnp.int32, (blocks, width, 1), 1).reshape(blocks * width, 1)
    column = jnp.where(slot < CAP, column, -1.0).astype(jnp.int32)
    rows = lax.broadcasted_iota(jnp.int32, (blocks * width, ROWS), 1)
    return jnp.where(column == rows, 1.0, 0.0).astype(BF16)


def push_body(core_ref, arrived_ref, base_ref, out_ref, hits_ref):
    blocks = RANKS // CORES
    arrived = arrived_ref[...].astype(F32).reshape(blocks, CORES, ATMOS_SLOTS, COLS)
    for core in range(CORES):
        part = arrived[:, core]
        hits = row_hits(part[:, CAP, :])
        hits_ref[core] = hits
        values = part.reshape(blocks * ATMOS_SLOTS, COLS).astype(BF16)
        pushed = lax.dot_general(
            hits, values, (((0,), (0,)), ((), ())), preferred_element_type=F32
        )
        out_ref[core] = pushed + jnp.where(core_ref[0] == core, base_ref[...], 0.0)


def pick_body(
    core_ref,
    mine_ref,
    mate_ref,
    weight_ref,
    mate_weight_ref,
    before_ref,
    after_ref,
    mate_before_ref,
    mate_after_ref,
    hits_ref,
    out_ref,
):
    blocks = RANKS // CORES
    row = lax.broadcasted_iota(jnp.int32, (ROWS, COLS), 0)
    own_rows = [before_ref[LEV, WIDE - 1 :, :], after_ref[LEV, :1, :]]
    mate_rows = [mate_before_ref[LEV, WIDE - 1 :, :], mate_after_ref[LEV, :1, :]]
    own = both_edges(own_rows[0], mate_rows[0], own_rows[1], mate_rows[1], weight_ref)
    mate = both_edges(mate_rows[0], own_rows[0], mate_rows[1], own_rows[1], mate_weight_ref)
    for core in range(CORES):
        above, below = (jnp.where(core_ref[0] == core, o, m) for o, m in zip(own, mate))
        top = mine_ref[core] + mate_ref[core]
        top += jnp.where(row == 0, above, 0.0) + jnp.where(row == ROWS - 1, below, 0.0)
        picked = jnp.dot(hits_ref[core], top.astype(BF16), preferred_element_type=F32)
        out_ref[:, core] = picked.astype(BF16).reshape(blocks, ATMOS_SLOTS, COLS)


def sums_body(arrived_ref, base_ref, share_ref, out_ref, first_ref, wide):
    width = OCEAN_SLOTS * NF
    wide[...] = arrived_ref[...].astype(F32).reshape(RANKS * width, COLS)
    labels = wide[pl.ds(CAP * NF, RANKS, stride=width), :]
    by_slot = jnp.concatenate([labels, labels], axis=0).T
    row = lax.broadcasted_iota(jnp.int32, (ROWS, COLS), 0).astype(F32)
    lane = lax.broadcasted_iota(jnp.int32, (1, COLS), 1)
    pieces = []
    for s in range(0, CAP, 2):
        pair = jnp.where(lane < RANKS, by_slot[s : s + 1, :], by_slot[s + 1 : s + 2, :])
        pieces.append(jnp.where(row == pair, 1.0, 0.0).astype(BF16))
    hits = jnp.concatenate(pieces, axis=1)
    forcing = []
    for f in range(0, NF, 2):
        values = [
            jnp.concatenate(
                [wide[pl.ds(s * NF + g, RANKS, stride=width), :] for s in range(CAP)], axis=0
            )
            for g in (f, f + 1)
        ]
        both = jnp.concatenate(values, axis=1).astype(BF16)
        summed = jnp.dot(hits, both, preferred_element_type=F32)
        forcing += [summed[:, :COLS], summed[:, COLS:]]
    first_ref[...] = forcing[0]
    for begin in range(0, ROWS, 32):
        part = slice(begin, begin + 32)
        near = [v[part] for v in forcing]
        for l in range(LEV):
            level = base_ref[l, part, :]
            for f in range(NF):
                level += share_ref[l, f] * near[f]
            out_ref[l, part, :] = level


def ocean_sums(arrived, base, share):
    return pl.pallas_call(
        sums_body,
        out_shape=(
            jax.ShapeDtypeStruct((LEV, ROWS, COLS), F32),
            jax.ShapeDtypeStruct((ROWS, COLS), F32),
        ),
        in_specs=[VMEM, VMEM, SMEM],
        out_specs=(VMEM, VMEM),
        scratch_shapes=[pltpu.VMEM((RANKS * OCEAN_SLOTS * NF, COLS), F32)],
        compiler_params=pltpu.CompilerParams(vmem_limit_bytes=24 << 20),
    )(arrived, base, share)


def remap_body(pos_hbm_ref, arrived_ref, w_ref, out_ref, held, pos_ref, values, own, sems):
    pos_copy = pltpu.make_async_copy(pos_hbm_ref, pos_ref, sems.at[ROWS // REMAP_ROWS])
    pos_copy.start()
    copy = weight_copies(w_ref, held, sems, REMAP_ROWS)
    for c in range(ROWS // REMAP_ROWS):
        copy(c).start()
    slots = RANKS * ATMOS_SLOTS
    by_column = arrived_ref[...].astype(F32).reshape(slots, COLS).T.astype(BF16)
    at = lax.broadcasted_iota(jnp.int32, (slots, ROWS), 0)
    groups = ROWS // COLS
    pos_copy.wait()
    for k in range(K):
        hits = jnp.where(at == pos_ref[K + k : K + k + 1, :], 1.0, 0.0).astype(BF16)
        found = jnp.dot(by_column, hits, preferred_element_type=F32).astype(BF16)
        for g in range(groups):
            values[g, k * COLS : (k + 1) * COLS, :] = found[:, g * COLS : (g + 1) * COLS]
    lane = lax.broadcasted_iota(jnp.int32, (COLS, COLS), 1)
    parts = COLS // REMAP_ROWS

    @pl.loop(0, ROWS // REMAP_ROWS)
    def _(c):
        copy(c).wait()
        block = held.at[pl.ds(c * REMAP_ROWS, REMAP_ROWS)]
        tiles = jnp.concatenate(
            [block[:, k].reshape(REMAP_ROWS * COLS, COLS) for k in range(K)], axis=1
        )
        crossed = jnp.dot(tiles, values[c // parts], preferred_element_type=F32)
        kept = own[c // parts]
        for i in range(REMAP_ROWS):
            mine = lane == (c % parts) * REMAP_ROWS + i
            kept = jnp.where(mine, crossed[i * COLS : (i + 1) * COLS], kept)
        own[c // parts] = kept

    for g in range(groups):
        out_ref[g * COLS : (g + 1) * COLS, :] = own[g].T


def remap(pos, arrived, weights):
    return pl.pallas_call(
        remap_body,
        out_shape=jax.ShapeDtypeStruct((ROWS, COLS), F32),
        in_specs=[ANY, VMEM, HBM],
        out_specs=VMEM,
        scratch_shapes=WEIGHTS_HELD
        + [
            pltpu.VMEM((2 * K, ROWS), jnp.int32),
            pltpu.VMEM((ROWS // COLS, K * COLS, COLS), BF16),
            pltpu.VMEM((ROWS // COLS, COLS, COLS), F32),
            pltpu.SemaphoreType.DMA((ROWS // REMAP_ROWS + 1,)),
        ],
        compiler_params=pltpu.CompilerParams(vmem_limit_bytes=32 << 20),
    )(pos, arrived, weights)


def to_peers(payload, axes):
    return lax.all_to_all(payload, axes, split_axis=0, concat_axis=0, tiled=True)


def local(
    layered_heat_profile,
    prior_marine_heat,
    transfer_factor_table,
    depth_fraction_matrix,
    adjacent_cell_table,
    destination_water_peer,
    destination_water_line,
    interpolation_matrix_blocks,
):
    is_atmosphere_side = lax.axis_index("comp") == 0
    own = layered_heat_profile[0]
    block = jax.ShapeDtypeStruct((LEV, ROWS, COLS), F32)
    plane = jax.ShapeDtypeStruct((ROWS, COLS), F32)
    swap = [(0, 1), (1, 0)]

    cross, last, first = cross_kernel(lax.axis_index("comp").reshape(1), own)
    other = lax.ppermute(cross, "comp", [(0, 1), (1, 0)])

    def atmosphere_early():
        packed, pos = atmos_flux(
            destination_water_peer,
            destination_water_line,
            own,
            prior_marine_heat,
            transfer_factor_table,
            interpolation_matrix_blocks,
            depth_fraction_matrix,
        )
        return packed, pos, unused((LEV, COLS), F32), unused((1, LEV, COLS), F32)

    def ocean_early():
        before, after = from_neighbours(last, first)
        packed = unused((RANKS, ATMOS_SLOTS, COLS), BF16)
        return packed, unused((2 * K, ROWS), jnp.int32), before, after[None]

    packed, pos, before, after = lax.cond(is_atmosphere_side, atmosphere_early, ocean_early)
    ocean_rows = (before, after[0])
    edge_shape = jax.ShapeDtypeStruct((len(ORDER), COLS), F32)

    def atmosphere():
        by_chip = (RANKS // CORES, CORES * ATMOS_SLOTS, COLS)
        *edges, later = lax.optimization_barrier((*edge_rows(own, other[:1]), other))
        rows = from_neighbours(*edges)
        arrived = to_peers(packed.reshape(by_chip), "gx")
        sides = from_mate(shadow_call(sides_body, plane, [VMEM])(own))
        moved = shadow_call(local_body, block, [VMEM], us=3)(own)
        base, weights = shadow_call(top_base_body, (plane, edge_shape), [VMEM] * 3, us=2)(
            other, from_mate(later), adjacent_cell_table
        )
        *rows, moved, base = lax.optimization_barrier((*rows, moved, base))
        rows = [*rows, *map(from_mate, rows)]
        core = lax.axis_index("gy").reshape(1)
        mine, hits = call(
            push_body,
            (
                jax.ShapeDtypeStruct((CORES, ROWS, COLS), F32),
                jax.ShapeDtypeStruct((CORES, RANKS // CORES * ATMOS_SLOTS, ROWS), BF16),
            ),
            [SMEM, VMEM, VMEM],
        )(core, arrived.reshape(RANKS, ATMOS_SLOTS, COLS), base)
        picked = call(
            pick_body,
            jax.ShapeDtypeStruct((RANKS // CORES, CORES, ATMOS_SLOTS, COLS), BF16),
            [SMEM] + [VMEM] * 9,
        )(core, mine, from_mate(mine), weights, from_mate(weights), *rows, hits)
        returned = to_peers(picked.reshape(by_chip), "gx")
        wide = pltpu.VMEM((LEV, EXTENDED, COLS), F32)
        final = shadow_call(
            substeps_body, block, [VMEM] * 6 + [ANY], scratch_shapes=[wide]
        )(moved, sides, *rows, picked)
        return final, remap(
            pos, returned.reshape(RANKS, ATMOS_SLOTS, COLS), interpolation_matrix_blocks
        )

    def ocean():
        payload = ocean_flux(
            destination_water_peer,
            destination_water_line,
            other,
            prior_marine_heat,
            transfer_factor_table,
            interpolation_matrix_blocks,
        )
        arrived = to_peers(payload.reshape(RANKS, OCEAN_SLOTS * NF, COLS), ("gx", "gy"))
        sides = from_mate(shadow_call(sides_body, plane, [VMEM])(own))
        base = shadow_call(
            ocean_base_body,
            block,
            [VMEM] * 7,
            scratch_shapes=[pltpu.VMEM((len(ORDER), ROWS, COLS), F32)],
        )(own, sides, *ocean_rows, *map(from_mate, ocean_rows), adjacent_cell_table)
        return ocean_sums(
            arrived.reshape(RANKS * OCEAN_SLOTS, NF, COLS), base, depth_fraction_matrix
        )

    state, plane_out = lax.cond(is_atmosphere_side, atmosphere, ocean)
    return state[None], plane_out[None]


def solution(mesh):
    return jax.shard_map(
        local,
        mesh=mesh,
        in_specs=(
            P("comp", None, "gx", "gy"),
            P("gx", "gy"),
            P(None, "gx", "gy"),
            P(),
            P(None, "gx", "gy"),
            P(("gx", "gy"), None),
            P(("gx", "gy"), None),
            P(("gx", "gy"), None, None, None),
        ),
        out_specs=(P("comp", None, "gx", "gy"), P("comp", "gx", "gy")),
        check_vma=False,
    )
```

```python
import functools

import jax
import jax.numpy as jnp
import numpy as np
from jax import lax
from jax.experimental import pallas as pl
from jax.experimental.pallas import tpu as pltpu
from jax.sharding import PartitionSpec as P

ATMOS_DIFFUSION = 0.01
MIXING = 0.2
OCEAN_DIFFUSION = 0.12

RANKS = 64
CAP = 18
CORES = 2
LEV = 8
NF = 8
ROWS = 256
COLS = 128
K = 2
WIDE = 8
OCEAN_SLOTS = 19
ATMOS_SLOTS = 24

VMEM = pl.BlockSpec(memory_space=pltpu.VMEM)
SMEM = pl.BlockSpec(memory_space=pltpu.SMEM)
ANY = pl.BlockSpec(memory_space=pl.ANY)
HBM = pl.BlockSpec(memory_space=pltpu.HBM)
F32 = jnp.float32
BF16 = jnp.bfloat16


def second_table():
    gll_nodes = np.array([-1.0, -1.0 / np.sqrt(5.0), 1.0 / np.sqrt(5.0), 1.0])
    poly_order = 3
    legendre = (5.0 * gll_nodes**3 - 3.0 * gll_nodes) / 2.0
    derivative = np.zeros((4, 4))
    for row_index in range(4):
        for col_index in range(4):
            if row_index != col_index:
                derivative[row_index, col_index] = legendre[row_index] / (
                    legendre[col_index] * (gll_nodes[row_index] - gll_nodes[col_index])
                )
    derivative[0, 0] = -poly_order * (poly_order + 1) / 4.0
    derivative[3, 3] = poly_order * (poly_order + 1) / 4.0
    return derivative @ derivative


SECOND = second_table()


def call(body, out_shape, specs, **params):
    return pl.pallas_call(
        body,
        out_shape=out_shape,
        in_specs=specs,
        out_specs=jax.tree.map(lambda _: VMEM, out_shape),
        compiler_params=pltpu.CompilerParams(vmem_limit_bytes=params.pop("vmem", 24 << 20)),
        **params,
    )


def shadow_call(body, out_shape, specs, us=0, **params):
    cost = pl.CostEstimate(flops=0, bytes_accessed=us * 3_690_000, transcendentals=0)
    return call(body, out_shape, specs, cost_estimate=cost, **params)


def unused(shape, dtype):
    return pl.pallas_call(lambda out_ref: None, out_shape=pltpu.HBM(shape, dtype), out_specs=HBM)()


def route(peer_ref, line_ref, pos_ref, label_ref):
    count = ROWS * K
    peer = jnp.concatenate([peer_ref[k : k + 1, :] for k in range(K)], axis=1)
    line = jnp.concatenate([line_ref[k : k + 1, :] for k in range(K)], axis=1)
    hits = lax.broadcasted_iota(jnp.int32, (RANKS, count), 0) == peer
    hits_f = jnp.where(hits, 1.0, 0.0)
    earlier = lax.broadcasted_iota(jnp.int32, (count, count), 0) < lax.broadcasted_iota(
        jnp.int32, (count, count), 1
    )
    before = jnp.dot(
        hits_f.astype(BF16),
        jnp.where(earlier, 1.0, 0.0).astype(BF16),
        preferred_element_type=F32,
    )
    slot = jnp.sum(hits_f * before, axis=0, keepdims=True).astype(jnp.int32)
    for width, at in ((OCEAN_SLOTS, 0), (ATMOS_SLOTS, K)):
        position = peer * width + slot
        for k in range(K):
            pos_ref[at + k : at + k + 1, :] = position[:, k * ROWS : (k + 1) * ROWS]
    slot_hits = lax.broadcasted_iota(jnp.int32, (COLS, count), 0) == slot
    shifted = jnp.where(hits, (line + 1).astype(F32), 0.0).astype(BF16)
    label_ref[...] = (
        lax.dot_general(
            shifted,
            jnp.where(slot_hits, 1.0, 0.0).astype(BF16),
            (((1,), (1,)), ((), ())),
            preferred_element_type=F32,
        )
        - 1.0
    )


def turned(field, lanes):
    lanes = lanes % COLS
    return field if lanes == 0 else pltpu.roll(field, lanes, 1)


def cross_body(side_ref, own_ref, out_ref, last_ref, first_ref, held, edges, sems):
    copies = [
        pltpu.make_async_copy(own_ref.at[pl.ds(0, 2)], held, sems.at[0]),
        pltpu.make_async_copy(own_ref.at[:, pl.ds(ROWS - WIDE, WIDE)], edges.at[0], sems.at[1]),
        pltpu.make_async_copy(own_ref.at[:, pl.ds(0, WIDE)], edges.at[1], sems.at[2]),
    ]
    for copy in copies:
        copy.start()
    copies[0].wait()
    top = held[0]
    high = top.astype(BF16)
    rest = top - high.astype(F32)
    out_ref[0] = high
    other = MIXING * held[1] + (1.0 - MIXING) * rest
    out_ref[1] = jnp.where(side_ref[0] == 0, rest, other).astype(BF16)
    for copy in copies[1:]:
        copy.wait()
    for l in range(LEV):
        last_ref[l : l + 1, :] = edges[0, l, WIDE - 1 :, :]
        first_ref[l : l + 1, :] = edges[1, l, :1, :]


def cross_kernel(side, own):
    edge = jax.ShapeDtypeStruct((LEV, COLS), F32)
    return call(
        cross_body,
        (jax.ShapeDtypeStruct((2, ROWS, COLS), BF16), edge, edge),
        [SMEM, HBM],
        scratch_shapes=[
            pltpu.VMEM((2, ROWS, COLS), F32),
            pltpu.VMEM((2, LEV, WIDE, COLS), F32),
            pltpu.SemaphoreType.DMA((3,)),
        ],
    )(side, own)


def packed_sides(levels, lane):
    packed = jnp.zeros(lane.shape, F32)
    for l, level in enumerate(levels):
        packed = jnp.where(lane // (2 * WIDE) == l, turned(level, WIDE + 2 * WIDE * l), packed)
    return packed


def sides_body(own_ref, out_ref):
    lane = lax.broadcasted_iota(jnp.int32, (ROWS, COLS), 1)
    out_ref[...] = packed_sides([own_ref[l] for l in range(LEV)], lane)


FLUX_ROWS = 16
REMAP_ROWS = 32
CHUNKS = ROWS // FLUX_ROWS


def weight_copies(source, held, sems, per):
    def copy(c):
        part = pl.ds(c * per, per)
        return pltpu.make_async_copy(source.at[part], held.at[part], sems.at[c])

    return copy


def side_by_side(held, b):
    return jnp.concatenate([held[b, k] for k in range(K)], axis=1)


WEIGHTS_HELD = [
    pltpu.VMEM((ROWS, K, COLS, COLS), BF16),
]
ROUTING = [
    pltpu.VMEM((K, ROWS), jnp.int32),
    pltpu.VMEM((K, ROWS), jnp.int32),
    pltpu.VMEM((RANKS, COLS), F32),
    pltpu.SMEM((2 * K, ROWS), jnp.int32),
]
FIELDS = [
    pltpu.VMEM((ROWS, COLS), F32),
    pltpu.VMEM((NF, ROWS, COLS), F32),
]


def ocean_flux_body(
    peer_ref,
    line_ref,
    air_hbm_ref,
    prior_ref,
    factor_ref,
    w_ref,
    out_ref,
    held,
    peer,
    line,
    label,
    pos,
    prior,
    factor,
    air_ref,
    pos_rows,
    packed,
    rows,
    sems,
):
    copy = weight_copies(w_ref, held, sems, FLUX_ROWS)
    index_copies = [
        pltpu.make_async_copy(peer_ref, peer, sems.at[CHUNKS]),
        pltpu.make_async_copy(line_ref, line, sems.at[CHUNKS + 1]),
    ]
    field_copies = [
        pltpu.make_async_copy(prior_ref, prior, sems.at[CHUNKS + 2]),
        pltpu.make_async_copy(air_hbm_ref, air_ref, sems.at[CHUNKS + 6]),
        pltpu.make_async_copy(factor_ref, factor, sems.at[CHUNKS + 3]),
    ]
    for started in index_copies + field_copies:
        started.start()
    for c in range(CHUNKS):
        copy(c).start()
    packed[...] = jnp.zeros_like(packed)
    for started in index_copies:
        started.wait()
    route(peer, line, pos_rows, label)
    to_scalars = pltpu.make_async_copy(pos_rows, pos, sems.at[CHUNKS + 4])
    to_scalars.start()
    for d in range(RANKS):
        packed[d * OCEAN_SLOTS + CAP] = jnp.broadcast_to(label[d : d + 1, :], (NF, COLS)).astype(
            BF16
        )
    for started in field_copies:
        started.wait()
    difference = air_ref[0].astype(F32) + air_ref[1].astype(F32) - prior[...]
    for f in range(NF):
        rows[pl.ds(f, ROWS, stride=NF), :] = factor[f] * difference
    to_scalars.wait()

    @pl.loop(0, CHUNKS)
    def _(c):
        copy(c).wait()
        for i in range(FLUX_ROWS):
            b = c * FLUX_ROWS + i
            flux = rows[pl.ds(pl.multiple_of(b * NF, NF), NF), :].astype(BF16)
            part = jnp.dot(flux, side_by_side(held, b), preferred_element_type=F32).astype(BF16)
            for k in range(K):
                packed[pos[k, b]] = part[:, k * COLS : (k + 1) * COLS]

    done = pltpu.make_async_copy(packed, out_ref, sems.at[CHUNKS + 5])
    done.start()
    done.wait()


def ocean_flux(peer, line, air, prior, factors, weights):
    return pl.pallas_call(
        ocean_flux_body,
        out_shape=pltpu.HBM((RANKS * OCEAN_SLOTS, NF, COLS), BF16),
        in_specs=[HBM, HBM, ANY, HBM, HBM, HBM],
        out_specs=HBM,
        scratch_shapes=WEIGHTS_HELD
        + ROUTING
        + FIELDS
        + [
            pltpu.VMEM((2, ROWS, COLS), BF16),
            pltpu.VMEM((2 * K, ROWS), jnp.int32),
            pltpu.VMEM((RANKS * OCEAN_SLOTS, NF, COLS), BF16),
            pltpu.VMEM((ROWS * NF, COLS), F32),
            pltpu.SemaphoreType.DMA((CHUNKS + 7,)),
        ],
        compiler_params=pltpu.CompilerParams(vmem_limit_bytes=32 << 20),
    )(peer.T, line.T, air, prior, factors, weights)


def atmos_flux_body(
    peer_ref,
    line_ref,
    own_ref,
    prior_ref,
    factor_ref,
    w_ref,
    share_ref,
    out_ref,
    pos_ref,
    held,
    peer,
    line,
    label,
    pos,
    prior,
    factor,
    air,
    packed,
    rows,
    sems,
):
    copy = weight_copies(w_ref, held, sems, FLUX_ROWS)
    index_copies = [
        pltpu.make_async_copy(peer_ref, peer, sems.at[CHUNKS]),
        pltpu.make_async_copy(line_ref, line, sems.at[CHUNKS + 1]),
    ]
    field_copies = [
        pltpu.make_async_copy(prior_ref, prior, sems.at[CHUNKS + 2]),
        pltpu.make_async_copy(own_ref.at[0], air, sems.at[CHUNKS + 3]),
        pltpu.make_async_copy(factor_ref, factor, sems.at[CHUNKS + 4]),
    ]
    for started in index_copies + field_copies:
        started.start()
    for c in range(CHUNKS):
        copy(c).start()
    packed[...] = jnp.zeros_like(packed)
    rows[...] = jnp.zeros_like(rows)
    for started in index_copies:
        started.wait()
    route(peer, line, pos_ref, label)
    to_scalars = pltpu.make_async_copy(pos_ref, pos, sems.at[CHUNKS + 5])
    to_scalars.start()
    for d in range(RANKS):
        packed[d * ATMOS_SLOTS + CAP : d * ATMOS_SLOTS + CAP + 1, :] = label[d : d + 1, :]
    for started in field_copies:
        started.wait()
    mixed = share_ref[0, 0] * factor[0]
    for f in range(1, NF):
        mixed += share_ref[0, f] * factor[f]
    flux = mixed * (air[...] - prior[...])
    high = flux.astype(BF16).astype(F32)
    rows[pl.ds(0, ROWS, stride=8), :] = high
    rows[pl.ds(1, ROWS, stride=8), :] = flux - high
    to_scalars.wait()

    @pl.loop(0, CHUNKS)
    def _(c):
        copy(c).wait()
        for i in range(FLUX_ROWS):
            b = c * FLUX_ROWS + i
            pair = rows[pl.ds(pl.multiple_of(b * 8, 8), 8), :].astype(BF16)
            part = jnp.dot(pair, side_by_side(held, b), preferred_element_type=F32)
            part = part[0:1, :] + part[1:2, :]
            for k in range(K):
                packed[pl.ds(pos[K + k, b], 1), :] = part[:, k * COLS : (k + 1) * COLS]

    out_ref[...] = packed[...].astype(BF16).reshape(RANKS, ATMOS_SLOTS, COLS)


def atmos_flux(peer, line, own, prior, factors, weights, share):
    return pl.pallas_call(
        atmos_flux_body,
        out_shape=(
            jax.ShapeDtypeStruct((RANKS, ATMOS_SLOTS, COLS), BF16),
            jax.ShapeDtypeStruct((2 * K, ROWS), jnp.int32),
        ),
        in_specs=[HBM, HBM, HBM, HBM, HBM, HBM, SMEM],
        out_specs=(VMEM, VMEM),
        scratch_shapes=WEIGHTS_HELD
        + ROUTING
        + FIELDS
        + [
            pltpu.VMEM((ROWS, COLS), F32),
            pltpu.VMEM((RANKS * ATMOS_SLOTS, COLS), F32),
            pltpu.VMEM((ROWS * 8, COLS), F32),
            pltpu.SemaphoreType.DMA((CHUNKS + 6,)),
        ],
        compiler_params=pltpu.CompilerParams(vmem_limit_bytes=32 << 20),
    )(peer.T, line.T, own, prior, factors, weights, share)


EXTENDED = ROWS + 2 * WIDE


def iotas(rows):
    return (
        lax.broadcasted_iota(jnp.int32, (rows, COLS), 0),
        lax.broadcasted_iota(jnp.int32, (rows, COLS), 1),
    )


def mate_ends(sides, level):
    return turned(sides, -(2 * WIDE * level + WIDE))


def column_left(field, ends, lane):
    return pltpu.roll(jnp.where(lane == COLS - 1, ends, field), 1, 1)


def column_right(field, ends, lane):
    return pltpu.roll(jnp.where(lane == 0, ends, field), COLS - 1, 1)


def second_along(field, axis, index):
    phase = index % 4
    total = None
    for shift in range(-3, 4):
        factor = jnp.zeros(index.shape, F32)
        for p in range(4):
            if 0 <= p + shift < 4:
                factor = jnp.where(phase == p, F32(SECOND[p, p + shift]), factor)
        moved = field if shift == 0 else pltpu.roll(field, (-shift) % field.shape[axis], axis)
        total = factor * moved if total is None else total + factor * moved
    return total


def diffused(field, above, below):
    groups = field.reshape(-1, 8, COLS)
    along = second_along(groups, 1, lax.broadcasted_iota(jnp.int32, (1, 8, COLS), 1))
    along = along.reshape(field.shape)
    along += second_along(field, 1, lax.broadcasted_iota(jnp.int32, (1, COLS), 1))
    return field + ATMOS_DIFFUSION * along + MIXING * (above + below - 2.0 * field)


def assembled(field, axis, phase, ahead, behind):
    return jnp.where(
        phase == 3,
        0.5 * (field + ahead),
        jnp.where(phase == 0, 0.5 * (field + behind), field),
    )


def assembled_rows(field, row):
    ahead = pltpu.roll(field, EXTENDED - 1, 0)
    return assembled(field, 0, row % 4, ahead, pltpu.roll(field, 1, 0))


def diffused_levels(levels):
    return [
        diffused(levels[l], levels[min(l + 1, LEV - 1)], levels[max(l - 1, 0)]) for l in range(LEV)
    ]


def local_body(u_ref, out_ref):
    for l, field in enumerate(diffused_levels([u_ref[l] for l in range(LEV)])):
        out_ref[l] = field


def substeps_body(
    local_ref, sides_ref, before_ref, after_ref, mate_before_ref, mate_after_ref, _, out_ref, main
):
    row, lane = iotas(EXTENDED)
    phase, part = lane % 4, lane % (2 * WIDE)
    edges = [diffused_levels([r[l] for l in range(LEV)]) for r in (before_ref, after_ref)]
    thin = lax.broadcasted_iota(jnp.int32, (WIDE, COLS), 1)
    ends = [
        packed_sides([r[l] for l in range(LEV)], thin) for r in (mate_before_ref, mate_after_ref)
    ]
    sides = jnp.concatenate([ends[0], sides_ref[...], ends[1]], axis=0)
    for substep in range(2):
        over = jnp.where(lane < COLS - 2 * WIDE, turned(sides, -2 * WIDE), sides)
        under = jnp.where(lane >= 2 * WIDE, turned(sides, 2 * WIDE), sides)
        sides = assembled_rows(diffused(sides, over, under), row)
        near = jnp.zeros((EXTENDED, COLS), F32)
        for l in range(LEV):
            if substep == 0:
                half = jnp.concatenate([edges[0][l], local_ref[l], edges[1][l]], axis=0)
            else:
                half = diffused(main[l], main[min(l + 1, LEV - 1)], main[max(l - 1, 0)])
            half = assembled_rows(half, row)
            if substep == 0:
                first = turned(half, 2 * WIDE * l + WIDE - 1)
                last = turned(half, 2 * WIDE * l + WIDE + 1)
                own_level = lane // (2 * WIDE) == l
                near = jnp.where(own_level, jnp.where(part < WIDE, first, last), near)
            ends = mate_ends(sides, l)
            whole = assembled(
                half, 1, phase, column_right(half, ends, lane), column_left(half, ends, lane)
            )
            if substep == 0:
                main[l] = whole
            else:
                out_ref[l] = whole[WIDE : WIDE + ROWS]
        if substep == 0:
            ahead = jnp.where(part == WIDE - 1, near, turned(sides, -1))
            behind = jnp.where(part == WIDE, near, turned(sides, 1))
            sides = assembled(sides, 1, phase, ahead, behind)


ORDER = [(dr, dc) for dr in (-1, 0, 1) for dc in (-1, 0, 1) if dr or dc]


def neighbour_counts(table_ref, row, lane):
    own = (row + 1) * (COLS + 2) + lane + 1
    counts = []
    for dr, dc in ORDER:
        target = own + (dr * (COLS + 2) + dc)
        count = jnp.zeros((ROWS, COLS), F32)
        for e in range(table_ref.shape[0]):
            count += jnp.where(table_ref[e] == target, 1.0, 0.0)
        counts.append(count)
    return counts


def neighbour_spread(field, ends, before, after, ends_before, ends_after, counts, row, lane):
    total = jnp.zeros((ROWS, COLS), F32)
    lines = {
        0: (field, ends),
        -1: tuple(
            jnp.where(row == 0, edge, pltpu.roll(v, 1, 0))
            for v, edge in ((field, before), (ends, ends_before))
        ),
        1: tuple(
            jnp.where(row == ROWS - 1, edge, pltpu.roll(v, ROWS - 1, 0))
            for v, edge in ((field, after), (ends, ends_after))
        ),
    }
    for (dr, dc), count in zip(ORDER, counts):
        line, line_ends = lines[dr]
        if dc == -1:
            line = column_left(line, line_ends, lane)
        elif dc == 1:
            line = column_right(line, line_ends, lane)
        total += count * (line - field)
    return total


def edge_weights(counts, weight_ref):
    weight_ref[...] = jnp.zeros_like(weight_ref)
    for n, (dr, _) in enumerate(ORDER):
        if dr:
            edge = 0 if dr < 0 else ROWS - 1
            weight_ref[n : n + 1, :] = counts[n][edge : edge + 1, :]


def top_base_body(other_ref, mate_ref, table_ref, out_ref, weight_ref):
    row, lane = iotas(ROWS)
    top = other_ref[0].astype(F32)
    counts = neighbour_counts(table_ref, row, lane)
    none = jnp.zeros((1, COLS), F32)
    spread = neighbour_spread(
        top, mate_ref[0].astype(F32), none, none, none, none, counts, row, lane
    )
    out_ref[...] = (1.0 - MIXING) * top + other_ref[1].astype(F32) + OCEAN_DIFFUSION * spread
    edge_weights(counts, weight_ref)


def edge_terms(line, ends, weights):
    lane = lax.broadcasted_iota(jnp.int32, (1, COLS), 1)
    total = weights[0] * column_left(line, ends, lane) + weights[1] * line
    return OCEAN_DIFFUSION * (total + weights[2] * column_right(line, ends, lane))


def both_edges(before, before_ends, after, after_ends, weight_ref):
    weights = [weight_ref[n : n + 1, :] for n in range(len(ORDER))]
    return edge_terms(before, before_ends, weights[:3]), edge_terms(after, after_ends, weights[5:])


def ocean_base_body(
    o_ref,
    sides_ref,
    before_ref,
    after_ref,
    mate_before_ref,
    mate_after_ref,
    table_ref,
    out_ref,
    counts_ref,
):
    row, lane = iotas(ROWS)
    for n, count in enumerate(neighbour_counts(table_ref, row, lane)):
        counts_ref[n] = count
    for l in range(LEV):
        field = o_ref[l]
        spread = neighbour_spread(
            field,
            mate_ends(sides_ref[...], l),
            before_ref[l : l + 1, :],
            after_ref[l : l + 1, :],
            mate_before_ref[l : l + 1, :],
            mate_after_ref[l : l + 1, :],
            [counts_ref[n] for n in range(len(ORDER))],
            row,
            lane,
        )
        below, above = o_ref[max(l - 1, 0)], o_ref[min(l + 1, LEV - 1)]
        out_ref[l] = field + OCEAN_DIFFUSION * spread + MIXING * (above + below - 2.0 * field)


def edge_rows(*fields):
    last = [v[..., ROWS - WIDE :, :].reshape(-1, WIDE, COLS).astype(F32) for v in fields]
    first = [v[..., :WIDE, :].reshape(-1, WIDE, COLS).astype(F32) for v in fields]
    return jnp.concatenate(last, axis=0), jnp.concatenate(first, axis=0)


def from_neighbours(last, first):
    size = lax.axis_size("gx")
    up = [(i, (i + 1) % size) for i in range(size)]
    down = [(j, i) for i, j in up]
    return lax.ppermute(last, "gx", up), lax.ppermute(first, "gx", down)


def from_mate(field):
    return lax.ppermute(field, "gy", [(0, 1), (1, 0)])


def row_hits(labels):
    blocks, width = labels.shape[0], ATMOS_SLOTS
    shape = (blocks, width, COLS)
    diagonal = lax.broadcasted_iota(jnp.int32, shape, 1) == lax.broadcasted_iota(jnp.int32, shape, 2)
    spread = jnp.where(diagonal, labels[:, None, :], 0.0)
    column = jnp.sum(spread, axis=2, keepdims=True).reshape(blocks * width, 1)
    slot = lax.broadcasted_iota(jnp.int32, (blocks, width, 1), 1).reshape(blocks * width, 1)
    column = jnp.where(slot < CAP, column, -1.0).astype(jnp.int32)
    rows = lax.broadcasted_iota(jnp.int32, (blocks * width, ROWS), 1)
    return jnp.where(column == rows, 1.0, 0.0).astype(BF16)


def push_body(core_ref, arrived_ref, base_ref, out_ref, hits_ref):
    blocks = RANKS // CORES
    arrived = arrived_ref[...].astype(F32).reshape(blocks, CORES, ATMOS_SLOTS, COLS)
    for core in range(CORES):
        part = arrived[:, core]
        hits = row_hits(part[:, CAP, :])
        hits_ref[core] = hits
        values = part.reshape(blocks * ATMOS_SLOTS, COLS).astype(BF16)
        pushed = lax.dot_general(
            hits, values, (((0,), (0,)), ((), ())), preferred_element_type=F32
        )
        out_ref[core] = pushed + jnp.where(core_ref[0] == core, base_ref[...], 0.0)


def pick_body(
    core_ref,
    mine_ref,
    mate_ref,
    weight_ref,
    mate_weight_ref,
    before_ref,
    after_ref,
    mate_before_ref,
    mate_after_ref,
    hits_ref,
    out_ref,
):
    blocks = RANKS // CORES
    row = lax.broadcasted_iota(jnp.int32, (ROWS, COLS), 0)
    own_rows = [before_ref[LEV, WIDE - 1 :, :], after_ref[LEV, :1, :]]
    mate_rows = [mate_before_ref[LEV, WIDE - 1 :, :], mate_after_ref[LEV, :1, :]]
    own = both_edges(own_rows[0], mate_rows[0], own_rows[1], mate_rows[1], weight_ref)
    mate = both_edges(mate_rows[0], own_rows[0], mate_rows[1], own_rows[1], mate_weight_ref)
    for core in range(CORES):
        above, below = (jnp.where(core_ref[0] == core, o, m) for o, m in zip(own, mate))
        top = mine_ref[core] + mate_ref[core]
        top += jnp.where(row == 0, above, 0.0) + jnp.where(row == ROWS - 1, below, 0.0)
        picked = jnp.dot(hits_ref[core], top.astype(BF16), preferred_element_type=F32)
        out_ref[:, core] = picked.astype(BF16).reshape(blocks, ATMOS_SLOTS, COLS)


def sums_body(arrived_ref, base_ref, share_ref, out_ref, first_ref, wide):
    width = OCEAN_SLOTS * NF
    wide[...] = arrived_ref[...].astype(F32).reshape(RANKS * width, COLS)
    labels = wide[pl.ds(CAP * NF, RANKS, stride=width), :]
    by_slot = jnp.concatenate([labels, labels], axis=0).T
    row = lax.broadcasted_iota(jnp.int32, (ROWS, COLS), 0).astype(F32)
    lane = lax.broadcasted_iota(jnp.int32, (1, COLS), 1)
    pieces = []
    for s in range(0, CAP, 2):
        pair = jnp.where(lane < RANKS, by_slot[s : s + 1, :], by_slot[s + 1 : s + 2, :])
        pieces.append(jnp.where(row == pair, 1.0, 0.0).astype(BF16))
    hits = jnp.concatenate(pieces, axis=1)
    forcing = []
    for f in range(0, NF, 2):
        values = [
            jnp.concatenate(
                [wide[pl.ds(s * NF + g, RANKS, stride=width), :] for s in range(CAP)], axis=0
            )
            for g in (f, f + 1)
        ]
        both = jnp.concatenate(values, axis=1).astype(BF16)
        summed = jnp.dot(hits, both, preferred_element_type=F32)
        forcing += [summed[:, :COLS], summed[:, COLS:]]
    first_ref[...] = forcing[0]
    for l in range(LEV):
        level = base_ref[l]
        for f in range(NF):
            level += share_ref[l, f] * forcing[f]
        out_ref[l] = level


def ocean_sums(arrived, base, share):
    return pl.pallas_call(
        sums_body,
        out_shape=(
            jax.ShapeDtypeStruct((LEV, ROWS, COLS), F32),
            jax.ShapeDtypeStruct((ROWS, COLS), F32),
        ),
        in_specs=[VMEM, VMEM, SMEM],
        out_specs=(VMEM, VMEM),
        scratch_shapes=[pltpu.VMEM((RANKS * OCEAN_SLOTS * NF, COLS), F32)],
        compiler_params=pltpu.CompilerParams(vmem_limit_bytes=24 << 20),
    )(arrived, base, share)


def remap_body(pos_hbm_ref, arrived_ref, w_ref, out_ref, held, pos_ref, values, own, sems):
    pos_copy = pltpu.make_async_copy(pos_hbm_ref, pos_ref, sems.at[ROWS // REMAP_ROWS])
    pos_copy.start()
    copy = weight_copies(w_ref, held, sems, REMAP_ROWS)
    for c in range(ROWS // REMAP_ROWS):
        copy(c).start()
    slots = RANKS * ATMOS_SLOTS
    by_column = arrived_ref[...].astype(F32).reshape(slots, COLS).T.astype(BF16)
    at = lax.broadcasted_iota(jnp.int32, (slots, ROWS), 0)
    groups = ROWS // COLS
    pos_copy.wait()
    for k in range(K):
        hits = jnp.where(at == pos_ref[K + k : K + k + 1, :], 1.0, 0.0).astype(BF16)
        found = jnp.dot(by_column, hits, preferred_element_type=F32).astype(BF16)
        for g in range(groups):
            values[g, k * COLS : (k + 1) * COLS, :] = found[:, g * COLS : (g + 1) * COLS]
    lane = lax.broadcasted_iota(jnp.int32, (COLS, COLS), 1)
    parts = COLS // REMAP_ROWS

    @pl.loop(0, ROWS // REMAP_ROWS)
    def _(c):
        copy(c).wait()
        block = held.at[pl.ds(c * REMAP_ROWS, REMAP_ROWS)]
        tiles = jnp.concatenate(
            [block[:, k].reshape(REMAP_ROWS * COLS, COLS) for k in range(K)], axis=1
        )
        crossed = jnp.dot(tiles, values[c // parts], preferred_element_type=F32)
        kept = own[c // parts]
        for i in range(REMAP_ROWS):
            mine = lane == (c % parts) * REMAP_ROWS + i
            kept = jnp.where(mine, crossed[i * COLS : (i + 1) * COLS], kept)
        own[c // parts] = kept

    for g in range(groups):
        out_ref[g * COLS : (g + 1) * COLS, :] = own[g].T


def remap(pos, arrived, weights):
    return pl.pallas_call(
        remap_body,
        out_shape=jax.ShapeDtypeStruct((ROWS, COLS), F32),
        in_specs=[ANY, VMEM, HBM],
        out_specs=VMEM,
        scratch_shapes=WEIGHTS_HELD
        + [
            pltpu.VMEM((2 * K, ROWS), jnp.int32),
            pltpu.VMEM((ROWS // COLS, K * COLS, COLS), BF16),
            pltpu.VMEM((ROWS // COLS, COLS, COLS), F32),
            pltpu.SemaphoreType.DMA((ROWS // REMAP_ROWS + 1,)),
        ],
        compiler_params=pltpu.CompilerParams(vmem_limit_bytes=32 << 20),
    )(pos, arrived, weights)


def to_peers(payload, axes):
    return lax.all_to_all(payload, axes, split_axis=0, concat_axis=0, tiled=True)


def local(
    layered_heat_profile,
    prior_marine_heat,
    transfer_factor_table,
    depth_fraction_matrix,
    adjacent_cell_table,
    destination_water_peer,
    destination_water_line,
    interpolation_matrix_blocks,
):
    is_atmosphere_side = lax.axis_index("comp") == 0
    own = layered_heat_profile[0]
    block = jax.ShapeDtypeStruct((LEV, ROWS, COLS), F32)
    plane = jax.ShapeDtypeStruct((ROWS, COLS), F32)
    swap = [(0, 1), (1, 0)]

    cross, last, first = cross_kernel(lax.axis_index("comp").reshape(1), own)
    other = lax.ppermute(cross, "comp", [(0, 1), (1, 0)])

    def atmosphere_early():
        packed, pos = atmos_flux(
            destination_water_peer,
            destination_water_line,
            own,
            prior_marine_heat,
            transfer_factor_table,
            interpolation_matrix_blocks,
            depth_fraction_matrix,
        )
        return packed, pos, unused((LEV, COLS), F32), unused((1, LEV, COLS), F32)

    def ocean_early():
        before, after = from_neighbours(last, first)
        packed = unused((RANKS, ATMOS_SLOTS, COLS), BF16)
        return packed, unused((2 * K, ROWS), jnp.int32), before, after[None]

    packed, pos, before, after = lax.cond(is_atmosphere_side, atmosphere_early, ocean_early)
    ocean_rows = (before, after[0])
    edge_shape = jax.ShapeDtypeStruct((len(ORDER), COLS), F32)

    def atmosphere():
        by_chip = (RANKS // CORES, CORES * ATMOS_SLOTS, COLS)
        rows = from_neighbours(*edge_rows(own, other[:1]))
        arrived = to_peers(packed.reshape(by_chip), "gx")
        sides = from_mate(shadow_call(sides_body, plane, [VMEM])(own))
        moved = shadow_call(local_body, block, [VMEM])(own)
        base, weights = shadow_call(top_base_body, (plane, edge_shape), [VMEM] * 3, us=2)(
            other, from_mate(other), adjacent_cell_table
        )
        *rows, base = lax.optimization_barrier((*rows, base))
        rows = [*rows, *map(from_mate, rows)]
        core = lax.axis_index("gy").reshape(1)
        mine, hits = call(
            push_body,
            (
                jax.ShapeDtypeStruct((CORES, ROWS, COLS), F32),
                jax.ShapeDtypeStruct((CORES, RANKS // CORES * ATMOS_SLOTS, ROWS), BF16),
            ),
            [SMEM, VMEM, VMEM],
        )(core, arrived.reshape(RANKS, ATMOS_SLOTS, COLS), base)
        picked = call(
            pick_body,
            jax.ShapeDtypeStruct((RANKS // CORES, CORES, ATMOS_SLOTS, COLS), BF16),
            [SMEM] + [VMEM] * 9,
        )(core, mine, from_mate(mine), weights, from_mate(weights), *rows, hits)
        returned = to_peers(picked.reshape(by_chip), "gx")
        wide = pltpu.VMEM((LEV, EXTENDED, COLS), F32)
        final = shadow_call(
            substeps_body, block, [VMEM] * 6 + [ANY], scratch_shapes=[wide]
        )(moved, sides, *rows, picked)
        return final, remap(
            pos, returned.reshape(RANKS, ATMOS_SLOTS, COLS), interpolation_matrix_blocks
        )

    def ocean():
        payload = ocean_flux(
            destination_water_peer,
            destination_water_line,
            other,
            prior_marine_heat,
            transfer_factor_table,
            interpolation_matrix_blocks,
        )
        arrived = to_peers(payload.reshape(RANKS, OCEAN_SLOTS * NF, COLS), ("gx", "gy"))
        sides = from_mate(shadow_call(sides_body, plane, [VMEM])(own))
        base = shadow_call(
            ocean_base_body,
            block,
            [VMEM] * 7,
            scratch_shapes=[pltpu.VMEM((len(ORDER), ROWS, COLS), F32)],
        )(own, sides, *ocean_rows, *map(from_mate, ocean_rows), adjacent_cell_table)
        return ocean_sums(
            arrived.reshape(RANKS * OCEAN_SLOTS, NF, COLS), base, depth_fraction_matrix
        )

    state, plane_out = lax.cond(is_atmosphere_side, atmosphere, ocean)
    return state[None], plane_out[None]


def solution(mesh):
    return jax.shard_map(
        local,
        mesh=mesh,
        in_specs=(
            P("comp", None, "gx", "gy"),
            P("gx", "gy"),
            P(None, "gx", "gy"),
            P(),
            P(None, "gx", "gy"),
            P(("gx", "gy"), None),
            P(("gx", "gy"), None),
            P(("gx", "gy"), None, None, None),
        ),
        out_specs=(P("comp", None, "gx", "gy"), P("comp", "gx", "gy")),
        check_vma=False,
    )
```
